256 devices in a mesh: dom: 32 (over x, y, core), col: 8 (over z).
Axes of the slice: x: 4, y: 4, z: 8, core: 2. Of those that a mesh axis runs over, the one named last changes fastest.
Arguments:
- node_states: bfloat16 [32768, 512], P(('dom', 'col')), may hold values from -6 to 6
- norm_gain: float32 [512], replicated, may hold values from 0.5 to 1.5
- qkv_weight: bfloat16 [1536, 512], P('col'), may hold values from -0.375 to 0.375
- out_weight: bfloat16 [512, 512], P('col'), may hold values from -0.25 to 0.25
- local_slots: int32 [256, 8], P('dom'), may hold values from 0 to 7
- local_live: int32 [256, 8], P('dom'), may hold values 0 or 1
- far_owner: int32 [256, 4], replicated, may hold values from 0 to 31, all different within a row; in each aligned block of 8 rows (0 to 7, 8 to 15, ...) at most 2 rows name the same one
- far_slot: int32 [256, 4], replicated, may hold values from 0 to 7
- out_grad: bfloat16 [32768, 512], P(('dom', 'col')), may hold values from -6 to 6
Outputs:
- layer_out: bfloat16 [32768, 512], P(('dom', 'col'))
- state_grad: bfloat16 [32768, 512], P(('dom', 'col'))
- qkv_grad: float32 [1536, 512], P('col')
- out_weight_grad: float32 [512, 512], P('col')
The draws below stay inside these ranges and needn't reach their ends.
Inputs may be any that keep to these rules, and one draw needn't show every extreme that they name: `far_owner`: each row names 4 different partitions; among the rows of one partition's 8 node blocks no partition is named by more than 2 rows, and in every draw some partition is named by exactly 2 of them.
All inputs are finite; a program needn't handle non-finite values. No bound on the sum of `local_live` on one device may be relied on, other than what follows from the above.
Results may differ from the reference program's by a relative error of at most 0.02.
Values may be sent and summed in bfloat16 or wider, within the bound.
No kernel may reach another device: no remote copies, remote signals or barrier semaphores. Data moves between devices by JAX's collectives and lax.ppermute only.
A program may use at most 64 MiB of HBM per device.

```python
import math
import jax
import jax.numpy as jnp
import numpy as np
from jax import lax

D = 512
HEADS = 8
HD = 64
HGRP = 1
BLK = 128
NB_DEV = 8
LOC = 8
DEG = 4
NBLK = 256
NODES = 32768
MOST = 2
N_DOM = 32


def place_ends(values, own_key, smallest, largest):
    index_at = [jax.random.randint(jax.random.fold_in(own_key, axis), (), 0, length) for axis, length in enumerate(values.shape)]
    longest = values.shape.index(max(values.shape))
    next_to = index_at[:longest] + [(index_at[longest] + 1) % values.shape[longest]] + index_at[longest + 1:]
    return values.at[tuple(index_at)].set(smallest).at[tuple(next_to)].set(largest)


def levels(key, dims, split, least, largest):
    def one(dim, blocks):
        draws = jax.random.uniform(jax.random.fold_in(jax.random.fold_in(key, 6), dim), (blocks,), jnp.float32, least / len(split), largest / len(split))
        return jnp.repeat(jnp.exp(draws), dims[dim] // blocks).reshape((-1,) + (1,) * (len(dims) - dim - 1))

    level = one(*split[0])
    for cut in split[1:]:
        level = level * one(*cut)
    return level


def shared_out(key, own, number, rows, number_of, top, most, slope):
    order = jax.random.permutation(key, number_of)
    crowded, common = load_shares(number_of, rows * top, most, slope, True), load_shares(number_of, rows * top, most, slope, False)
    places = jnp.arange(number_of)

    def named(tallies, turn):
        used = int((tallies > 0).sum())
        fixed = max(1, used // 4)
        passed = fixed + (places - fixed + turn * (used - fixed)) % max(1, number_of - fixed)
        return jnp.zeros((number_of,), jnp.int32).at[order[jnp.where(places < fixed, places, passed)]].set(jnp.asarray(tallies, jnp.int32))

    tallies = jnp.where(number % 4 == 0, named(crowded, number // 4), named(common, number - number // 4 - 1))
    mixed = jax.random.permutation(jax.random.fold_in(own, 3), number_of)
    source_of, taker = mixed[0:number_of // 2 * 2:2], mixed[1:number_of // 2 * 2:2]
    margin = jnp.minimum(tallies[source_of] - 1, most - tallies[taker]) // 2
    margin = jnp.where((source_of == order[0]) | (taker == order[0]) | (tallies[taker] == 0), 0, jnp.maximum(margin, 0))
    passed = jax.random.randint(jax.random.fold_in(own, 4), (number_of // 2,), 0, 1 << 20) % (margin + 1)
    tallies = tallies.at[source_of].add(-passed).at[taker].add(passed)
    labels = jnp.searchsorted(jnp.cumsum(tallies), jnp.arange(rows * top), side="right").astype(jnp.int32)
    listing = labels.reshape(top, rows).T
    listing = listing[jax.random.permutation(jax.random.fold_in(own, 1), rows)]
    turn = jax.random.randint(jax.random.fold_in(own, 2), (rows, 1), 0, top)
    return jnp.take_along_axis(listing, (jnp.arange(top)[None, :] + turn) % top, axis=1)


def load_shares(number_of, total, most, skew, full):
    loads = [(1 << 20) // math.isqrt(standing ** skew) + 1 for standing in range(1, number_of + 1)]
    largest = most if full else min(most, max(-(-total // number_of), total * loads[0] // sum(loads)))
    least = 1 if total - largest >= number_of - 1 else 0
    counts, spare = [largest] + [least] * (number_of - 1), total - largest - least * (number_of - 1)
    while spare > 0:
        movable = [i for i in range(1, number_of) if counts[i] < largest] or [i for i in range(1, number_of) if counts[i] < most]
        whole, remaining = sum([loads[i] for i in movable]), spare
        for i in movable:
            more = min(most - counts[i], max(1, remaining * loads[i] // whole), spare)
            counts[i] = counts[i] + more
            spare = spare - more
    return np.array(counts)


def gaussian(rng, dims, width, bound, shards=(), kind=jnp.bfloat16):
    result = width * jax.random.normal(rng, dims, jnp.float32)
    if shards:
        result = result * levels(rng, dims, shards, -0.22, 0.18)
    return jnp.clip(result, -bound, bound).astype(kind)


def setup_inputs(seed: int = 0) -> dict:
    key_list = jax.random.split(jax.random.key(seed), 10)
    node_states = gaussian(key_list[0], (NODES, D), 1.0, 6.0, ((0, 256),))
    norm_gain = jnp.clip(jax.random.uniform(key_list[1], (D,), jnp.float32, 0.5, 1.5), 0.5, 1.5)
    qkv_weight = gaussian(key_list[2], (3 * D, D), (D // 2) ** -0.5, 0.375, ((0, 8),))
    out_weight = gaussian(key_list[3], (D, D), D ** -0.5, 0.25, ((0, 8),))
    local_slots = place_ends(jax.random.randint(key_list[4], (NBLK, LOC), 0, NB_DEV), jax.random.fold_in(key_list[4], 1), 0, NB_DEV - 1).astype(jnp.int32)
    local_live = place_ends((jax.random.randint(key_list[5], (NBLK, LOC), 0, 4) < 3).astype(jnp.int32), jax.random.fold_in(key_list[5], 1), 0, 1)
    far_owner_keys = jax.random.split(jax.random.fold_in(key_list[6], 1), NBLK // NB_DEV)
    far_owner_turns = jax.random.permutation(jax.random.fold_in(key_list[6], 3), NBLK // NB_DEV)
    far_owner = jax.vmap(lambda own, number: shared_out(jax.random.fold_in(key_list[6], 2), own, number, NB_DEV, N_DOM, DEG, MOST, 2))(far_owner_keys, far_owner_turns).reshape((NBLK, DEG))
    far_slot = place_ends(jax.random.randint(key_list[7], (NBLK, DEG), 0, NB_DEV), jax.random.fold_in(key_list[7], 1), 0, NB_DEV - 1).astype(jnp.int32)
    out_grad = gaussian(key_list[8], (NODES, D), 1.0, 6.0, ((0, 256),))
    return {"node_states": node_states, "norm_gain": norm_gain, "qkv_weight": qkv_weight, "out_weight": out_weight, "local_slots": local_slots, "local_live": local_live, "far_owner": far_owner, "far_slot": far_slot, "out_grad": out_grad}


def block_keys(local_slots, local_live, far_owner, far_slot):
    block_total = far_owner.shape[0]
    blocks = jnp.arange(block_total, dtype=jnp.int32)
    owner_part = blocks // NB_DEV
    key_lists = jnp.concatenate([blocks[:, None], owner_part[:, None] * NB_DEV + local_slots, far_owner * NB_DEV + far_slot], axis=1).astype(jnp.int32)
    key_live = jnp.concatenate([jnp.ones((block_total, 1), jnp.float32), local_live.astype(jnp.float32), jnp.ones((block_total, DEG), jnp.float32)], axis=1)
    return (key_lists, key_live)

def weights_of(query_block, key_blocks, live_row, score_scale):
    scores = jnp.einsum('qhc,mkhc->hqmk', query_block.astype(jnp.float32), key_blocks.astype(jnp.float32)) * score_scale
    return jnp.exp(scores) * live_row[None, None, :, None]

def rounded(value):
    return lax.optimization_barrier(value.astype(jnp.bfloat16)).astype(jnp.float32)

def reference(node_states, norm_gain, qkv_weight, out_weight, local_slots, local_live, far_owner, far_slot, out_grad):
    score_scale = 1.0 / math.sqrt(HD)
    state_float = node_states.astype(jnp.float32)
    inv_rms = lax.rsqrt(lax.optimization_barrier(jnp.mean(state_float * state_float, axis=1, keepdims=True)) + 1e-06)
    hidden = (state_float * inv_rms * norm_gain).astype(jnp.bfloat16)
    projected = lax.optimization_barrier(lax.dot_general(hidden, qkv_weight, (((1,), (1,)), ((), ())), preferred_element_type=jnp.float32).astype(jnp.bfloat16))
    projected = projected.reshape(NBLK, BLK, HEADS, 3, HD)
    queries = projected[:, :, :, 0]
    keyed = projected[:, :, :, 1]
    valued = projected[:, :, :, 2]
    key_lists, key_live = block_keys(local_slots, local_live, far_owner, far_slot)

    def forward_block(block_index):
        key_blocks = keyed[key_lists[block_index]]
        value_blocks = valued[key_lists[block_index]]
        probabilities = weights_of(queries[block_index], key_blocks, key_live[block_index], score_scale)
        numerator = jnp.einsum('hqmk,mkhc->qhc', rounded(probabilities), value_blocks.astype(jnp.float32))
        denominator = lax.optimization_barrier(jnp.sum(probabilities, axis=(2, 3))).T
        return (numerator, denominator)
    numerator, denominator = lax.map(forward_block, jnp.arange(NBLK, dtype=jnp.int32))
    attn_float = numerator / denominator[..., None]
    attn_rounded = attn_float.astype(jnp.bfloat16).reshape(NODES, D)
    group_width = D // (HEADS // HGRP)
    summed = state_float
    for group_index in range(HEADS // HGRP):
        partial_value = jnp.dot(attn_rounded[:, group_index * group_width:(group_index + 1) * group_width], out_weight[group_index * group_width:(group_index + 1) * group_width], preferred_element_type=jnp.float32)
        summed = summed + rounded(partial_value)
    layer_out = summed.astype(jnp.bfloat16)
    attn_grad = jnp.dot(out_grad, out_weight.T, preferred_element_type=jnp.float32).reshape(NBLK, BLK, HEADS, HD)
    scaled = lax.optimization_barrier((attn_grad / denominator[..., None]).astype(jnp.bfloat16))
    correction = lax.optimization_barrier(jnp.sum(attn_grad * attn_float, axis=3)) / denominator
    entry_count = 1 + LOC + DEG
    far_mask = (jnp.arange(entry_count, dtype=jnp.int32) >= 1 + LOC)[:, None, None, None]

    def backward_block(carried, block_index):
        key_acc, value_acc = carried
        key_blocks = keyed[key_lists[block_index]]
        value_blocks = valued[key_lists[block_index]]
        query_block = queries[block_index].astype(jnp.float32)
        scaled_block = scaled[block_index].astype(jnp.float32)
        probabilities = weights_of(queries[block_index], key_blocks, key_live[block_index], score_scale)
        prob_grad = jnp.einsum('qhc,mkhc->hqmk', scaled_block, value_blocks.astype(jnp.float32)) - correction[block_index].T[:, :, None, None]
        score_grad = rounded(probabilities * prob_grad)
        query_grad = jnp.einsum('hqmk,mkhc->qhc', score_grad, key_blocks.astype(jnp.float32)) * score_scale
        key_grad = jnp.einsum('hqmk,qhc->mkhc', score_grad, query_block) * score_scale
        value_grad = jnp.einsum('hqmk,qhc->mkhc', rounded(probabilities), scaled_block)
        key_grad = jnp.where(far_mask, rounded(key_grad), key_grad)
        value_grad = jnp.where(far_mask, rounded(value_grad), value_grad)
        key_acc = key_acc.at[key_lists[block_index]].add(key_grad)
        value_acc = value_acc.at[key_lists[block_index]].add(value_grad)
        return ((key_acc, value_acc), query_grad)
    empty_acc = jnp.zeros((NBLK, BLK, HEADS, HD), jnp.float32)
    (key_acc, value_acc), query_grad = lax.scan(backward_block, (empty_acc, empty_acc), jnp.arange(NBLK, dtype=jnp.int32))
    proj_grad = jnp.stack([query_grad, key_acc, value_acc], axis=3).astype(jnp.bfloat16).reshape(NODES, 3 * D)
    group_cols = 3 * group_width
    back_sum = jnp.zeros((NODES, D), jnp.float32)
    for group_index in range(HEADS // HGRP):
        partial_value = jnp.dot(proj_grad[:, group_index * group_cols:(group_index + 1) * group_cols], qkv_weight[group_index * group_cols:(group_index + 1) * group_cols], preferred_element_type=jnp.float32)
        back_sum = back_sum + rounded(partial_value)
    norm_stat = lax.optimization_barrier(jnp.sum(norm_gain * back_sum * state_float, axis=1, keepdims=True))
    state_grad = (out_grad.astype(jnp.float32) + inv_rms * norm_gain * back_sum - state_float * inv_rms * inv_rms * inv_rms * norm_stat / D).astype(jnp.bfloat16)
    inv_root = 1.0 / math.sqrt(NODES)
    qkv_grad = lax.dot_general(proj_grad, hidden, (((0,), (0,)), ((), ())), preferred_element_type=jnp.float32) * inv_root
    out_weight_grad = jnp.dot(attn_rounded.T, out_grad, preferred_element_type=jnp.float32) * inv_root
    return (layer_out, state_grad, qkv_grad, out_weight_grad)
```

```python
import math

import jax
import jax.numpy as jnp
from jax import lax
from jax.experimental import pallas as pl
from jax.experimental.pallas import tpu as pltpu
from jax.sharding import PartitionSpec as P

D = 512
HD = 64
BLK = 128
NB = 8
DEG = 4
CAP = 2
ROWS = NB * BLK
EPS = 1e-06
SCALE = 1.0 / math.sqrt(HD)

F32 = jnp.float32
BF16 = jnp.bfloat16
VMEM_LIMIT = 40 * 1024 * 1024

NT = (((1,), (1,)), ((), ()))
TN = (((0,), (0,)), ((), ()))


def dot(a, b):
    return jnp.dot(a, b, preferred_element_type=F32)


def dot_nt(a, b):
    return lax.dot_general(a, b, NT, preferred_element_type=F32)


def whole(shape=None):
    return pl.BlockSpec(memory_space=pltpu.VMEM)


def scalars():
    return pl.BlockSpec(memory_space=pltpu.SMEM)


def call(body, outs, ins, scratch=(), flops=0, name=None):
    return pl.pallas_call(
        body,
        out_shape=outs,
        in_specs=ins,
        out_specs=jax.tree.map(lambda _: whole(), outs),
        scratch_shapes=list(scratch),
        compiler_params=pltpu.CompilerParams(vmem_limit_bytes=VMEM_LIMIT),
        cost_estimate=pl.CostEstimate(flops=flops, bytes_accessed=4 << 20, transcendentals=0),
        name=name,
    )


def lanes_low(shape):
    return lax.broadcasted_iota(jnp.int32, shape, len(shape) - 1) < HD


def rows_of(b):
    return pl.ds(pl.multiple_of(b * BLK, BLK), BLK)


def project_body(send_ref, state_ref, gain_ref, weight_ref, hidden_ref, query_ref, kv_ref, out_ref):
    gain = gain_ref[...]
    weight = weight_ref[...]
    wide = jnp.concatenate(
        [weight[:HD], jnp.zeros((HD, D), BF16), weight[HD:]], axis=0
    )

    def step(b, _):
        x = state_ref[b].astype(F32)
        inv = lax.rsqrt(jnp.mean(x * x, axis=1, keepdims=True) + EPS)
        hidden = (x * inv * gain).astype(BF16)
        hidden_ref[rows_of(b), :] = hidden
        proj = dot_nt(hidden, wide).astype(BF16)
        query_ref[rows_of(b), :] = proj[:, :BLK] * jnp.asarray(SCALE, BF16)
        kv_ref[b] = proj[:, BLK:]
        return 0

    lax.fori_loop(0, NB, step, 0, unroll=True)

    def fill(s, _):
        out_ref[s] = kv_ref[send_ref[s]]
        return 0

    lax.fori_loop(0, out_ref.shape[0], fill, 0, unroll=8)


def near_forward_body(query_ref, kv_ref, count_ref, num_ref, ones_ref):
    kv = kv_ref[...].reshape(ROWS, BLK)
    ones_ref[...] = jnp.where(lanes_low(kv.shape), jnp.asarray(1, BF16), kv)

    def step(b, _):
        score = dot_nt(query_ref[rows_of(b), :], kv_ref[...].reshape(ROWS, BLK))
        prob = jnp.exp(score) * count_ref[pl.ds(b, 1), :]
        num_ref[rows_of(b), :] = dot(prob.astype(BF16), ones_ref[...])
        return 0

    lax.fori_loop(0, NB, step, 0, unroll=2)


def far_body(
    place_ref,
    query_ref,
    far_ref,
    num_ref,
    grad_ref,
    weight_ref,
    attn_ref,
    scaled_ref,
    extra_ref,
    back_ref,
    kv_ref,
    ag_ref,
):
    wide = jnp.concatenate([jnp.zeros((HD, D), BF16), weight_ref[...]], axis=0)
    ag_ref[...] = dot_nt(grad_ref[...].reshape(ROWS, D), wide)

    def step(b, _):
        rows = rows_of(b)
        for j in range(DEG):
            kv_ref[pl.ds(j * BLK, BLK), :] = far_ref[place_ref[b * DEG + j]]
        kv = kv_ref[...]
        query = query_ref[rows, :]
        prob = jnp.exp(dot_nt(query, kv))
        prob_low = prob.astype(BF16)
        values = jnp.where(lanes_low(kv.shape), jnp.asarray(1, BF16), kv)
        num = num_ref[rows, :] + dot(prob_low, values)
        low = lanes_low(num.shape)
        den = jnp.where(low, num, pltpu.roll(num, HD, 1))
        attn = num / den
        grad = ag_ref[rows, :]
        scaled = (grad / den).astype(BF16)
        scaled_ref[rows, :] = scaled
        corr = jnp.sum(grad * attn, axis=1, keepdims=True) / den
        attn_ref[:, rows] = attn.T[HD:].astype(BF16)
        diff = dot_nt(scaled, kv) - corr[:, :1]
        score_grad = (prob * diff).astype(BF16)
        extra_ref[rows, :] = jnp.where(low, dot(score_grad, kv), corr)
        both = (query + scaled).astype(F32).T.astype(BF16)
        key_grad = dot(both[:HD], score_grad).astype(BF16)
        value_grad = dot(both[HD:], prob_low).astype(BF16)
        for j in range(DEG):
            place = place_ref[b * DEG + j]
            back_ref[place, :HD, :] = key_grad[:, j * BLK : (j + 1) * BLK]
            back_ref[place, HD:, :] = value_grad[:, j * BLK : (j + 1) * BLK]
        return 0

    lax.fori_loop(0, NB, step, 0)


def near_backward_body(
    query_ref, kv_ref, count_ref, scaled_ref, extra_ref, query_grad_ref, acc_ref
):
    acc_ref[...] = jnp.zeros_like(acc_ref)

    def step(b, _):
        rows = rows_of(b)
        query, scaled, extra = query_ref[rows, :], scaled_ref[rows, :], extra_ref[rows, :]
        kv = kv_ref[...].reshape(ROWS, BLK)
        prob = jnp.exp(dot_nt(query, kv)) * count_ref[pl.ds(b, 1), :]
        diff = dot_nt(scaled, kv) - extra[:, HD : HD + 1]
        score_grad = (prob * diff).astype(BF16)
        query_grad = dot(score_grad, kv) + extra
        query_grad_ref[:, rows] = (query_grad.T[:HD] * SCALE).astype(BF16)
        both = (query + scaled).astype(F32).T.astype(BF16)
        acc_ref[:HD, :] += dot(both[:HD], score_grad)
        acc_ref[HD:, :] += dot(both[HD:], prob.astype(BF16))
        return 0

    lax.fori_loop(0, NB, step, 0)


def gather_grads_body(
    home_ref,
    returned_ref,
    near_ref,
    query_grad_ref,
    attn_ref,
    hidden_ref,
    grad_ref,
    node_ref,
    part_ref,
    acc_ref,
):
    for n in range(NB):
        acc_ref[n] = near_ref[:, n * BLK : (n + 1) * BLK]

    def add(s, _):
        home = home_ref[s]

        @pl.when(home >= 0)
        def _():
            acc_ref[home] += returned_ref[s].astype(F32)

        return 0

    lax.fori_loop(0, returned_ref.shape[0], add, 0)
    for n in range(NB):
        cols = slice(n * BLK, (n + 1) * BLK)
        node_ref[n, :HD, :] = query_grad_ref[:, cols]
        node_ref[n, HD : 3 * HD, :] = acc_ref[n].astype(BF16)
        node_ref[n, 3 * HD :, :] = attn_ref[:, cols]
    proj = jnp.concatenate([node_ref[n, : 3 * HD, :] for n in range(NB)], axis=1)
    part_ref[: 3 * HD, :] = dot(proj, hidden_ref[...]).astype(BF16)
    part_ref[3 * HD :, :] = dot(attn_ref[...], grad_ref[...].reshape(ROWS, D)).astype(BF16)


def sum_body(share_ref, total_ref):
    total = jnp.sum(share_ref[...].astype(F32), axis=0).astype(BF16)
    total_ref[...] = jnp.broadcast_to(total[None], total_ref.shape)


def finish_body(node_ref, weight_ref, out_weight_ref, state_ref, grad_ref, gain_ref, layer_ref, back_ref):
    heads = node_ref.shape[0]
    out = jnp.zeros((BLK, D), F32)
    back = jnp.zeros((BLK, D), F32)
    for h in range(heads):
        terms = node_ref[h].astype(F32).T.astype(BF16)
        back += dot(terms[:, : 3 * HD], weight_ref[h])
        out += dot(terms[:, 3 * HD :], out_weight_ref[h])
    state = state_ref[...].astype(F32)
    gain = gain_ref[...]
    layer_ref[...] = (state + out).astype(BF16)
    inv = lax.rsqrt(jnp.mean(state * state, axis=1, keepdims=True) + EPS)
    stat = jnp.sum(gain * back * state, axis=1, keepdims=True)
    back_ref[...] = (
        grad_ref[...].astype(F32) + inv * gain * back - state * (inv * inv * inv * stat / D)
    ).astype(BF16)


def shards(
    node_states,
    norm_gain,
    qkv_weight,
    out_weight,
    local_slots,
    local_live,
    far_owner,
    far_slot,
    out_grad,
):
    doms = lax.axis_size("dom")
    cols = lax.axis_size("col")
    me = lax.axis_index("dom")
    slots = doms * CAP
    gain = norm_gain[None]

    state_whole = lax.all_to_all(
        jnp.broadcast_to(node_states[None], (cols, BLK, D)), "col", 0, 0, tiled=True
    )
    grad_whole = lax.all_gather(out_grad, "col", axis=0)
    weight_whole = lax.all_gather(qkv_weight, "col", axis=0)
    out_weight_whole = lax.all_gather(out_weight, "col", axis=0)

    entries = NB * DEG
    owners = far_owner.reshape(doms, entries)
    wanted = far_slot.reshape(doms, entries)
    place = jnp.arange(entries, dtype=jnp.int32)
    before = place[None, :] < place[:, None]
    rank = jnp.sum((owners[:, :, None] == owners[:, None, :]) & before[None], axis=2, dtype=jnp.int32)
    mine = (owners == me)[:, None, :] & (
        rank[:, None, :] == jnp.arange(CAP, dtype=jnp.int32)[None, :, None]
    )
    home = jnp.max(jnp.where(mine, wanted[:, None, :], -1), axis=2).reshape(slots)
    send = jnp.maximum(home, 0)
    places = (
        lax.dynamic_index_in_dim(owners, me, 0, keepdims=False) * CAP
        + lax.dynamic_index_in_dim(rank, me, 0, keepdims=False)
    )
    block = jnp.arange(NB, dtype=jnp.int32)
    hits = (local_slots[:, :, None] == block[None, None, :]) & (local_live[:, :, None] != 0)
    count = jnp.sum(hits, axis=1, dtype=jnp.int32) + (block[:, None] == block[None, :])
    count = jnp.repeat(count.astype(F32), BLK, axis=1)

    unit = 2 * ROWS * ROWS * BLK
    hidden, query, kv, outgoing = call(
        project_body,
        (
            jax.ShapeDtypeStruct((ROWS, D), BF16),
            jax.ShapeDtypeStruct((ROWS, BLK), BF16),
            jax.ShapeDtypeStruct((NB, BLK, BLK), BF16),
            jax.ShapeDtypeStruct((slots, BLK, BLK), BF16),
        ),
        [scalars(), whole(), whole(), whole()],
        flops=2 * ROWS * D * 256,
        name="project",
    )(send, state_whole, gain, qkv_weight)

    fetched = lax.all_to_all(outgoing, "dom", 0, 0, tiled=True)

    near = call(
        near_forward_body,
        jax.ShapeDtypeStruct((ROWS, BLK), F32),
        [whole()] * 3,
        scratch=[pltpu.VMEM((ROWS, BLK), BF16)],
        flops=2 * unit,
        name="near_forward",
    )(query, kv, count)

    attn, scaled, extra, outgoing_back = call(
        far_body,
        (
            jax.ShapeDtypeStruct((HD, ROWS), BF16),
            jax.ShapeDtypeStruct((ROWS, BLK), BF16),
            jax.ShapeDtypeStruct((ROWS, BLK), F32),
            jax.ShapeDtypeStruct((slots, BLK, BLK), BF16),
        ),
        [scalars()] + [whole()] * 5,
        scratch=[pltpu.VMEM((DEG * BLK, BLK), BF16), pltpu.VMEM((ROWS, BLK), F32)],
        flops=2 * unit,
        name="far_both",
    )(places, query, fetched, near, grad_whole, out_weight)

    returned = lax.all_to_all(outgoing_back, "dom", 0, 0, tiled=True)

    query_grad, near_grad = call(
        near_backward_body,
        (
            jax.ShapeDtypeStruct((HD, ROWS), BF16),
            jax.ShapeDtypeStruct((BLK, ROWS), F32),
        ),
        [whole()] * 5,
        flops=5 * unit,
        name="near_backward",
    )(query, kv, count, scaled, extra)

    node_terms, part = call(
        gather_grads_body,
        (
            jax.ShapeDtypeStruct((NB, 4 * HD, BLK), BF16),
            jax.ShapeDtypeStruct((4 * HD, D), BF16),
        ),
        [scalars()] + [whole()] * 6,
        scratch=[pltpu.VMEM((NB, BLK, BLK), F32)],
        flops=2 * ROWS * D * 256,
        name="gather_grads",
    )(home, returned, near_grad, query_grad, attn, hidden, grad_whole)

    share_rows = 4 * HD // doms
    shares = lax.all_to_all(part.reshape(doms, share_rows, D), "dom", 0, 0, tiled=True)
    node_whole = lax.all_to_all(node_terms, "col", 0, 0, tiled=True)

    totals = call(
        sum_body,
        jax.ShapeDtypeStruct((doms, share_rows, D), BF16),
        [whole()],
        name="sum_shares",
    )(shares)
    total = lax.all_to_all(totals, "dom", 0, 0, tiled=True).reshape(4 * HD, D)

    layer_out, state_grad = call(
        finish_body,
        (
            jax.ShapeDtypeStruct((BLK, D), BF16),
            jax.ShapeDtypeStruct((BLK, D), BF16),
        ),
        [whole()] * 6,
        flops=2 * BLK * D * 2048,
        name="finish",
    )(node_whole, weight_whole, out_weight_whole, node_states, out_grad, gain)

    inv_root = 1.0 / math.sqrt(far_owner.shape[0] * BLK)
    grads = total.astype(F32) * inv_root
    return (layer_out, state_grad, grads[: 3 * HD], grads[3 * HD :])


def solution(mesh):
    placed = (
        P(("dom", "col"), None),
        P(),
        P("col", None),
        P("col", None),
        P("dom", None),
        P("dom", None),
        P(),
        P(),
        P(("dom", "col"), None),
    )
    return jax.shard_map(
        shards,
        mesh=mesh,
        in_specs=placed,
        out_specs=(
            P(("dom", "col"), None),
            P(("dom", "col"), None),
            P("col", None),
            P("col", None),
        ),
        check_vma=False,
    )
```

```python
import functools
import math

import jax
import jax.numpy as jnp
from jax import lax
from jax.experimental import pallas as pl
from jax.experimental.pallas import tpu as pltpu
from jax.sharding import PartitionSpec as P

D = 512
HD = 64
BLK = 128
NB = 8
DEG = 4
CAP = 2
ROWS = NB * BLK
EPS = 1e-06
SCALE = 1.0 / math.sqrt(HD)

F32 = jnp.float32
BF16 = jnp.bfloat16
VMEM_LIMIT = 60 * 1024 * 1024

NT = (((1,), (1,)), ((), ()))
TN = (((0,), (0,)), ((), ()))


def dot(a, b):
    return jnp.dot(a, b, preferred_element_type=F32)


def dot_nt(a, b):
    return lax.dot_general(a, b, NT, preferred_element_type=F32)


def whole():
    return pl.BlockSpec(memory_space=pltpu.VMEM)


def scalars():
    return pl.BlockSpec(memory_space=pltpu.SMEM)


def left():
    return pl.BlockSpec(memory_space=pl.ANY)


def shaped(*dims, kind=BF16):
    return jax.ShapeDtypeStruct(dims, kind)


def call(body, outs, ins, scratch=(), flops=0, name=None, out_specs=None, limit=VMEM_LIMIT):
    return pl.pallas_call(
        body,
        out_shape=outs,
        in_specs=ins,
        out_specs=out_specs or [left() for _ in outs],
        scratch_shapes=list(scratch),
        compiler_params=pltpu.CompilerParams(vmem_limit_bytes=limit),
        cost_estimate=pl.CostEstimate(flops=flops, bytes_accessed=1 << 20, transcendentals=0),
        name=name,
    )


def held(shapes):
    return [pltpu.VMEM(s.shape, s.dtype) for s in shapes]


def copies(sources, targets, sems):
    return [
        pltpu.make_async_copy(a, b, sems.at[i]) for i, (a, b) in enumerate(zip(sources, targets, strict=True))
    ]


def start_all(jobs):
    for job in jobs:
        job.start()


def wait_all(jobs):
    for job in jobs:
        job.wait()


def staged(body, numbers, ins, outs, scratch=()):
    def run(*refs):
        scalar_refs, refs = refs[:numbers], refs[numbers:]
        in_refs, refs = refs[: len(ins)], refs[len(ins) :]
        out_refs, refs = refs[: len(outs)], refs[len(outs) :]
        in_held, refs = refs[: len(ins)], refs[len(ins) :]
        out_held, refs = refs[: len(outs)], refs[len(outs) :]
        own, (in_sems, out_sems) = refs[:-2], refs[-2:]
        loads = copies(in_refs, in_held, in_sems)
        start_all(loads)
        wait_all(loads)
        body(*scalar_refs, *in_held, *out_held, *own)
        stores = copies(out_held, out_refs, out_sems)
        start_all(stores)
        wait_all(stores)

    return {
        "body": run,
        "outs": tuple(outs),
        "ins": [scalars()] * numbers + [left()] * len(ins),
        "scratch": [
            *held(ins),
            *held(outs),
            *scratch,
            pltpu.SemaphoreType.DMA((len(ins),)),
            pltpu.SemaphoreType.DMA((len(outs),)),
        ],
    }


def lanes_low(shape):
    return lax.broadcasted_iota(jnp.int32, shape, len(shape) - 1) < HD


def rows_of(b):
    return pl.ds(pl.multiple_of(b * BLK, BLK), BLK)


def ring_gather(x, axis, n):
    up = [(i, (i + 1) % n) for i in range(n)]
    down = [(i, (i - 1) % n) for i in range(n)]
    chunks = [x] * n
    ahead = behind = x
    for k in range(1, n // 2 + 1):
        chunks[k] = ahead = lax.ppermute(ahead, axis, up)
        if k < n - k:
            chunks[n - k] = behind = lax.ppermute(behind, axis, down)
    return chunks


def ring_scatter(pieces, axis, n):
    return [pieces[0]] + [
        lax.ppermute(pieces[k], axis, [(i, (i + k) % n) for i in range(n)]) for k in range(1, n)
    ]


def block_before(col, k):
    return lax.rem(col + NB - k, NB)


def block_after(col, k):
    return lax.rem(col + k, NB)


def project_body(col_ref, send_ref, *refs):
    chunk_refs, refs = refs[:NB], refs[NB:]
    gain_in, weight_in, hidden_out, query_out, kv_out, sent_out, *refs = refs
    chunk_ref, gain_ref, weight_ref, hidden_ref, query_ref, kv_ref, sent_ref, in_sems, out_sems = refs
    loads = copies(
        [gain_in, weight_in, *chunk_refs],
        [gain_ref, weight_ref, *(chunk_ref.at[k] for k in range(NB))],
        in_sems,
    )
    start_all(loads)
    wait_all(loads[:2])
    col = col_ref[0]
    gain = gain_ref[...]
    weight = weight_ref[...]
    wide = jnp.concatenate([weight[:HD], jnp.zeros((HD, D), BF16), weight[HD:]], axis=0)
    for k in range(NB):
        loads[2 + k].wait()
        b = block_before(col, k)
        x = chunk_ref[k].astype(F32)
        inv = lax.rsqrt(jnp.mean(x * x, axis=1, keepdims=True) + EPS)
        hidden = (x * inv * gain).astype(BF16)
        hidden_ref[rows_of(b), :] = hidden
        proj = dot_nt(hidden, wide).astype(BF16)
        query_ref[rows_of(b), :] = proj[:, :BLK] * jnp.asarray(SCALE, BF16)
        kv_ref[b] = proj[:, BLK:]
    parts = out_sems.shape[0] - 3
    step = sent_ref.shape[0] // parts
    stores = copies(
        [hidden_ref, query_ref, kv_ref, *(sent_ref.at[pl.ds(i * step, step)] for i in range(parts))],
        [hidden_out, query_out, kv_out, *(sent_out.at[pl.ds(i * step, step)] for i in range(parts))],
        out_sems,
    )
    for i in range(parts):

        def fill(s, _):
            sent_ref[i * step + s] = kv_ref[send_ref[i * step + s]]
            return 0

        lax.fori_loop(0, step, fill, 0, unroll=True)
        stores[3 + i].start()
    start_all(stores[:3])
    wait_all(stores)


def near_forward_body(query_ref, kv_ref, count_ref, num_ref, ones_ref):
    kv = kv_ref[...].reshape(ROWS, BLK)
    ones_ref[...] = jnp.where(lanes_low(kv.shape), jnp.asarray(1, BF16), kv)

    def step(b, _):
        score = dot_nt(query_ref[rows_of(b), :], kv_ref[...].reshape(ROWS, BLK))
        prob = jnp.exp(score) * count_ref[pl.ds(b, 1), :]
        num_ref[rows_of(b), :] = dot(prob.astype(BF16), ones_ref[...])
        return 0

    lax.fori_loop(0, NB, step, 0, unroll=2)


def attn_grad_body(col_ref, *refs):
    chunk_refs = refs[:NB]
    weight_ref, ag_ref = refs[NB:]
    col = col_ref[0]
    wide = jnp.concatenate([jnp.zeros((HD, D), BF16), weight_ref[...]], axis=0)
    for k in range(NB):
        ag_ref[rows_of(block_before(col, k)), :] = dot_nt(chunk_refs[k][...], wide)


def far_body(
    place_ref,
    query_in,
    far_in,
    num_in,
    ag_in,
    attn_out,
    scaled_out,
    extra_out,
    back_out,
    far_ref,
    query_ref,
    num_ref,
    ag_ref,
    attn_ref,
    scaled_ref,
    extra_ref,
    prob_ref,
    prob_low_ref,
    both_ref,
    stage_ref,
    far_sems,
    in_sems,
    out_sems,
    back_sems,
):
    entries = NB * DEG
    loads = copies([query_in, num_in, ag_in], [query_ref, num_ref, ag_ref], in_sems)
    fetches = copies(
        [far_in.at[place_ref[e]] for e in range(entries)],
        [far_ref.at[pl.ds(e * BLK, BLK)] for e in range(entries)],
        far_sems,
    )
    loads[0].start()
    start_all(fetches)
    start_all(loads[1:])
    wait_all(loads)
    width = DEG * BLK

    for b in range(NB):
        rows = slice(b * BLK, (b + 1) * BLK)
        wait_all(fetches[b * DEG : (b + 1) * DEG])
        kv = far_ref[b * width : (b + 1) * width, :]
        prob = jnp.exp(dot_nt(query_ref[rows, :], kv))
        prob_ref[rows, :] = prob
        prob_low = prob.astype(BF16)
        prob_low_ref[rows, :] = prob_low
        values = jnp.where(lanes_low(kv.shape), jnp.asarray(1, BF16), kv)
        extra_ref[rows, :] = num_ref[rows, :] + dot(prob_low, values)
    for b in range(NB):
        rows = slice(b * BLK, (b + 1) * BLK)
        num = extra_ref[rows, :]
        den = jnp.where(lanes_low(num.shape), num, pltpu.roll(num, HD, 1))
        attn = num / den
        grad = ag_ref[rows, :]
        scaled = (grad / den).astype(BF16)
        scaled_ref[rows, :] = scaled
        extra_ref[rows, :] = jnp.sum(grad * attn, axis=1, keepdims=True) / den
        attn_ref[:, rows] = attn.T[HD:].astype(BF16)
        both_ref[:, rows] = (query_ref[rows, :] + scaled).astype(F32).T.astype(BF16)
    backs = []
    for b in range(NB):
        rows = slice(b * BLK, (b + 1) * BLK)
        kv = far_ref[b * width : (b + 1) * width, :]
        corr = extra_ref[rows, :]
        diff = dot_nt(scaled_ref[rows, :], kv) - corr[:, :1]
        score_grad = (prob_ref[rows, :] * diff).astype(BF16)
        extra_ref[rows, :] = jnp.where(lanes_low(corr.shape), dot(score_grad, kv), corr)
        key_grad = dot(both_ref[:HD, rows], score_grad).astype(BF16)
        value_grad = dot(both_ref[HD:, rows], prob_low_ref[rows, :]).astype(BF16)
        for j in range(DEG):
            e = b * DEG + j
            stage_ref[e, :HD, :] = key_grad[:, j * BLK : (j + 1) * BLK]
            stage_ref[e, HD:, :] = value_grad[:, j * BLK : (j + 1) * BLK]
            back = pltpu.make_async_copy(stage_ref.at[e], back_out.at[place_ref[e]], back_sems.at[e])
            back.start()
            backs.append(back)
    stores = copies([attn_ref, scaled_ref, extra_ref], [attn_out, scaled_out, extra_out], out_sems)
    start_all(stores)
    wait_all(backs)
    wait_all(stores)


def near_backward_body(col_ref, query_ref, kv_ref, count_ref, scaled_ref, extra_ref, attn_ref, hidden_ref, *refs):
    chunk_refs = refs[:NB]
    query_grad_ref, near_ref, part_ref, acc_ref = refs[NB:]
    col = col_ref[0]
    acc_ref[...] = jnp.zeros_like(acc_ref)

    def step(b, _):
        rows = rows_of(b)
        query, scaled, extra = query_ref[rows, :], scaled_ref[rows, :], extra_ref[rows, :]
        kv = kv_ref[...].reshape(ROWS, BLK)
        prob = jnp.exp(dot_nt(query, kv)) * count_ref[pl.ds(b, 1), :]
        diff = dot_nt(scaled, kv) - extra[:, HD : HD + 1]
        score_grad = (prob * diff).astype(BF16)
        query_grad = dot(score_grad, kv) + extra
        query_grad_ref[:, rows] = (query_grad.T[:HD] * SCALE).astype(BF16)
        both = (query + scaled).astype(F32).T.astype(BF16)
        acc_ref[:HD, :] += dot(both[:HD], score_grad)
        acc_ref[HD:, :] += dot(both[HD:], prob.astype(BF16))
        return 0

    lax.fori_loop(0, NB, step, 0)
    for n in range(NB):
        near_ref[n] = acc_ref[:, n * BLK : (n + 1) * BLK]
    part_ref[:HD, :] = dot(query_grad_ref[...], hidden_ref[...]).astype(BF16)
    out_part = jnp.zeros((HD, D), F32)
    for k in range(NB):
        out_part += dot(attn_ref[:, rows_of(block_before(col, k))], chunk_refs[k][...])
    part_ref[HD:, :] = out_part.astype(BF16)


def gather_grads_body(col_ref, home_ref, *refs):
    ins, outs, refs = refs[:6], refs[6 : 7 + NB], refs[7 + NB :]
    returned_in, near_in, query_grad_in, attn_in, hidden_in, early_in = ins
    *piece_refs, part_out = outs
    returned_ref, even_ref, odd_ref, proj_ref, hidden_ref, part_ref, in_sems, out_sems, far_sems = refs
    col = col_ref[0]
    parts = far_sems.shape[0]
    step = returned_in.shape[0] // parts
    fetches = copies(
        [returned_in.at[pl.ds(i * step, step)] for i in range(parts)],
        [returned_ref.at[pl.ds(i * step, step)] for i in range(parts)],
        far_sems,
    )
    loads = copies(
        [near_in, query_grad_in, attn_in, hidden_in, early_in.at[pl.ds(0, HD)], early_in.at[pl.ds(HD, HD)]],
        [
            even_ref.at[pl.ds(0, NB)],
            proj_ref.at[pl.ds(0, HD)],
            proj_ref.at[pl.ds(3 * HD, HD)],
            hidden_ref,
            part_ref.at[pl.ds(0, HD)],
            part_ref.at[pl.ds(3 * HD, HD)],
        ],
        in_sems,
    )
    start_all(loads[:1])
    start_all(fetches)
    start_all(loads[1:])
    odd_ref[...] = jnp.zeros_like(odd_ref)
    loads[0].wait()
    for i in range(parts):
        fetches[i].wait()

        def add(s, _):
            at = i * step + 2 * s
            even, odd = home_ref[at], home_ref[at + 1]
            even_ref[even] += returned_ref[at].astype(F32)
            odd_ref[odd] += returned_ref[at + 1].astype(F32)
            return 0

        lax.fori_loop(0, step // 2, add, 0, unroll=True)
    for n in range(NB):
        proj_ref[HD : 3 * HD, n * BLK : (n + 1) * BLK] = (even_ref[n] + odd_ref[n]).astype(BF16)
    wait_all(loads[1:])
    part_ref[HD : 3 * HD, :] = dot(proj_ref[HD : 3 * HD, :], hidden_ref[...]).astype(BF16)
    stores = copies(
        [part_ref, *(proj_ref.at[:, rows_of(block_after(col, k))] for k in range(NB))],
        [part_out, *piece_refs],
        out_sems,
    )
    start_all(stores)
    wait_all(stores)


def sum_body(share_ref, total_ref):
    total = jnp.sum(share_ref[...].astype(F32), axis=0).astype(BF16)
    total_ref[...] = jnp.broadcast_to(total[None], total_ref.shape)


def scale_body(inv_root, total_ref, qkv_ref, out_ref):
    total = total_ref[...].astype(F32) * inv_root
    qkv_ref[...] = total[: 3 * HD]
    out_ref[...] = total[3 * HD :]


def finish_body(*refs):
    piece_refs, weight_refs = refs[:NB], refs[NB : 2 * NB]
    state_ref, grad_ref, gain_ref, layer_ref, back_ref = refs[2 * NB :]
    out = jnp.zeros((BLK, D), F32)
    back = jnp.zeros((BLK, D), F32)
    for k in range(NB):
        terms = piece_refs[k][...].astype(F32).T.astype(BF16)
        back += dot(terms[:, : 3 * HD], weight_refs[k][: 3 * HD, :])
        out += dot(terms[:, 3 * HD :], weight_refs[k][3 * HD :, :])
    state = state_ref[...].astype(F32)
    gain = gain_ref[...]
    layer_ref[...] = (state + out).astype(BF16)
    inv = lax.rsqrt(jnp.mean(state * state, axis=1, keepdims=True) + EPS)
    stat = jnp.sum(gain * back * state, axis=1, keepdims=True)
    back_ref[...] = (
        grad_ref[...].astype(F32) + inv * gain * back - state * (inv * inv * inv * stat / D)
    ).astype(BF16)


def shards(
    node_states,
    norm_gain,
    qkv_weight,
    out_weight,
    local_slots,
    local_live,
    far_owner,
    far_slot,
    out_grad,
):
    doms = lax.axis_size("dom")
    me = lax.axis_index("dom")
    col = lax.axis_index("col").astype(jnp.int32).reshape(1)
    slots = doms * CAP
    gain = norm_gain[None]

    state_chunks = ring_gather(node_states, "col", NB)

    entries = NB * DEG
    owners = far_owner.reshape(doms, entries)
    wanted = far_slot.reshape(doms, entries)
    place = jnp.arange(entries, dtype=jnp.int32)
    before = place[None, :] < place[:, None]
    rank = jnp.sum((owners[:, :, None] == owners[:, None, :]) & before[None], axis=2, dtype=jnp.int32)
    mine = (owners == me)[:, None, :] & (
        rank[:, None, :] == jnp.arange(CAP, dtype=jnp.int32)[None, :, None]
    )
    home = jnp.min(jnp.where(mine, wanted[:, None, :], NB), axis=2).reshape(slots)
    send = jnp.minimum(home, NB - 1)
    places = (
        lax.dynamic_index_in_dim(owners, me, 0, keepdims=False) * CAP
        + lax.dynamic_index_in_dim(rank, me, 0, keepdims=False)
    )
    block = jnp.arange(NB, dtype=jnp.int32)
    hits = (local_slots[:, :, None] == block[None, None, :]) & (local_live[:, :, None] != 0)
    count = jnp.sum(hits, axis=1, dtype=jnp.int32) + (block[:, None] == block[None, :])
    count = jnp.repeat(count.astype(F32), BLK, axis=1)

    unit = 2 * ROWS * ROWS * BLK
    node = shaped(BLK, D)
    heads_node = shaped(ROWS, BLK)
    heads_float = shaped(ROWS, BLK, kind=F32)
    across = shaped(HD, ROWS)
    blocks = shaped(NB, BLK, BLK)
    exchanged = shaped(slots, BLK, BLK)
    row = shaped(1, D, kind=F32)
    counts = shaped(NB, ROWS, kind=F32)
    states = shaped(ROWS, D)
    piece = shaped(4 * HD, BLK)

    def gather_sems(n):
        return pltpu.SemaphoreType.DMA((n,))

    hidden, query, kv, outgoing = call(
        project_body,
        (states, heads_node, blocks, exchanged),
        [scalars()] * 2 + [left()] * (NB + 2),
        scratch=[
            *held([shaped(NB, BLK, D), row, shaped(3 * HD, D), states, heads_node, blocks, exchanged]),
            gather_sems(NB + 2),
            gather_sems(3 + 4),
        ],
        flops=2 * ROWS * D * 256,
        name="project",
    )(col, send, *state_chunks, gain, qkv_weight)

    outgoing, grad_own = lax.optimization_barrier((outgoing, out_grad))
    fetched = lax.all_to_all(outgoing, "dom", 0, 0, tiled=True)
    grad_chunks = ring_gather(grad_own, "col", NB)

    (near,) = call(
        **staged(near_forward_body, 0, [heads_node, blocks, counts], [heads_float], held([heads_node])),
        flops=2 * unit,
        name="near_forward",
    )(query, kv, count)

    (attn_grad,) = call(
        **staged(attn_grad_body, 1, [node] * NB + [shaped(HD, D)], [heads_float]),
        flops=2 * ROWS * D * BLK,
        name="attn_grad",
    )(col, *grad_chunks, out_weight)

    attn, scaled, extra, outgoing_back = call(
        far_body,
        (across, heads_node, heads_float, exchanged),
        [scalars()] + [left()] * 4,
        scratch=[
            *held([shaped(entries * BLK, BLK), heads_node, heads_float, heads_float]),
            *held([across, heads_node, heads_float]),
            *held([shaped(ROWS, DEG * BLK, kind=F32), shaped(ROWS, DEG * BLK), shaped(BLK, ROWS)]),
            *held([shaped(entries, BLK, BLK)]),
            gather_sems(entries),
            gather_sems(3),
            gather_sems(3),
            gather_sems(entries),
        ],
        flops=2 * unit,
        name="far_both",
    )(places, query, fetched, near, attn_grad)

    outgoing_back, weights_own = lax.optimization_barrier(
        (outgoing_back, jnp.concatenate([qkv_weight, out_weight], axis=0))
    )
    returned = lax.all_to_all(outgoing_back, "dom", 0, 0, tiled=True)
    weight_chunks = ring_gather(weights_own, "col", NB)

    query_grad, near_grad, early = call(
        **staged(
            near_backward_body,
            1,
            [heads_node, blocks, counts, heads_node, heads_float, across, states] + [node] * NB,
            [across, shaped(NB, BLK, BLK, kind=F32), shaped(2 * HD, D)],
            held([shaped(BLK, ROWS, kind=F32)]),
        ),
        flops=5 * unit,
        name="near_backward",
    )(col, query, kv, count, scaled, extra, attn, hidden, *grad_chunks)

    returned, near_grad, *weight_chunks = lax.optimization_barrier((returned, near_grad, *weight_chunks))

    *pieces, part = call(
        gather_grads_body,
        (piece,) * NB + (shaped(4 * HD, D),),
        [scalars()] * 2 + [left()] * 6,
        scratch=[
            *held([exchanged, shaped(NB + 1, BLK, BLK, kind=F32), shaped(NB + 1, BLK, BLK, kind=F32)]),
            *held([shaped(4 * HD, ROWS), states, shaped(4 * HD, D)]),
            gather_sems(6),
            gather_sems(1 + NB),
            gather_sems(4),
        ],
        flops=2 * ROWS * D * 128,
        name="gather_grads",
    )(col, home, returned, near_grad, query_grad, attn, hidden, early)

    share_rows = 4 * HD // doms
    shares = lax.all_to_all(part.reshape(doms, share_rows, D), "dom", 0, 0, tiled=True)
    arrived = ring_scatter(pieces, "col", NB)

    small = 4 * 1024 * 1024
    (totals,) = call(
        sum_body,
        (shaped(doms, share_rows, D),),
        [whole()],
        out_specs=[whole()],
        name="sum_shares",
        limit=small,
    )(shares)
    total = lax.all_to_all(totals, "dom", 0, 0, tiled=True).reshape(4 * HD, D)
    inv_root = 1.0 / math.sqrt(far_owner.shape[0] * BLK)
    qkv_grad, out_weight_grad = call(
        functools.partial(scale_body, inv_root),
        (shaped(3 * HD, D, kind=F32), shaped(HD, D, kind=F32)),
        [whole()],
        out_specs=[whole()] * 2,
        name="scale",
        limit=small,
    )(total)

    layer_out, state_grad = call(
        **staged(
            finish_body,
            0,
            [piece] * NB + [shaped(4 * HD, D)] * NB + [node, node, row],
            [node, node],
        ),
        flops=2 * BLK * D * 2048,
        name="finish",
    )(*arrived, *weight_chunks, node_states, out_grad, gain)

    return (layer_out, state_grad, qkv_grad, out_weight_grad)


def solution(mesh):
    placed = (
        P(("dom", "col"), None),
        P(),
        P("col", None),
        P("col", None),
        P("dom", None),
        P("dom", None),
        P(),
        P(),
        P(("dom", "col"), None),
    )
    return jax.shard_map(
        shards,
        mesh=mesh,
        in_specs=placed,
        out_specs=(
            P(("dom", "col"), None),
            P(("dom", "col"), None),
            P("col", None),
            P("col", None),
        ),
        check_vma=False,
    )
```

```python
import functools
import math

import jax
import jax.numpy as jnp
from jax import lax
from jax.experimental import pallas as pl
from jax.experimental.pallas import tpu as pltpu
from jax.sharding import PartitionSpec as P

D = 512
HD = 64
BLK = 128
NB = 8
DEG = 4
CAP = 2
ROWS = NB * BLK
EPS = 1e-06
SCALE = 1.0 / math.sqrt(HD)

F32 = jnp.float32
BF16 = jnp.bfloat16
MIB = 1024 * 1024
LIMIT = 64
ORDER = (0, 1, 7, 2, 6, 3, 5, 4)

NT = (((1,), (1,)), ((), ()))
TN = (((0,), (0,)), ((), ()))


def dot(a, b):
    return jnp.dot(a, b, preferred_element_type=F32)


def dot_nt(a, b):
    return lax.dot_general(a, b, NT, preferred_element_type=F32)


def whole():
    return pl.BlockSpec(memory_space=pltpu.VMEM)


def scalars():
    return pl.BlockSpec(memory_space=pltpu.SMEM)


def left():
    return pl.BlockSpec(memory_space=pl.ANY)


def shaped(*dims, kind=BF16):
    return jax.ShapeDtypeStruct(dims, kind)


def call(body, outs, ins, scratch=(), flops=0, name=None, out_specs=None, limit=LIMIT, aliases=None):
    return pl.pallas_call(
        body,
        out_shape=outs,
        in_specs=ins,
        out_specs=out_specs or [left() for _ in outs],
        scratch_shapes=list(scratch),
        input_output_aliases=aliases or {},
        compiler_params=pltpu.CompilerParams(vmem_limit_bytes=limit * MIB),
        cost_estimate=pl.CostEstimate(flops=flops, bytes_accessed=1 << 20, transcendentals=0),
        name=name,
    )


def held(*shapes):
    return [pltpu.VMEM(s.shape, s.dtype) for s in shapes]


def dma_sems(n):
    return pltpu.SemaphoreType.DMA((n,))


def copies(sources, targets, sems):
    return [
        pltpu.make_async_copy(a, b, sems.at[i]) for i, (a, b) in enumerate(zip(sources, targets, strict=True))
    ]


def start_all(jobs):
    for job in jobs:
        job.start()


def wait_all(jobs):
    for job in jobs:
        job.wait()


def lanes_low(shape):
    return lax.broadcasted_iota(jnp.int32, shape, len(shape) - 1) < HD


def rows_at(i):
    return slice(i * BLK, (i + 1) * BLK)


def shifted(x, k):
    return lax.ppermute(x, "col", [(i, (i + k) % NB) for i in range(NB)])


def ring_round(behind, ahead):
    return shifted(behind, 1), shifted(ahead, -1)


def block_at(col, i):
    return lax.rem(col + NB - ORDER[i], NB)


def tables_body(where_ref, owner_ref, slot_ref, near_ref, live_ref, place_ref, home_ref, count_ref):
    me, col = where_ref[0], where_ref[1]
    owner = owner_ref[...]
    lane = lax.broadcasted_iota(jnp.int32, owner.shape, 1)
    row = lax.rem(lane, NB)
    rank = jnp.zeros_like(owner)
    for d in range(1, NB):
        earlier = pltpu.roll(owner, d, 1)
        for j in range(DEG):
            same = (owner == earlier[j : j + 1, :]) & (row >= d)
            rank += same.astype(jnp.int32)
    place_ref[...] = owner * CAP + rank
    wanted = jnp.zeros_like(owner)
    for i in range(NB):
        wanted += jnp.where(slot_ref[...] == block_at(col, i), i, 0)
    for c in range(CAP):
        asked = jnp.where((owner == me) & (rank == c), wanted, NB)
        least = asked[0:1, :]
        for j in range(1, DEG):
            least = jnp.minimum(least, asked[j : j + 1, :])
        for d in (1, 2, 4):
            least = jnp.minimum(least, pltpu.roll(least, d, 1))
        home_ref[c : c + 1, :] = least
    near, live = near_ref[...], live_ref[...]
    own = lax.broadcasted_iota(jnp.int32, (NB, 1), 0)
    for i in range(NB):
        block = block_at(col, i)
        hits = ((near == block) & (live != 0)).astype(F32)
        count = jnp.sum(hits, axis=1, keepdims=True) + (own == block).astype(F32)
        count_ref[:, rows_at(i)] = jnp.broadcast_to(count, (NB, BLK))


def asked(home_ref, s):
    return home_ref[s % CAP, (s // CAP) * NB + NB - 1]


def normed(x_low, gain):
    x = x_low.astype(F32)
    inv = lax.rsqrt(jnp.mean(x * x, axis=1, keepdims=True) + EPS)
    return (x * inv * gain).astype(BF16)


def project(x_low, gain, wide):
    proj = dot_nt(normed(x_low, gain), wide).astype(BF16)
    return proj[:, :BLK] * jnp.asarray(SCALE, BF16), proj[:, BLK:]


def wide_weight(weight):
    return jnp.concatenate([weight[:HD], jnp.zeros((HD, D), BF16), weight[HD:]], axis=0)


def project_most_body(send_ref, *refs):
    chunk_ins, refs = refs[: NB - 1], refs[NB - 1 :]
    gain_in, weight_in, query_out, kv_out, sent_out, *refs = refs
    chunk_ref, gain_ref, weight_ref, hidden_ref, query_ref, kv_ref, sent_ref, *refs = refs
    in_sems, out_sems, sent_sems = refs
    loads = copies(
        [weight_in, gain_in, *chunk_ins],
        [weight_ref, gain_ref, *(chunk_ref.at[i] for i in range(NB - 1))],
        in_sems,
    )
    start_all(loads)
    wait_all(loads[:2])
    gain = gain_ref[...]
    wide = wide_weight(weight_ref[...])
    for i in range(NB - 1):
        loads[2 + i].wait()
        hidden_ref[rows_at(i), :] = normed(chunk_ref[i], gain)
    proj = dot_nt(hidden_ref[...], wide).astype(BF16)
    for i in range(NB - 1):
        query_ref[i] = proj[rows_at(i), :BLK] * jnp.asarray(SCALE, BF16)
        kv_ref[i] = proj[rows_at(i), BLK:]
    most = pl.ds(0, NB - 1)
    parts = sent_sems.shape[0]
    step = sent_ref.shape[0] // parts
    sends = copies(
        [sent_ref.at[pl.ds(i * step, step)] for i in range(parts)],
        [sent_out.at[pl.ds(i * step, step)] for i in range(parts)],
        sent_sems,
    )
    stores = copies([query_ref, kv_ref], [query_out.at[most], kv_out.at[most]], out_sems)
    start_all(stores)
    for i in range(parts):

        def fill(s, _):
            sent_ref[i * step + s] = kv_ref[jnp.minimum(asked(send_ref, i * step + s), NB - 2)]
            return 0

        lax.fori_loop(0, step, fill, 0, unroll=True)
        sends[i].start()
    wait_all(stores)
    wait_all(sends)


def project_last_body(send_ref, chunk_in, gain_in, weight_in, query_in, kv_in, sent_in, *refs):
    query_out, kv_out, sent_out, *refs = refs
    chunk_ref, gain_ref, weight_ref, query_ref, kv_ref, in_sems, out_sems, sent_sems = refs
    loads = copies([chunk_in, gain_in, weight_in], [chunk_ref, gain_ref, weight_ref], in_sems)
    start_all(loads)
    wait_all(loads)
    query_ref[...], kv_ref[...] = project(chunk_ref[...], gain_ref[...], wide_weight(weight_ref[...]))

    def over_slots(act):
        for slot in range(sent_sems.shape[0]):

            @pl.when(asked(send_ref, slot) == NB - 1)
            def _():
                act(pltpu.make_async_copy(kv_ref, sent_out.at[slot], sent_sems.at[slot]))

    over_slots(lambda job: job.start())
    stores = copies([query_ref, kv_ref], [query_out.at[NB - 1], kv_out.at[NB - 1]], out_sems)
    start_all(stores)
    over_slots(lambda job: job.wait())
    wait_all(stores)


def attn_grad_body(*refs):
    n = NB - 1
    chunk_ins, refs = refs[:n], refs[n:]
    weight_in, ag_out, chunk_ref, weight_ref, ag_ref, sems, out_sems = refs
    loads = copies([weight_in, *chunk_ins], [weight_ref, *(chunk_ref.at[i] for i in range(n))], sems)
    start_all(loads)
    wait_all(loads)
    wide = jnp.concatenate([jnp.zeros((HD, D), BF16), weight_ref[...]], axis=0)
    ag_ref[...] = dot_nt(chunk_ref[...].reshape(n * BLK, D), wide).reshape(n, BLK, BLK)
    store = pltpu.make_async_copy(ag_ref, ag_out.at[pl.ds(0, n)], out_sems.at[0])
    store.start()
    store.wait()


def attn_grad_last_body(chunk_in, weight_in, ag_in, ag_out, chunk_ref, weight_ref, ag_ref, sems, out_sems):
    loads = copies([chunk_in, weight_in], [chunk_ref, weight_ref], sems)
    start_all(loads)
    wait_all(loads)
    wide = jnp.concatenate([jnp.zeros((HD, D), BF16), weight_ref[...]], axis=0)
    ag_ref[...] = dot_nt(chunk_ref[...], wide)
    store = pltpu.make_async_copy(ag_ref, ag_out.at[NB - 1], out_sems.at[0])
    store.start()
    store.wait()


def near_forward_body(col_ref, query_in, kv_in, count_in, num_out, *refs):
    query_ref, kv_ref, count_ref, num_ref, ones_ref, in_sems, out_sems = refs
    loads = copies([kv_in, query_in, count_in], [kv_ref, query_ref, count_ref], in_sems)
    start_all(loads)
    wait_all(loads)
    kv = kv_ref[...].reshape(ROWS, BLK)
    ones_ref[...] = jnp.where(lanes_low(kv.shape), jnp.asarray(1, BF16), kv)
    stores = copies([num_ref.at[i] for i in range(NB)], [num_out.at[i] for i in range(NB)], out_sems)
    for i in range(NB):
        score = dot_nt(query_ref[i], kv_ref[...].reshape(ROWS, BLK))
        prob = jnp.exp(score) * count_ref[pl.ds(block_at(col_ref[0], i), 1), :]
        num_ref[i] = dot(prob.astype(BF16), ones_ref[...])
        stores[i].start()
    wait_all(stores)


def far_body(where_ref, place_ref, query_in, far_in, num_in, ag_in, *refs):
    attn_out, scaled_out, extra_out, back_out, *refs = refs
    query_ref, far_ref, num_ref, ag_ref, *refs = refs
    attn_ref, scaled_ref, extra_ref, prob_ref, prob_low_ref, diff_ref, den_ref, both_ref, stage_ref, *refs = refs
    far_sems, in_sems, out_sems, extra_sems, back_sems = refs
    me, col = where_ref[0], where_ref[1]
    places = [place_ref[j, me * NB + block_at(col, i)] for i in range(NB) for j in range(DEG)]
    parts = far_sems.shape[0]
    step = far_in.shape[0] // parts
    fetches = copies(
        [far_in.at[pl.ds(i * step, step)] for i in range(parts)],
        [far_ref.at[pl.ds(i * step, step)] for i in range(parts)],
        far_sems,
    )
    loads = copies([query_in, ag_in, num_in], [query_ref, ag_ref, num_ref], in_sems)
    loads[0].start()
    start_all(fetches)
    start_all(loads[1:])

    def keys(i):
        return jnp.concatenate([far_ref[places[i * DEG + j]] for j in range(DEG)], axis=0)

    wait_all(loads[:1])
    wait_all(fetches)
    wait_all(loads[1:2])
    for i in range(NB):
        kv = keys(i)
        both = jnp.concatenate([query_ref[i], ag_ref[i].astype(BF16)], axis=0)
        score = dot_nt(both, kv)
        prob = jnp.exp(score[:BLK])
        prob_ref[i] = prob
        diff_ref[i] = score[BLK:]
        prob_low = prob.astype(BF16)
        prob_low_ref[i] = prob_low
        values = jnp.where(lanes_low(kv.shape), jnp.asarray(1, BF16), kv)
        extra_ref[i] = dot(prob_low, values)
    loads[2].wait()
    stores = copies([attn_ref, scaled_ref], [attn_out, scaled_out], out_sems)
    for i in range(NB):
        num = num_ref[i] + extra_ref[i]
        den = jnp.where(lanes_low(num.shape), num, pltpu.roll(num, HD, 1))
        inv = 1.0 / den
        attn = num * inv
        grad = ag_ref[i]
        scaled = (grad * inv).astype(BF16)
        scaled_ref[i] = scaled
        den_ref[i] = inv
        extra_ref[i] = jnp.sum(grad * attn, axis=1, keepdims=True) * inv
        attn_ref[:, rows_at(i)] = attn.T[HD:].astype(BF16)
        both_ref[i] = (query_ref[i] + scaled).astype(F32).T.astype(BF16)
    start_all(stores)
    jobs = []
    for i in range(NB):
        kv = keys(i)
        corr = extra_ref[i]
        diff = diff_ref[i] * den_ref[i, :, :1] - corr[:, :1]
        score_grad = (prob_ref[i] * diff).astype(BF16)
        extra_ref[i] = jnp.where(lanes_low(corr.shape), dot(score_grad, kv), corr)
        key_grad = dot(both_ref[i, :HD], score_grad).astype(BF16)
        value_grad = dot(both_ref[i, HD:], prob_low_ref[i]).astype(BF16)
        for j in range(DEG):
            e = i * DEG + j
            stage_ref[e, :HD, :] = key_grad[:, rows_at(j)]
            stage_ref[e, HD:, :] = value_grad[:, rows_at(j)]
            jobs.append(pltpu.make_async_copy(stage_ref.at[e], back_out.at[places[e]], back_sems.at[e]))
            jobs[-1].start()
        jobs.append(pltpu.make_async_copy(extra_ref.at[i], extra_out.at[i], extra_sems.at[i]))
        jobs[-1].start()
    wait_all(stores)
    wait_all(jobs)


def near_backward_body(col_ref, *refs):
    grad_ins, state_ins, refs = refs[:NB], refs[NB : 2 * NB], refs[2 * NB :]
    gain_in, query_in, kv_in, count_in, scaled_in, extra_in, attn_in, *refs = refs
    query_grad_out, near_out, part_out, hidden_out, *refs = refs
    grad_ref, state_ref, gain_ref, query_ref, kv_ref, count_ref, scaled_ref, extra_ref, attn_ref, hidden_ref, *refs = refs
    query_grad_ref, near_ref, part_ref, acc_ref, in_sems, late_sems, out_sems = refs
    loads = copies(
        [kv_in, query_in, count_in, scaled_in, extra_in],
        [kv_ref, query_ref, count_ref, scaled_ref, extra_ref],
        in_sems,
    )
    late = copies(
        [gain_in, *state_ins, attn_in, *grad_ins],
        [
            gain_ref,
            *(state_ref.at[i] for i in range(NB)),
            attn_ref,
            *(grad_ref.at[i] for i in range(NB)),
        ],
        late_sems,
    )
    start_all(loads)
    start_all(late)
    wait_all(loads)
    acc_ref[...] = jnp.zeros_like(acc_ref)
    col = col_ref[0]
    for i in range(NB):
        query, scaled, extra = query_ref[i], scaled_ref[i], extra_ref[i]
        kv = kv_ref[...].reshape(ROWS, BLK)
        prob = jnp.exp(dot_nt(query, kv)) * count_ref[pl.ds(block_at(col, i), 1), :]
        diff = dot_nt(scaled, kv) - extra[:, HD : HD + 1]
        score_grad = (prob * diff).astype(BF16)
        query_grad = dot(score_grad, kv) + extra
        query_grad_ref[:, rows_at(i)] = (query_grad.T[:HD] * SCALE).astype(BF16)
        both = (query + scaled).astype(F32).T.astype(BF16)
        acc_ref[:HD, :] += dot(both[:HD], score_grad)
        acc_ref[HD:, :] += dot(both[HD:], prob.astype(BF16))
    for i in range(NB):
        near_ref[i] = acc_ref[:, rows_at(i)]
    stores = copies(
        [query_grad_ref, near_ref, hidden_ref, part_ref],
        [query_grad_out, near_out, hidden_out, part_out],
        out_sems,
    )
    start_all(stores[:2])
    wait_all(late)
    gain = gain_ref[...]
    for i in range(NB):
        hidden_ref[i] = normed(state_ref[i], gain)
    stores[2].start()
    part_ref[:HD, :] = dot(query_grad_ref[...], hidden_ref[...].reshape(ROWS, D)).astype(BF16)
    part_ref[HD:, :] = dot(attn_ref[...], grad_ref[...].reshape(ROWS, D)).astype(BF16)
    stores[3].start()
    wait_all(stores)


def gather_grads_body(home_ref, returned_in, near_in, query_grad_in, attn_in, hidden_in, early_in, *refs):
    piece_refs, refs = refs[:NB], refs[NB:]
    part_out, returned_ref, near_ref, even_ref, odd_ref, proj_ref, hidden_ref, part_ref, *refs = refs
    far_sems, in_sems, out_sems = refs
    parts = far_sems.shape[0]
    step = returned_in.shape[0] // parts
    fetches = copies(
        [returned_in.at[pl.ds(i * step, step)] for i in range(parts)],
        [returned_ref.at[pl.ds(i * step, step)] for i in range(parts)],
        far_sems,
    )
    loads = copies(
        [
            near_in,
            hidden_in,
            query_grad_in,
            attn_in,
            early_in.at[pl.ds(0, HD)],
            early_in.at[pl.ds(HD, HD)],
        ],
        [
            near_ref,
            hidden_ref,
            proj_ref.at[pl.ds(0, HD)],
            proj_ref.at[pl.ds(3 * HD, HD)],
            part_ref.at[pl.ds(0, HD)],
            part_ref.at[pl.ds(3 * HD, HD)],
        ],
        in_sems,
    )
    start_all(fetches)
    start_all(loads)
    even_ref[...] = jnp.zeros_like(even_ref)
    odd_ref[...] = jnp.zeros_like(odd_ref)
    for i in range(parts):
        fetches[i].wait()

        def add(s, _):
            at = i * step + 2 * s
            even, odd = asked(home_ref, at), asked(home_ref, at + 1)
            even_ref[even] += returned_ref[at].astype(F32)
            odd_ref[odd] += returned_ref[at + 1].astype(F32)
            return 0

        lax.fori_loop(0, step // 2, add, 0, unroll=True)
    wait_all(loads)
    for i in range(NB):
        proj_ref[HD : 3 * HD, rows_at(i)] = (near_ref[i] + (even_ref[i] + odd_ref[i])).astype(BF16)
    at = [ORDER.index((NB - k) % NB) for k in range(NB)]
    stores = copies(
        [part_ref, *(proj_ref.at[:, pl.ds(at[k] * BLK, BLK)] for k in range(NB))],
        [part_out, *piece_refs],
        out_sems,
    )
    start_all(stores[1:])
    hidden = hidden_ref[...].reshape(ROWS, D)
    part_ref[HD : 3 * HD, :] = dot(proj_ref[HD : 3 * HD, :], hidden).astype(BF16)
    stores[0].start()
    wait_all(stores)


def sum_body(share_ref, total_ref):
    total = jnp.sum(share_ref[...].astype(F32), axis=0).astype(BF16)
    total_ref[...] = jnp.broadcast_to(total[None], total_ref.shape)


def add_heads(piece_ins, weight_ins, piece_ref, weight_ref, piece_sems, weight_sems):
    n = len(piece_ins)
    pieces = copies(piece_ins, [piece_ref.at[k] for k in range(n)], piece_sems)
    weights = copies(weight_ins, [weight_ref.at[k] for k in range(n)], weight_sems)
    for k in range(n):
        pieces[k].start()
        weights[k].start()
    out = jnp.zeros((BLK, D), F32)
    back = jnp.zeros((BLK, D), F32)
    for k in range(n):
        pieces[k].wait()
        terms = piece_ref[k].astype(F32).T.astype(BF16)
        weights[k].wait()
        back += dot(terms[:, : 3 * HD], weight_ref[k, : 3 * HD, :])
        out += dot(terms[:, 3 * HD :], weight_ref[k, 3 * HD :, :])
    return out, back


def first_heads_body(n, *refs):
    piece_ins, weight_ins, (sum_out, piece_ref, weight_ref, sum_ref, *sems, out_sem) = (
        refs[:n],
        refs[n : 2 * n],
        refs[2 * n :],
    )
    sum_ref[0], sum_ref[1] = add_heads(piece_ins, weight_ins, piece_ref, weight_ref, *sems)
    store = pltpu.make_async_copy(sum_ref, sum_out, out_sem.at[0])
    store.start()
    store.wait()


def finish_body(inv_root, n, *refs):
    piece_ins, weight_ins, refs = refs[:n], refs[n : 2 * n], refs[2 * n :]
    sum_in, state_in, grad_in, gain_in, total_in, layer_out, back_out, qkv_out, weight_out, *refs = refs
    piece_ref, weight_ref, sum_ref, state_ref, grad_ref, gain_ref, total_ref, layer_ref, back_ref, scaled_ref, *refs = refs
    piece_sems, weight_sems, in_sems, out_sems = refs
    loads = copies(
        [total_in, sum_in, state_in, grad_in, gain_in],
        [total_ref, sum_ref, state_ref, grad_ref, gain_ref],
        in_sems,
    )
    stores = copies(
        [scaled_ref.at[pl.ds(0, 3 * HD)], scaled_ref.at[pl.ds(3 * HD, HD)], layer_ref, back_ref],
        [qkv_out, weight_out, layer_out, back_out],
        out_sems,
    )
    start_all(loads)
    out, back = add_heads(piece_ins, weight_ins, piece_ref, weight_ref, piece_sems, weight_sems)
    loads[0].wait()
    scaled_ref[...] = total_ref[...].astype(F32) * inv_root
    start_all(stores[:2])
    wait_all(loads[1:])
    out += sum_ref[0]
    back += sum_ref[1]
    state = state_ref[...].astype(F32)
    gain = gain_ref[...]
    layer_ref[...] = (state + out).astype(BF16)
    stores[2].start()
    inv = lax.rsqrt(jnp.mean(state * state, axis=1, keepdims=True) + EPS)
    stat = jnp.sum(gain * back * state, axis=1, keepdims=True)
    back_ref[...] = (
        grad_ref[...].astype(F32) + inv * gain * back - state * (inv * inv * inv * stat / D)
    ).astype(BF16)
    stores[3].start()
    wait_all(stores)


def shards(
    node_states,
    norm_gain,
    qkv_weight,
    out_weight,
    local_slots,
    local_live,
    far_owner,
    far_slot,
    out_grad,
):
    doms = lax.axis_size("dom")
    me = lax.axis_index("dom")
    col_index = lax.axis_index("col").astype(jnp.int32)
    col = col_index.reshape(1)
    slots = doms * CAP
    entries = NB * DEG
    gain = norm_gain[None]

    where = jnp.stack([me.astype(jnp.int32), col_index])
    names = shaped(*far_owner.shape[::-1], kind=jnp.int32)
    places, home, count = call(
        tables_body,
        (names, shaped(CAP, far_owner.shape[0], kind=jnp.int32), shaped(NB, ROWS, kind=F32)),
        [scalars()] + [whole()] * 4,
        out_specs=[whole()] * 3,
        name="tables",
    )(where, far_owner.T, far_slot.T, local_slots, local_live)

    unit = 2 * ROWS * ROWS * BLK
    node = shaped(BLK, D)
    across = shaped(HD, ROWS)
    block, blocks, blocks_float = shaped(BLK, BLK), shaped(NB, BLK, BLK), shaped(NB, BLK, BLK, kind=F32)
    blocks_most = shaped(NB - 1, BLK, BLK)
    wide, wide_float = shaped(NB, BLK, DEG * BLK), shaped(NB, BLK, DEG * BLK, kind=F32)
    exchanged = shaped(slots, BLK, BLK)
    row = shaped(1, D, kind=F32)
    counts = shaped(NB, ROWS, kind=F32)
    states, states_most = shaped(NB, BLK, D), shaped(NB - 1, BLK, D)
    piece = shaped(4 * HD, BLK)
    head_weight, out_piece = shaped(3 * HD, D), shaped(HD, D)

    x1, x7 = ring_round(node_states, node_states)
    x1, x7, home, places, count = lax.optimization_barrier((x1, x7, home, places, count))
    x2, x6 = ring_round(x1, x7)
    x3, x5 = ring_round(x2, x6)
    x4 = shifted(x3, 1)
    state_chunks = (node_states, x1, x7, x2, x6, x3, x5, x4)
    projected = call(
        project_most_body,
        (blocks, blocks, exchanged),
        [scalars()] + [left()] * (NB + 1),
        scratch=[
            *held(states_most, row, head_weight, shaped((NB - 1) * BLK, D), blocks_most, blocks_most, exchanged),
            dma_sems(NB + 1),
            dma_sems(2),
            dma_sems(4),
        ],
        flops=2 * ROWS * D * 256,
        name="project_most",
    )(home, node_states, x1, x7, x2, x6, x3, x5, gain, qkv_weight)
    query, kv, outgoing = call(
        project_last_body,
        (blocks, blocks, exchanged),
        [scalars()] + [left()] * 6,
        scratch=[
            *held(node, row, head_weight, block, block),
            dma_sems(3),
            dma_sems(2),
            dma_sems(slots),
        ],
        flops=2 * BLK * D * 256,
        name="project_last",
        aliases={4: 0, 5: 1, 6: 2},
    )(home, x4, gain, qkv_weight, *projected)

    outgoing, grad_own = lax.optimization_barrier((outgoing, out_grad))
    fetched = lax.all_to_all(outgoing, "dom", 0, 0, tiled=True)
    g1, g7 = ring_round(grad_own, grad_own)
    g2, g6 = ring_round(g1, g7)
    g3, g5 = ring_round(g2, g6)
    g4 = shifted(g3, 1)
    grad_chunks = (out_grad, g1, g7, g2, g6, g3, g5, g4)

    (attn_grad,) = call(
        attn_grad_body,
        (blocks_float,),
        [left()] * NB,
        scratch=[
            *held(states_most, out_piece, shaped(NB - 1, BLK, BLK, kind=F32)),
            dma_sems(NB),
            dma_sems(1),
        ],
        flops=2 * ROWS * D * BLK,
        name="attn_grad",
    )(*grad_chunks[:-1], out_weight)

    (near,) = call(
        near_forward_body,
        (blocks_float,),
        [scalars()] + [left()] * 3,
        scratch=[*held(blocks, blocks, counts, blocks_float, shaped(ROWS, BLK)), dma_sems(3), dma_sems(NB)],
        flops=2 * unit,
        name="near_forward",
    )(col, query, kv, count)

    (attn_grad,) = call(
        attn_grad_last_body,
        (blocks_float,),
        [left()] * 3,
        scratch=[*held(node, out_piece, shaped(BLK, BLK, kind=F32)), dma_sems(2), dma_sems(1)],
        flops=2 * BLK * D * BLK,
        name="attn_grad_last",
        aliases={2: 0},
    )(g4, out_weight, attn_grad)

    attn, scaled, extra, outgoing_back = call(
        far_body,
        (across, blocks, blocks_float, exchanged),
        [scalars()] * 2 + [left()] * 4,
        scratch=[
            *held(blocks, exchanged, blocks_float, blocks_float),
            *held(across, blocks, blocks_float, wide_float, wide, wide_float, blocks_float),
            *held(blocks, shaped(entries, BLK, BLK)),
            dma_sems(4),
            dma_sems(3),
            dma_sems(2),
            dma_sems(NB),
            dma_sems(entries),
        ],
        flops=2 * unit,
        name="far_both",
    )(where, places, query, fetched, near, attn_grad)

    outgoing_back, weights_own = lax.optimization_barrier(
        (outgoing_back, jnp.concatenate([qkv_weight, out_weight], axis=0))
    )
    returned = lax.all_to_all(outgoing_back, "dom", 0, 0, tiled=True)
    w1, w7 = ring_round(weights_own, weights_own)
    w2, w6 = ring_round(w1, w7)

    query_grad, near_grad, early, hidden = call(
        near_backward_body,
        (across, blocks_float, shaped(2 * HD, D), states),
        [scalars()] + [left()] * (2 * NB + 7),
        scratch=[
            *held(states, states, row, blocks, blocks, counts, blocks, blocks_float, across, states),
            *held(across, blocks_float, shaped(2 * HD, D), shaped(BLK, ROWS, kind=F32)),
            dma_sems(5),
            dma_sems(2 * NB + 2),
            dma_sems(4),
        ],
        flops=5 * unit,
        name="near_backward",
    )(col, *grad_chunks, *state_chunks, gain, query, kv, count, scaled, extra, attn)

    w2, w6, near_grad = lax.optimization_barrier((w2, w6, near_grad))
    w3, w5 = ring_round(w2, w6)
    returned, w3, w5 = lax.optimization_barrier((returned, w3, w5))
    w4 = shifted(w3, 1)

    *pieces, part = call(
        gather_grads_body,
        (piece,) * NB + (shaped(4 * HD, D),),
        [scalars()] + [left()] * 6,
        scratch=[
            *held(exchanged, blocks_float, shaped(NB + 1, BLK, BLK, kind=F32)),
            *held(shaped(NB + 1, BLK, BLK, kind=F32), shaped(4 * HD, ROWS), states, shaped(4 * HD, D)),
            dma_sems(4),
            dma_sems(6),
            dma_sems(1 + NB),
        ],
        flops=2 * ROWS * D * 128,
        name="gather_grads",
    )(home, returned, near_grad, query_grad, attn, hidden, early)

    share_rows = 4 * HD // doms
    shares = lax.all_to_all(part.reshape(doms, share_rows, D), "dom", 0, 0, tiled=True)
    arrived = [pieces[0], *(shifted(pieces[k], k) for k in range(1, NB))]

    (totals,) = call(
        sum_body,
        (shaped(doms, share_rows, D),),
        [whole()],
        out_specs=[whole()],
        name="sum_shares",
        limit=4,
    )(shares)
    total = lax.all_to_all(totals, "dom", 0, 0, tiled=True).reshape(4 * HD, D)
    weights = (weights_own, w1, w2, w3, w4, w5, w6, w7)
    cut = 5
    sums = shaped(2, BLK, D, kind=F32)
    (first,) = call(
        functools.partial(first_heads_body, cut),
        (sums,),
        [left()] * (2 * cut),
        scratch=[
            *held(shaped(cut, 4 * HD, BLK), shaped(cut, 4 * HD, D), sums),
            dma_sems(cut),
            dma_sems(cut),
            dma_sems(1),
        ],
        flops=2 * BLK * D * 256 * cut,
        name="first_heads",
    )(*arrived[:cut], *weights[:cut])
    rest = NB - cut
    total_shape, total_float = shaped(4 * HD, D), shaped(4 * HD, D, kind=F32)
    layer_out, state_grad, qkv_grad, out_weight_grad = call(
        functools.partial(finish_body, 1.0 / math.sqrt(far_owner.shape[0] * BLK), rest),
        (node, node, shaped(3 * HD, D, kind=F32), shaped(HD, D, kind=F32)),
        [left()] * (2 * rest + 5),
        scratch=[
            *held(shaped(rest, 4 * HD, BLK), shaped(rest, 4 * HD, D), sums, node, node, row, total_shape),
            *held(node, node, total_float),
            dma_sems(rest),
            dma_sems(rest),
            dma_sems(5),
            dma_sems(4),
        ],
        flops=2 * BLK * D * 256 * rest,
        name="finish",
    )(*arrived[cut:], *weights[cut:], first, node_states, out_grad, gain, total)

    return (layer_out, state_grad, qkv_grad, out_weight_grad)


def solution(mesh):
    placed = (
        P(("dom", "col"), None),
        P(),
        P("col", None),
        P("col", None),
        P("dom", None),
        P("dom", None),
        P(),
        P(),
        P(("dom", "col"), None),
    )
    return jax.shard_map(
        shards,
        mesh=mesh,
        in_specs=placed,
        out_specs=(
            P(("dom", "col"), None),
            P(("dom", "col"), None),
            P("col", None),
            P("col", None),
        ),
        check_vma=False,
    )
```

```python
import functools
import math

import jax
import jax.numpy as jnp
from jax import lax
from jax.experimental import pallas as pl
from jax.experimental.pallas import tpu as pltpu
from jax.sharding import PartitionSpec as P

D = 512
HD = 64
BLK = 128
NB = 8
DEG = 4
CAP = 2
ROWS = NB * BLK
EPS = 1e-06
SCALE = 1.0 / math.sqrt(HD)

F32 = jnp.float32
BF16 = jnp.bfloat16
MIB = 1024 * 1024
LIMIT = 64
ORDER = (0, 1, 7, 2, 6, 3, 5, 4)

NT = (((1,), (1,)), ((), ()))
TN = (((0,), (0,)), ((), ()))


def dot(a, b):
    return jnp.dot(a, b, preferred_element_type=F32)


def dot_nt(a, b):
    return lax.dot_general(a, b, NT, preferred_element_type=F32)


def whole():
    return pl.BlockSpec(memory_space=pltpu.VMEM)


def scalars():
    return pl.BlockSpec(memory_space=pltpu.SMEM)


def left():
    return pl.BlockSpec(memory_space=pl.ANY)


def shaped(*dims, kind=BF16):
    return jax.ShapeDtypeStruct(dims, kind)


def call(body, outs, ins, scratch=(), flops=0, name=None, out_specs=None, limit=LIMIT, aliases=None):
    return pl.pallas_call(
        body,
        out_shape=outs,
        in_specs=ins,
        out_specs=out_specs or [left() for _ in outs],
        scratch_shapes=list(scratch),
        input_output_aliases=aliases or {},
        compiler_params=pltpu.CompilerParams(vmem_limit_bytes=limit * MIB),
        cost_estimate=pl.CostEstimate(flops=flops, bytes_accessed=1 << 20, transcendentals=0),
        name=name,
    )


def held(*shapes):
    return [pltpu.VMEM(s.shape, s.dtype) for s in shapes]


def dma_sems(n):
    return pltpu.SemaphoreType.DMA((n,))


def copies(sources, targets, sems):
    return [
        pltpu.make_async_copy(a, b, sems.at[i]) for i, (a, b) in enumerate(zip(sources, targets, strict=True))
    ]


def start_all(jobs):
    for job in jobs:
        job.start()


def wait_all(jobs):
    for job in jobs:
        job.wait()


def lanes_low(shape):
    return lax.broadcasted_iota(jnp.int32, shape, len(shape) - 1) < HD


def rows_at(i):
    return slice(i * BLK, (i + 1) * BLK)


def shifted(x, k):
    return lax.ppermute(x, "col", [(i, (i + k) % NB) for i in range(NB)])


def ring_round(behind, ahead):
    return shifted(behind, 1), shifted(ahead, -1)


def paired(x):
    return lax.ppermute(x, "col", [(i, i ^ 1) for i in range(NB)])


def block_at(col, i):
    return lax.rem(col + NB - ORDER[i], NB)


def tables_body(where_ref, owner_ref, slot_ref, near_ref, live_ref, place_ref, home_ref, count_ref):
    me, col = where_ref[0], where_ref[1]
    owner = owner_ref[...]
    lane = lax.broadcasted_iota(jnp.int32, owner.shape, 1)
    row = lax.rem(lane, NB)
    rank = jnp.zeros_like(owner)
    for d in range(1, NB):
        earlier = pltpu.roll(owner, d, 1)
        for j in range(DEG):
            same = (owner == earlier[j : j + 1, :]) & (row >= d)
            rank += same.astype(jnp.int32)
    place_ref[...] = owner * CAP + rank
    wanted = jnp.zeros_like(owner)
    for i in range(NB):
        wanted += jnp.where(slot_ref[...] == block_at(col, i), i, 0)
    for c in range(CAP):
        asked = jnp.where((owner == me) & (rank == c), wanted, NB)
        least = asked[0:1, :]
        for j in range(1, DEG):
            least = jnp.minimum(least, asked[j : j + 1, :])
        for d in (1, 2, 4):
            least = jnp.minimum(least, pltpu.roll(least, d, 1))
        home_ref[c : c + 1, :] = least
    near, live = near_ref[...], live_ref[...]
    own = lax.broadcasted_iota(jnp.int32, (NB, 1), 0)
    for i in range(NB):
        block = block_at(col, i)
        hits = ((near == block) & (live != 0)).astype(F32)
        count = jnp.sum(hits, axis=1, keepdims=True) + (own == block).astype(F32)
        count_ref[:, rows_at(i)] = jnp.broadcast_to(count, (NB, BLK))


def asked(home_ref, s):
    return home_ref[s % CAP, (s // CAP) * NB + NB - 1]


def normed(x_low, gain):
    x = x_low.astype(F32)
    inv = lax.rsqrt(jnp.mean(x * x, axis=1, keepdims=True) + EPS)
    return (x * inv * gain).astype(BF16)


def project(x_low, gain, wide):
    proj = dot_nt(normed(x_low, gain), wide).astype(BF16)
    return proj[:, :BLK] * jnp.asarray(SCALE, BF16), proj[:, BLK:]


def wide_weight(weight):
    return jnp.concatenate([weight[:HD], jnp.zeros((HD, D), BF16), weight[HD:]], axis=0)


def project_most_body(send_ref, *refs):
    chunk_ins, refs = refs[: NB - 1], refs[NB - 1 :]
    gain_in, weight_in, query_out, kv_out, sent_out, *refs = refs
    chunk_ref, gain_ref, weight_ref, hidden_ref, query_ref, kv_ref, sent_ref, *refs = refs
    in_sems, out_sems, sent_sems = refs
    loads = copies(
        [weight_in, gain_in, *chunk_ins],
        [weight_ref, gain_ref, *(chunk_ref.at[i] for i in range(NB - 1))],
        in_sems,
    )
    start_all(loads)
    wait_all(loads[:2])
    gain = gain_ref[...]
    wide = wide_weight(weight_ref[...])
    for i in range(NB - 1):
        loads[2 + i].wait()
        hidden_ref[rows_at(i), :] = normed(chunk_ref[i], gain)
    proj = dot_nt(hidden_ref[...], wide).astype(BF16)
    for i in range(NB - 1):
        query_ref[i] = proj[rows_at(i), :BLK] * jnp.asarray(SCALE, BF16)
        kv_ref[i] = proj[rows_at(i), BLK:]
    most = pl.ds(0, NB - 1)
    parts = sent_sems.shape[0]
    step = sent_ref.shape[0] // parts
    sends = copies(
        [sent_ref.at[pl.ds(i * step, step)] for i in range(parts)],
        [sent_out.at[pl.ds(i * step, step)] for i in range(parts)],
        sent_sems,
    )
    stores = copies([query_ref, kv_ref], [query_out.at[most], kv_out.at[most]], out_sems)
    start_all(stores)
    for i in range(parts):

        def fill(s, _):
            sent_ref[i * step + s] = kv_ref[jnp.minimum(asked(send_ref, i * step + s), NB - 2)]
            return 0

        lax.fori_loop(0, step, fill, 0, unroll=True)
        sends[i].start()
    wait_all(stores)
    wait_all(sends)


def project_last_body(send_ref, chunk_in, gain_in, weight_in, query_in, kv_in, sent_in, *refs):
    query_out, kv_out, sent_out, *refs = refs
    chunk_ref, gain_ref, weight_ref, query_ref, kv_ref, in_sems, out_sems, sent_sems = refs
    loads = copies([chunk_in, gain_in, weight_in], [chunk_ref, gain_ref, weight_ref], in_sems)
    start_all(loads)
    wait_all(loads)
    query_ref[...], kv_ref[...] = project(chunk_ref[...], gain_ref[...], wide_weight(weight_ref[...]))

    def over_slots(act):
        for slot in range(sent_sems.shape[0]):

            @pl.when(asked(send_ref, slot) == NB - 1)
            def _():
                act(pltpu.make_async_copy(kv_ref, sent_out.at[slot], sent_sems.at[slot]))

    over_slots(lambda job: job.start())
    stores = copies([query_ref, kv_ref], [query_out.at[NB - 1], kv_out.at[NB - 1]], out_sems)
    start_all(stores)
    over_slots(lambda job: job.wait())
    wait_all(stores)


def attn_grad_body(*refs):
    n = NB - 1
    chunk_ins, refs = refs[:n], refs[n:]
    weight_in, ag_out, chunk_ref, weight_ref, ag_ref, sems, out_sems = refs
    loads = copies([weight_in, *chunk_ins], [weight_ref, *(chunk_ref.at[i] for i in range(n))], sems)
    start_all(loads)
    wait_all(loads)
    wide = jnp.concatenate([jnp.zeros((HD, D), BF16), weight_ref[...]], axis=0)
    ag_ref[...] = dot_nt(chunk_ref[...].reshape(n * BLK, D), wide).reshape(n, BLK, BLK)
    store = pltpu.make_async_copy(ag_ref, ag_out.at[pl.ds(0, n)], out_sems.at[0])
    store.start()
    store.wait()


def attn_grad_last_body(chunk_in, weight_in, ag_in, ag_out, chunk_ref, weight_ref, ag_ref, sems, out_sems):
    loads = copies([chunk_in, weight_in], [chunk_ref, weight_ref], sems)
    start_all(loads)
    wait_all(loads)
    wide = jnp.concatenate([jnp.zeros((HD, D), BF16), weight_ref[...]], axis=0)
    ag_ref[...] = dot_nt(chunk_ref[...], wide)
    store = pltpu.make_async_copy(ag_ref, ag_out.at[NB - 1], out_sems.at[0])
    store.start()
    store.wait()


def near_forward_body(col_ref, query_in, kv_in, count_in, num_out, *refs):
    query_ref, kv_ref, count_ref, num_ref, ones_ref, in_sems, out_sems = refs
    loads = copies([kv_in, query_in, count_in], [kv_ref, query_ref, count_ref], in_sems)
    start_all(loads)
    wait_all(loads)
    kv = kv_ref[...].reshape(ROWS, BLK)
    ones_ref[...] = jnp.where(lanes_low(kv.shape), jnp.asarray(1, BF16), kv)
    stores = copies([num_ref.at[i] for i in range(NB)], [num_out.at[i] for i in range(NB)], out_sems)
    for i in range(NB):
        score = dot_nt(query_ref[i], kv_ref[...].reshape(ROWS, BLK))
        prob = jnp.exp(score) * count_ref[pl.ds(block_at(col_ref[0], i), 1), :]
        num_ref[i] = dot(prob.astype(BF16), ones_ref[...])
        stores[i].start()
    wait_all(stores)


def far_body(where_ref, place_ref, query_in, far_in, num_in, ag_in, *refs):
    attn_out, scaled_out, extra_out, back_out, *refs = refs
    query_ref, far_ref, num_ref, ag_ref, *refs = refs
    attn_ref, scaled_ref, extra_ref, prob_ref, prob_low_ref, diff_ref, den_ref, both_ref, stage_ref, *refs = refs
    far_sems, in_sems, out_sems, extra_sems, back_sems = refs
    me, col = where_ref[0], where_ref[1]
    places = [place_ref[j, me * NB + block_at(col, i)] for i in range(NB) for j in range(DEG)]
    parts = far_sems.shape[0]
    step = far_in.shape[0] // parts
    fetches = copies(
        [far_in.at[pl.ds(i * step, step)] for i in range(parts)],
        [far_ref.at[pl.ds(i * step, step)] for i in range(parts)],
        far_sems,
    )
    loads = copies([query_in, ag_in, num_in], [query_ref, ag_ref, num_ref], in_sems)
    loads[0].start()
    start_all(fetches)
    start_all(loads[1:])

    def keys(i):
        return jnp.concatenate([far_ref[places[i * DEG + j]] for j in range(DEG)], axis=0)

    wait_all(loads[:1])
    wait_all(fetches)
    wait_all(loads[1:2])
    for i in range(NB):
        kv = keys(i)
        both = jnp.concatenate([query_ref[i], ag_ref[i].astype(BF16)], axis=0)
        score = dot_nt(both, kv)
        prob = jnp.exp(score[:BLK])
        prob_ref[i] = prob
        diff_ref[i] = score[BLK:]
        prob_low = prob.astype(BF16)
        prob_low_ref[i] = prob_low
        values = jnp.where(lanes_low(kv.shape), jnp.asarray(1, BF16), kv)
        extra_ref[i] = dot(prob_low, values)
    loads[2].wait()
    stores = copies([attn_ref, scaled_ref], [attn_out, scaled_out], out_sems)
    for i in range(NB):
        num = num_ref[i] + extra_ref[i]
        den = jnp.where(lanes_low(num.shape), num, pltpu.roll(num, HD, 1))
        inv = 1.0 / den
        attn = num * inv
        grad = ag_ref[i]
        scaled = (grad * inv).astype(BF16)
        scaled_ref[i] = scaled
        den_ref[i] = inv
        extra_ref[i] = jnp.sum(grad * attn, axis=1, keepdims=True) * inv
        attn_ref[:, rows_at(i)] = attn.T[HD:].astype(BF16)
        both_ref[i] = (query_ref[i] + scaled).astype(F32).T.astype(BF16)
    start_all(stores)
    jobs = []
    for i in range(NB):
        kv = keys(i)
        corr = extra_ref[i]
        diff = diff_ref[i] * den_ref[i, :, :1] - corr[:, :1]
        score_grad = (prob_ref[i] * diff).astype(BF16)
        extra_ref[i] = jnp.where(lanes_low(corr.shape), dot(score_grad, kv), corr)
        key_grad = dot(both_ref[i, :HD], score_grad).astype(BF16)
        value_grad = dot(both_ref[i, HD:], prob_low_ref[i]).astype(BF16)
        for j in range(DEG):
            e = i * DEG + j
            stage_ref[e, :HD, :] = key_grad[:, rows_at(j)]
            stage_ref[e, HD:, :] = value_grad[:, rows_at(j)]
            jobs.append(pltpu.make_async_copy(stage_ref.at[e], back_out.at[places[e]], back_sems.at[e]))
            jobs[-1].start()
        jobs.append(pltpu.make_async_copy(extra_ref.at[i], extra_out.at[i], extra_sems.at[i]))
        jobs[-1].start()
    wait_all(stores)
    wait_all(jobs)


def near_backward_body(col_ref, *refs):
    grad_ins, state_ins, refs = refs[:NB], refs[NB : 2 * NB], refs[2 * NB :]
    gain_in, query_in, kv_in, count_in, scaled_in, extra_in, attn_in, *refs = refs
    query_grad_out, near_out, part_out, hidden_out, *refs = refs
    grad_ref, state_ref, gain_ref, query_ref, kv_ref, count_ref, scaled_ref, extra_ref, attn_ref, hidden_ref, *refs = refs
    query_grad_ref, near_ref, part_ref, acc_ref, in_sems, late_sems, out_sems = refs
    loads = copies(
        [kv_in, query_in, count_in, scaled_in, extra_in],
        [kv_ref, query_ref, count_ref, scaled_ref, extra_ref],
        in_sems,
    )
    late = copies(
        [gain_in, *state_ins, attn_in, *grad_ins],
        [
            gain_ref,
            *(state_ref.at[i] for i in range(NB)),
            attn_ref,
            *(grad_ref.at[i] for i in range(NB)),
        ],
        late_sems,
    )
    start_all(loads)
    start_all(late)
    wait_all(loads)
    acc_ref[...] = jnp.zeros_like(acc_ref)
    col = col_ref[0]
    for i in range(NB):
        query, scaled, extra = query_ref[i], scaled_ref[i], extra_ref[i]
        kv = kv_ref[...].reshape(ROWS, BLK)
        prob = jnp.exp(dot_nt(query, kv)) * count_ref[pl.ds(block_at(col, i), 1), :]
        diff = dot_nt(scaled, kv) - extra[:, HD : HD + 1]
        score_grad = (prob * diff).astype(BF16)
        query_grad = dot(score_grad, kv) + extra
        query_grad_ref[:, rows_at(i)] = (query_grad.T[:HD] * SCALE).astype(BF16)
        both = (query + scaled).astype(F32).T.astype(BF16)
        acc_ref[:HD, :] += dot(both[:HD], score_grad)
        acc_ref[HD:, :] += dot(both[HD:], prob.astype(BF16))
    for i in range(NB):
        near_ref[i] = acc_ref[:, rows_at(i)]
    stores = copies(
        [query_grad_ref, near_ref, hidden_ref, part_ref],
        [query_grad_out, near_out, hidden_out, part_out],
        out_sems,
    )
    start_all(stores[:2])
    wait_all(late)
    gain = gain_ref[...]
    for i in range(NB):
        hidden_ref[i] = normed(state_ref[i], gain)
    stores[2].start()
    part_ref[:HD, :] = dot(query_grad_ref[...], hidden_ref[...].reshape(ROWS, D)).astype(BF16)
    part_ref[HD:, :] = dot(attn_ref[...], grad_ref[...].reshape(ROWS, D)).astype(BF16)
    stores[3].start()
    wait_all(stores)


def gather_grads_body(col_ref, home_ref, returned_in, near_in, query_grad_in, attn_in, hidden_in, early_in, *refs):
    *pair_outs, part_out = refs[: 1 + NB // 2]
    refs = refs[1 + NB // 2 :]
    returned_ref, near_ref, even_ref, odd_ref, proj_ref, hidden_ref, part_ref, *refs = refs
    far_sems, in_sems, out_sems = refs
    parts = far_sems.shape[0]
    step = returned_in.shape[0] // parts
    fetches = copies(
        [returned_in.at[pl.ds(i * step, step)] for i in range(parts)],
        [returned_ref.at[pl.ds(i * step, step)] for i in range(parts)],
        far_sems,
    )
    loads = copies(
        [
            near_in,
            hidden_in,
            query_grad_in,
            attn_in,
            early_in.at[pl.ds(0, HD)],
            early_in.at[pl.ds(HD, HD)],
        ],
        [
            near_ref,
            hidden_ref,
            proj_ref.at[pl.ds(0, HD)],
            proj_ref.at[pl.ds(3 * HD, HD)],
            part_ref.at[pl.ds(0, HD)],
            part_ref.at[pl.ds(3 * HD, HD)],
        ],
        in_sems,
    )
    start_all(fetches)
    start_all(loads)
    even_ref[...] = jnp.zeros_like(even_ref)
    odd_ref[...] = jnp.zeros_like(odd_ref)
    for i in range(parts):
        fetches[i].wait()

        def add(s, _):
            at = i * step + 2 * s
            even, odd = asked(home_ref, at), asked(home_ref, at + 1)
            even_ref[even] += returned_ref[at].astype(F32)
            odd_ref[odd] += returned_ref[at + 1].astype(F32)
            return 0

        lax.fori_loop(0, step // 2, add, 0, unroll=True)
    wait_all(loads)
    for i in range(NB):
        proj_ref[HD : 3 * HD, rows_at(i)] = (near_ref[i] + (even_ref[i] + odd_ref[i])).astype(BF16)
    odd_place = lax.rem(col_ref[0], 2)
    far_pieces, near_pieces = [], []
    for j in range(NB // 2):
        at = ORDER.index((NB - 2 * j) % NB)
        near_pieces.append(proj_ref.at[:, pl.ds(at * BLK, BLK)])
        next_at, last_at = ORDER.index((NB - 1 - 2 * j) % NB), ORDER.index((NB + 1 - 2 * j) % NB)
        at = jnp.where(odd_place == 1, last_at, next_at)
        far_pieces.append(proj_ref.at[:, pl.ds(pl.multiple_of(at * BLK, BLK), BLK)])
    stores = copies(
        [part_ref, *far_pieces, *near_pieces],
        [part_out, *(out.at[1] for out in pair_outs), *(out.at[0] for out in pair_outs)],
        out_sems,
    )
    start_all(stores[1:])
    hidden = hidden_ref[...].reshape(ROWS, D)
    part_ref[HD : 3 * HD, :] = dot(proj_ref[HD : 3 * HD, :], hidden).astype(BF16)
    stores[0].start()
    wait_all(stores)


def sum_body(share_ref, total_ref):
    total = jnp.sum(share_ref[...].astype(F32), axis=0).astype(BF16)
    total_ref[...] = jnp.broadcast_to(total[None], total_ref.shape)


def scale_body(inv_root, total_ref, qkv_ref, out_ref):
    total = total_ref[...].astype(F32) * inv_root
    qkv_ref[...] = total[: 3 * HD]
    out_ref[...] = total[3 * HD :]


def finish_body(col_ref, *refs):
    half = NB // 2
    pair_ins, beside_in, weight_ins, refs = refs[:half], refs[half], refs[half + 1 : half + 1 + NB], refs[half + 1 + NB :]
    state_in, grad_in, gain_in, layer_out, back_out, *refs = refs
    piece_ref, weight_ref, state_ref, grad_ref, gain_ref, layer_ref, back_ref, *refs = refs
    piece_sems, weight_sems, in_sems, out_sems = refs
    pieces = copies(
        [*(pair.at[0] for pair in pair_ins), beside_in],
        [*(piece_ref.at[0, j] for j in range(half)), piece_ref.at[1]],
        piece_sems,
    )
    weights = copies(weight_ins, [weight_ref.at[k] for k in range(NB)], weight_sems)
    loads = copies([state_in, grad_in, gain_in], [state_ref, grad_ref, gain_ref], in_sems)
    start_all(pieces)
    start_all(weights)
    start_all(loads)
    wait_all(pieces)
    wait_all(weights)
    odd_place = lax.rem(col_ref[0], 2)
    out = jnp.zeros((BLK, D), F32)
    back = jnp.zeros((BLK, D), F32)
    for j in range(half):
        beside = jnp.where(odd_place == 1, (2 * j + 1) % NB, (2 * j + NB - 1) % NB)
        for own, head in ((0, 2 * j), (1, beside)):
            terms = piece_ref[own, j].astype(F32).T.astype(BF16)
            back += dot(terms[:, : 3 * HD], weight_ref[head, : 3 * HD, :])
            out += dot(terms[:, 3 * HD :], weight_ref[head, 3 * HD :, :])
    wait_all(loads)
    state = state_ref[...].astype(F32)
    gain = gain_ref[...]
    layer_ref[...] = (state + out).astype(BF16)
    stores = copies([layer_ref, back_ref], [layer_out, back_out], out_sems)
    stores[0].start()
    inv = lax.rsqrt(jnp.mean(state * state, axis=1, keepdims=True) + EPS)
    stat = jnp.sum(gain * back * state, axis=1, keepdims=True)
    back_ref[...] = (
        grad_ref[...].astype(F32) + inv * gain * back - state * (inv * inv * inv * stat / D)
    ).astype(BF16)
    stores[1].start()
    wait_all(stores)


def shards(
    node_states,
    norm_gain,
    qkv_weight,
    out_weight,
    local_slots,
    local_live,
    far_owner,
    far_slot,
    out_grad,
):
    doms = lax.axis_size("dom")
    me = lax.axis_index("dom")
    col_index = lax.axis_index("col").astype(jnp.int32)
    col = col_index.reshape(1)
    slots = doms * CAP
    entries = NB * DEG
    gain = norm_gain[None]

    where = jnp.stack([me.astype(jnp.int32), col_index])
    names = shaped(*far_owner.shape[::-1], kind=jnp.int32)
    places, home, count = call(
        tables_body,
        (names, shaped(CAP, far_owner.shape[0], kind=jnp.int32), shaped(NB, ROWS, kind=F32)),
        [scalars()] + [whole()] * 4,
        out_specs=[whole()] * 3,
        name="tables",
    )(where, far_owner.T, far_slot.T, local_slots, local_live)

    unit = 2 * ROWS * ROWS * BLK
    node = shaped(BLK, D)
    across = shaped(HD, ROWS)
    block, blocks, blocks_float = shaped(BLK, BLK), shaped(NB, BLK, BLK), shaped(NB, BLK, BLK, kind=F32)
    blocks_most = shaped(NB - 1, BLK, BLK)
    wide, wide_float = shaped(NB, BLK, DEG * BLK), shaped(NB, BLK, DEG * BLK, kind=F32)
    exchanged = shaped(slots, BLK, BLK)
    row = shaped(1, D, kind=F32)
    counts = shaped(NB, ROWS, kind=F32)
    states, states_most = shaped(NB, BLK, D), shaped(NB - 1, BLK, D)
    head_weight, out_piece = shaped(3 * HD, D), shaped(HD, D)

    x1, x7 = ring_round(node_states, node_states)
    x1, x7, home, places, count = lax.optimization_barrier((x1, x7, home, places, count))
    x2, x6 = ring_round(x1, x7)
    x3, x5 = ring_round(x2, x6)
    x4 = shifted(x3, 1)
    state_chunks = (node_states, x1, x7, x2, x6, x3, x5, x4)
    projected = call(
        project_most_body,
        (blocks, blocks, exchanged),
        [scalars()] + [left()] * (NB + 1),
        scratch=[
            *held(states_most, row, head_weight, shaped((NB - 1) * BLK, D), blocks_most, blocks_most, exchanged),
            dma_sems(NB + 1),
            dma_sems(2),
            dma_sems(4),
        ],
        flops=2 * ROWS * D * 256,
        name="project_most",
    )(home, node_states, x1, x7, x2, x6, x3, x5, gain, qkv_weight)
    query, kv, outgoing = call(
        project_last_body,
        (blocks, blocks, exchanged),
        [scalars()] + [left()] * 6,
        scratch=[
            *held(node, row, head_weight, block, block),
            dma_sems(3),
            dma_sems(2),
            dma_sems(slots),
        ],
        flops=2 * BLK * D * 256,
        name="project_last",
        aliases={4: 0, 5: 1, 6: 2},
    )(home, x4, gain, qkv_weight, *projected)

    outgoing, grad_own = lax.optimization_barrier((outgoing, out_grad))
    fetched = lax.all_to_all(outgoing, "dom", 0, 0, tiled=True)
    g1, g7 = ring_round(grad_own, grad_own)
    g2, g6 = ring_round(g1, g7)
    g3, g5 = ring_round(g2, g6)
    g4 = shifted(g3, 1)
    grad_chunks = (out_grad, g1, g7, g2, g6, g3, g5, g4)

    (attn_grad,) = call(
        attn_grad_body,
        (blocks_float,),
        [left()] * NB,
        scratch=[
            *held(states_most, out_piece, shaped(NB - 1, BLK, BLK, kind=F32)),
            dma_sems(NB),
            dma_sems(1),
        ],
        flops=2 * ROWS * D * BLK,
        name="attn_grad",
    )(*grad_chunks[:-1], out_weight)

    (near,) = call(
        near_forward_body,
        (blocks_float,),
        [scalars()] + [left()] * 3,
        scratch=[*held(blocks, blocks, counts, blocks_float, shaped(ROWS, BLK)), dma_sems(3), dma_sems(NB)],
        flops=2 * unit,
        name="near_forward",
    )(col, query, kv, count)

    (attn_grad,) = call(
        attn_grad_last_body,
        (blocks_float,),
        [left()] * 3,
        scratch=[*held(node, out_piece, shaped(BLK, BLK, kind=F32)), dma_sems(2), dma_sems(1)],
        flops=2 * BLK * D * BLK,
        name="attn_grad_last",
        aliases={2: 0},
    )(g4, out_weight, attn_grad)

    attn, scaled, extra, outgoing_back = call(
        far_body,
        (across, blocks, blocks_float, exchanged),
        [scalars()] * 2 + [left()] * 4,
        scratch=[
            *held(blocks, exchanged, blocks_float, blocks_float),
            *held(across, blocks, blocks_float, wide_float, wide, wide_float, blocks_float),
            *held(blocks, shaped(entries, BLK, BLK)),
            dma_sems(4),
            dma_sems(3),
            dma_sems(2),
            dma_sems(NB),
            dma_sems(entries),
        ],
        flops=2 * unit,
        name="far_both",
    )(where, places, query, fetched, near, attn_grad)

    outgoing_back, weights_own = lax.optimization_barrier(
        (outgoing_back, jnp.concatenate([qkv_weight, out_weight], axis=0))
    )
    returned = lax.all_to_all(outgoing_back, "dom", 0, 0, tiled=True)
    w1, w7 = ring_round(weights_own, weights_own)
    w2, w6 = ring_round(w1, w7)

    query_grad, near_grad, early, hidden = call(
        near_backward_body,
        (across, blocks_float, shaped(2 * HD, D), states),
        [scalars()] + [left()] * (2 * NB + 7),
        scratch=[
            *held(states, states, row, blocks, blocks, counts, blocks, blocks_float, across, states),
            *held(across, blocks_float, shaped(2 * HD, D), shaped(BLK, ROWS, kind=F32)),
            dma_sems(5),
            dma_sems(2 * NB + 2),
            dma_sems(4),
        ],
        flops=5 * unit,
        name="near_backward",
    )(col, *grad_chunks, *state_chunks, gain, query, kv, count, scaled, extra, attn)

    w2, w6, near_grad = lax.optimization_barrier((w2, w6, near_grad))
    w3, w5 = ring_round(w2, w6)
    returned, w3, w5 = lax.optimization_barrier((returned, w3, w5))
    w4 = shifted(w3, 1)

    half = NB // 2
    *pairs, part = call(
        gather_grads_body,
        (*(shaped(2, 4 * HD, BLK),) * half, shaped(4 * HD, D)),
        [scalars()] * 2 + [left()] * 6,
        scratch=[
            *held(exchanged, blocks_float, shaped(NB + 1, BLK, BLK, kind=F32)),
            *held(shaped(NB + 1, BLK, BLK, kind=F32), shaped(4 * HD, ROWS), states, shaped(4 * HD, D)),
            dma_sems(4),
            dma_sems(6),
            dma_sems(1 + NB),
        ],
        flops=2 * ROWS * D * 128,
        name="gather_grads",
    )(col, home, returned, near_grad, query_grad, attn, hidden, early)

    share_rows = 4 * HD // doms
    shares = lax.all_to_all(part.reshape(doms, share_rows, D), "dom", 0, 0, tiled=True)
    pairs = [pairs[0], *(shifted(pairs[j], 2 * j) for j in range(1, half))]
    beside = paired(jnp.stack([pair[1] for pair in pairs]))
    (totals,) = call(
        sum_body,
        (shaped(doms, share_rows, D),),
        [whole()],
        out_specs=[whole()],
        name="sum_shares",
        limit=4,
    )(shares)
    total = lax.all_to_all(totals, "dom", 0, 0, tiled=True).reshape(4 * HD, D)
    weights = (weights_own, w1, w2, w3, w4, w5, w6, w7)
    layer_out, state_grad = call(
        finish_body,
        (node, node),
        [scalars()] + [left()] * (half + 1 + NB + 3),
        scratch=[
            *held(shaped(2, half, 4 * HD, BLK), shaped(NB, 4 * HD, D), node, node, row, node, node),
            dma_sems(half + 1),
            dma_sems(NB),
            dma_sems(3),
            dma_sems(2),
        ],
        flops=2 * BLK * D * 2048,
        name="finish",
    )(col, *pairs, beside, *weights, node_states, out_grad, gain)
    total, layer_out, state_grad = lax.optimization_barrier((total, layer_out, state_grad))
    qkv_grad, out_weight_grad = call(
        functools.partial(scale_body, 1.0 / math.sqrt(far_owner.shape[0] * BLK)),
        (shaped(3 * HD, D, kind=F32), shaped(HD, D, kind=F32)),
        [whole()],
        out_specs=[whole()] * 2,
        name="scale",
        limit=4,
    )(total)

    return (layer_out, state_grad, qkv_grad, out_weight_grad)


def solution(mesh):
    placed = (
        P(("dom", "col"), None),
        P(),
        P("col", None),
        P("col", None),
        P("dom", None),
        P("dom", None),
        P(),
        P(),
        P(("dom", "col"), None),
    )
    return jax.shard_map(
        shards,
        mesh=mesh,
        in_specs=placed,
        out_specs=(
            P(("dom", "col"), None),
            P(("dom", "col"), None),
            P("col", None),
            P("col", None),
        ),
        check_vma=False,
    )
```

```python
import functools
import math

import jax
import jax.numpy as jnp
from jax import lax
from jax.experimental import pallas as pl
from jax.experimental.pallas import tpu as pltpu
from jax.sharding import PartitionSpec as P

D = 512
HD = 64
BLK = 128
NB = 8
DEG = 4
CAP = 2
ROWS = NB * BLK
EPS = 1e-06
SCALE = 1.0 / math.sqrt(HD)

F32 = jnp.float32
BF16 = jnp.bfloat16
MIB = 1024 * 1024
LIMIT = 64
ORDER = (0, 1, 7, 2, 6, 3, 5, 4)

NT = (((1,), (1,)), ((), ()))
TN = (((0,), (0,)), ((), ()))


def dot(a, b):
    return jnp.dot(a, b, preferred_element_type=F32)


def dot_nt(a, b):
    return lax.dot_general(a, b, NT, preferred_element_type=F32)


def whole():
    return pl.BlockSpec(memory_space=pltpu.VMEM)


def scalars():
    return pl.BlockSpec(memory_space=pltpu.SMEM)


def left():
    return pl.BlockSpec(memory_space=pl.ANY)


def shaped(*dims, kind=BF16):
    return jax.ShapeDtypeStruct(dims, kind)


def call(body, outs, ins, scratch=(), flops=0, name=None, out_specs=None, limit=LIMIT, aliases=None):
    return pl.pallas_call(
        body,
        out_shape=outs,
        in_specs=ins,
        out_specs=out_specs or [left() for _ in outs],
        scratch_shapes=list(scratch),
        input_output_aliases=aliases or {},
        compiler_params=pltpu.CompilerParams(vmem_limit_bytes=limit * MIB),
        cost_estimate=pl.CostEstimate(flops=flops, bytes_accessed=1 << 20, transcendentals=0),
        name=name,
    )


def held(*shapes):
    return [pltpu.VMEM(s.shape, s.dtype) for s in shapes]


def dma_sems(n):
    return pltpu.SemaphoreType.DMA((n,))


def copies(sources, targets, sems):
    return [
        pltpu.make_async_copy(a, b, sems.at[i]) for i, (a, b) in enumerate(zip(sources, targets, strict=True))
    ]


def start_all(jobs):
    for job in jobs:
        job.start()


def wait_all(jobs):
    for job in jobs:
        job.wait()


def lanes_low(shape):
    return lax.broadcasted_iota(jnp.int32, shape, len(shape) - 1) < HD


def rows_at(i):
    return slice(i * BLK, (i + 1) * BLK)


def shifted(x, k):
    return lax.ppermute(x, "col", [(i, (i + k) % NB) for i in range(NB)])


def ring_round(behind, ahead):
    return shifted(behind, 1), shifted(ahead, -1)


def paired(x):
    return lax.ppermute(x, "col", [(i, i ^ 1) for i in range(NB)])


def block_at(col, i):
    return lax.rem(col + NB - ORDER[i], NB)


def tables_body(where_ref, owner_ref, slot_ref, near_ref, live_ref, place_ref, home_ref, count_ref):
    me, col = where_ref[0], where_ref[1]
    owner = owner_ref[...]
    lane = lax.broadcasted_iota(jnp.int32, owner.shape, 1)
    row = lax.rem(lane, NB)
    rank = jnp.zeros_like(owner)
    for d in range(1, NB):
        earlier = pltpu.roll(owner, d, 1)
        for j in range(DEG):
            same = (owner == earlier[j : j + 1, :]) & (row >= d)
            rank += same.astype(jnp.int32)
    place_ref[...] = owner * CAP + rank
    wanted = jnp.zeros_like(owner)
    for i in range(NB):
        wanted += jnp.where(slot_ref[...] == block_at(col, i), i, 0)
    for c in range(CAP):
        asked = jnp.where((owner == me) & (rank == c), wanted, NB)
        least = asked[0:1, :]
        for j in range(1, DEG):
            least = jnp.minimum(least, asked[j : j + 1, :])
        for d in (1, 2, 4):
            least = jnp.minimum(least, pltpu.roll(least, d, 1))
        home_ref[c : c + 1, :] = least
    near, live = near_ref[...], live_ref[...]
    own = lax.broadcasted_iota(jnp.int32, (NB, 1), 0)
    for i in range(NB):
        block = block_at(col, i)
        hits = ((near == block) & (live != 0)).astype(F32)
        count = jnp.sum(hits, axis=1, keepdims=True) + (own == block).astype(F32)
        count_ref[:, rows_at(i)] = jnp.broadcast_to(count, (NB, BLK))


def asked(home_ref, s):
    return home_ref[s % CAP, (s // CAP) * NB + NB - 1]


def normed(x_low, gain):
    x = x_low.astype(F32)
    inv = lax.rsqrt(jnp.mean(x * x, axis=1, keepdims=True) + EPS)
    return (x * inv * gain).astype(BF16)


def project(x_low, gain, wide):
    proj = dot_nt(normed(x_low, gain), wide).astype(BF16)
    return proj[:, :BLK] * jnp.asarray(SCALE, BF16), proj[:, BLK:]


def wide_weight(weight):
    return jnp.concatenate([weight[:HD], jnp.zeros((HD, D), BF16), weight[HD:]], axis=0)


def project_most_body(send_ref, *refs):
    chunk_ins, refs = refs[: NB - 1], refs[NB - 1 :]
    gain_in, weight_in, query_out, kv_out, sent_out, *refs = refs
    chunk_ref, gain_ref, weight_ref, hidden_ref, query_ref, kv_ref, sent_ref, *refs = refs
    in_sems, out_sems, sent_sems = refs
    loads = copies(
        [weight_in, gain_in, *chunk_ins],
        [weight_ref, gain_ref, *(chunk_ref.at[i] for i in range(NB - 1))],
        in_sems,
    )
    start_all(loads)
    wait_all(loads[:2])
    gain = gain_ref[...]
    wide = wide_weight(weight_ref[...])
    for i in range(NB - 1):
        loads[2 + i].wait()
        hidden_ref[rows_at(i), :] = normed(chunk_ref[i], gain)
    proj = dot_nt(hidden_ref[...], wide).astype(BF16)
    for i in range(NB - 1):
        query_ref[i] = proj[rows_at(i), :BLK] * jnp.asarray(SCALE, BF16)
        kv_ref[i] = proj[rows_at(i), BLK:]
    most = pl.ds(0, NB - 1)
    parts = sent_sems.shape[0]
    step = sent_ref.shape[0] // parts
    sends = copies(
        [sent_ref.at[pl.ds(i * step, step)] for i in range(parts)],
        [sent_out.at[pl.ds(i * step, step)] for i in range(parts)],
        sent_sems,
    )
    stores = copies([query_ref, kv_ref], [query_out.at[most], kv_out.at[most]], out_sems)
    start_all(stores)
    for i in range(parts):

        def fill(s, _):
            sent_ref[i * step + s] = kv_ref[jnp.minimum(asked(send_ref, i * step + s), NB - 2)]
            return 0

        lax.fori_loop(0, step, fill, 0, unroll=True)
        sends[i].start()
    wait_all(stores)
    wait_all(sends)


def project_last_body(send_ref, chunk_in, gain_in, weight_in, query_in, kv_in, sent_in, *refs):
    query_out, kv_out, sent_out, *refs = refs
    chunk_ref, gain_ref, weight_ref, query_ref, kv_ref, in_sems, out_sems, sent_sems = refs
    loads = copies([chunk_in, gain_in, weight_in], [chunk_ref, gain_ref, weight_ref], in_sems)
    start_all(loads)
    wait_all(loads)
    query_ref[...], kv_ref[...] = project(chunk_ref[...], gain_ref[...], wide_weight(weight_ref[...]))

    def over_slots(act):
        for slot in range(sent_sems.shape[0]):

            @pl.when(asked(send_ref, slot) == NB - 1)
            def _():
                act(pltpu.make_async_copy(kv_ref, sent_out.at[slot], sent_sems.at[slot]))

    over_slots(lambda job: job.start())
    stores = copies([query_ref, kv_ref], [query_out.at[NB - 1], kv_out.at[NB - 1]], out_sems)
    start_all(stores)
    over_slots(lambda job: job.wait())
    wait_all(stores)


def attn_grad_body(*refs):
    n = NB - 1
    chunk_ins, refs = refs[:n], refs[n:]
    weight_in, ag_out, chunk_ref, weight_ref, ag_ref, sems, out_sems = refs
    loads = copies([weight_in, *chunk_ins], [weight_ref, *(chunk_ref.at[i] for i in range(n))], sems)
    start_all(loads)
    wait_all(loads)
    wide = jnp.concatenate([jnp.zeros((HD, D), BF16), weight_ref[...]], axis=0)
    ag_ref[...] = dot_nt(chunk_ref[...].reshape(n * BLK, D), wide).reshape(n, BLK, BLK)
    store = pltpu.make_async_copy(ag_ref, ag_out.at[pl.ds(0, n)], out_sems.at[0])
    store.start()
    store.wait()


def attn_grad_last_body(chunk_in, weight_in, ag_in, ag_out, chunk_ref, weight_ref, ag_ref, sems, out_sems):
    loads = copies([chunk_in, weight_in], [chunk_ref, weight_ref], sems)
    start_all(loads)
    wait_all(loads)
    wide = jnp.concatenate([jnp.zeros((HD, D), BF16), weight_ref[...]], axis=0)
    ag_ref[...] = dot_nt(chunk_ref[...], wide)
    store = pltpu.make_async_copy(ag_ref, ag_out.at[NB - 1], out_sems.at[0])
    store.start()
    store.wait()


def near_forward_body(col_ref, query_in, kv_in, count_in, num_out, *refs):
    query_ref, kv_ref, count_ref, num_ref, ones_ref, in_sems, out_sems = refs
    loads = copies([kv_in, query_in, count_in], [kv_ref, query_ref, count_ref], in_sems)
    start_all(loads)
    wait_all(loads)
    kv = kv_ref[...].reshape(ROWS, BLK)
    ones_ref[...] = jnp.where(lanes_low(kv.shape), jnp.asarray(1, BF16), kv)
    stores = copies([num_ref.at[i] for i in range(NB)], [num_out.at[i] for i in range(NB)], out_sems)
    for i in range(NB):
        score = dot_nt(query_ref[i], kv_ref[...].reshape(ROWS, BLK))
        prob = jnp.exp(score) * count_ref[pl.ds(block_at(col_ref[0], i), 1), :]
        num_ref[i] = dot(prob.astype(BF16), ones_ref[...])
        stores[i].start()
    wait_all(stores)


def far_body(where_ref, place_ref, query_in, far_in, num_in, ag_in, *refs):
    attn_out, scaled_out, extra_out, back_out, *refs = refs
    query_ref, far_ref, num_ref, ag_ref, *refs = refs
    attn_ref, scaled_ref, extra_ref, prob_ref, prob_low_ref, diff_ref, den_ref, both_ref, stage_ref, *refs = refs
    far_sems, in_sems, out_sems, extra_sems, back_sems = refs
    me, col = where_ref[0], where_ref[1]
    places = [place_ref[j, me * NB + block_at(col, i)] for i in range(NB) for j in range(DEG)]
    parts = far_sems.shape[0]
    step = far_in.shape[0] // parts
    fetches = copies(
        [far_in.at[pl.ds(i * step, step)] for i in range(parts)],
        [far_ref.at[pl.ds(i * step, step)] for i in range(parts)],
        far_sems,
    )
    loads = copies([query_in, ag_in, num_in], [query_ref, ag_ref, num_ref], in_sems)
    loads[0].start()
    start_all(fetches)
    start_all(loads[1:])

    def keys(i):
        return jnp.concatenate([far_ref[places[i * DEG + j]] for j in range(DEG)], axis=0)

    wait_all(loads[:1])
    wait_all(fetches)
    wait_all(loads[1:2])
    for i in range(NB):
        kv = keys(i)
        both = jnp.concatenate([query_ref[i], ag_ref[i].astype(BF16)], axis=0)
        score = dot_nt(both, kv)
        prob = jnp.exp(score[:BLK])
        prob_ref[i] = prob
        diff_ref[i] = score[BLK:]
        prob_low = prob.astype(BF16)
        prob_low_ref[i] = prob_low
        values = jnp.where(lanes_low(kv.shape), jnp.asarray(1, BF16), kv)
        extra_ref[i] = dot(prob_low, values)
    loads[2].wait()
    stores = copies([attn_ref, scaled_ref], [attn_out, scaled_out], out_sems)
    for i in range(NB):
        num = num_ref[i] + extra_ref[i]
        den = jnp.where(lanes_low(num.shape), num, pltpu.roll(num, HD, 1))
        inv = 1.0 / den
        attn = num * inv
        grad = ag_ref[i]
        scaled = (grad * inv).astype(BF16)
        scaled_ref[i] = scaled
        den_ref[i] = inv
        extra_ref[i] = jnp.sum(grad * attn, axis=1, keepdims=True) * inv
        attn_ref[:, rows_at(i)] = attn.T[HD:].astype(BF16)
        both_ref[i] = (query_ref[i] + scaled).astype(F32).T.astype(BF16)
    start_all(stores)
    jobs = []
    for i in range(NB):
        kv = keys(i)
        corr = extra_ref[i]
        diff = diff_ref[i] * den_ref[i, :, :1] - corr[:, :1]
        score_grad = (prob_ref[i] * diff).astype(BF16)
        extra_ref[i] = jnp.where(lanes_low(corr.shape), dot(score_grad, kv), corr)
        key_grad = dot(both_ref[i, :HD], score_grad).astype(BF16)
        value_grad = dot(both_ref[i, HD:], prob_low_ref[i]).astype(BF16)
        for j in range(DEG):
            e = i * DEG + j
            stage_ref[e, :HD, :] = key_grad[:, rows_at(j)]
            stage_ref[e, HD:, :] = value_grad[:, rows_at(j)]
            jobs.append(pltpu.make_async_copy(stage_ref.at[e], back_out.at[places[e]], back_sems.at[e]))
            jobs[-1].start()
        jobs.append(pltpu.make_async_copy(extra_ref.at[i], extra_out.at[i], extra_sems.at[i]))
        jobs[-1].start()
    wait_all(stores)
    wait_all(jobs)


def near_backward_body(col_ref, *refs):
    grad_ins, state_ins, refs = refs[:NB], refs[NB : 2 * NB], refs[2 * NB :]
    gain_in, query_in, kv_in, count_in, scaled_in, extra_in, attn_in, *refs = refs
    query_grad_out, near_out, part_out, hidden_out, *refs = refs
    grad_ref, state_ref, gain_ref, query_ref, kv_ref, count_ref, scaled_ref, extra_ref, attn_ref, hidden_ref, *refs = refs
    query_grad_ref, near_ref, part_ref, acc_ref, in_sems, late_sems, out_sems = refs
    loads = copies(
        [kv_in, query_in, count_in, scaled_in, extra_in],
        [kv_ref, query_ref, count_ref, scaled_ref, extra_ref],
        in_sems,
    )
    late = copies(
        [gain_in, *state_ins, attn_in, *grad_ins],
        [
            gain_ref,
            *(state_ref.at[i] for i in range(NB)),
            attn_ref,
            *(grad_ref.at[i] for i in range(NB)),
        ],
        late_sems,
    )
    start_all(loads)
    start_all(late)
    wait_all(loads)
    acc_ref[...] = jnp.zeros_like(acc_ref)
    col = col_ref[0]
    for i in range(NB):
        query, scaled, extra = query_ref[i], scaled_ref[i], extra_ref[i]
        kv = kv_ref[...].reshape(ROWS, BLK)
        prob = jnp.exp(dot_nt(query, kv)) * count_ref[pl.ds(block_at(col, i), 1), :]
        diff = dot_nt(scaled, kv) - extra[:, HD : HD + 1]
        score_grad = (prob * diff).astype(BF16)
        query_grad = dot(score_grad, kv) + extra
        query_grad_ref[:, rows_at(i)] = (query_grad.T[:HD] * SCALE).astype(BF16)
        both = (query + scaled).astype(F32).T.astype(BF16)
        acc_ref[:HD, :] += dot(both[:HD], score_grad)
        acc_ref[HD:, :] += dot(both[HD:], prob.astype(BF16))
    for i in range(NB):
        near_ref[i] = acc_ref[:, rows_at(i)]
    stores = copies(
        [query_grad_ref, near_ref, hidden_ref, part_ref],
        [query_grad_out, near_out, hidden_out, part_out],
        out_sems,
    )
    start_all(stores[:2])
    wait_all(late)
    gain = gain_ref[...]
    for i in range(NB):
        hidden_ref[i] = normed(state_ref[i], gain)
    stores[2].start()
    part_ref[:HD, :] = dot(query_grad_ref[...], hidden_ref[...].reshape(ROWS, D)).astype(BF16)
    part_ref[HD:, :] = dot(attn_ref[...], grad_ref[...].reshape(ROWS, D)).astype(BF16)
    stores[3].start()
    wait_all(stores)


def gather_grads_body(col_ref, home_ref, returned_in, near_in, query_grad_in, attn_in, hidden_in, early_in, *refs):
    *pair_outs, part_out = refs[: 1 + NB // 2]
    refs = refs[1 + NB // 2 :]
    returned_ref, near_ref, even_ref, odd_ref, proj_ref, hidden_ref, part_ref, *refs = refs
    far_sems, in_sems, out_sems = refs
    parts = far_sems.shape[0]
    step = returned_in.shape[0] // parts
    fetches = copies(
        [returned_in.at[pl.ds(i * step, step)] for i in range(parts)],
        [returned_ref.at[pl.ds(i * step, step)] for i in range(parts)],
        far_sems,
    )
    loads = copies(
        [
            near_in,
            hidden_in,
            query_grad_in,
            attn_in,
            early_in.at[pl.ds(0, HD)],
            early_in.at[pl.ds(HD, HD)],
        ],
        [
            near_ref,
            hidden_ref,
            proj_ref.at[pl.ds(0, HD)],
            proj_ref.at[pl.ds(3 * HD, HD)],
            part_ref.at[pl.ds(0, HD)],
            part_ref.at[pl.ds(3 * HD, HD)],
        ],
        in_sems,
    )
    start_all(fetches)
    start_all(loads)
    even_ref[...] = jnp.zeros_like(even_ref)
    odd_ref[...] = jnp.zeros_like(odd_ref)
    for i in range(parts):
        fetches[i].wait()

        def add(s, _):
            at = i * step + 2 * s
            even, odd = asked(home_ref, at), asked(home_ref, at + 1)
            even_ref[even] += returned_ref[at].astype(F32)
            odd_ref[odd] += returned_ref[at + 1].astype(F32)
            return 0

        lax.fori_loop(0, step // 2, add, 0, unroll=True)
    wait_all(loads)
    for i in range(NB):
        proj_ref[HD : 3 * HD, rows_at(i)] = (near_ref[i] + (even_ref[i] + odd_ref[i])).astype(BF16)
    odd_place = lax.rem(col_ref[0], 2)
    far_pieces, near_pieces = [], []
    for j in range(NB // 2):
        at = ORDER.index((NB - 2 * j) % NB)
        near_pieces.append(proj_ref.at[:, pl.ds(at * BLK, BLK)])
        next_at, last_at = ORDER.index((NB - 1 - 2 * j) % NB), ORDER.index((NB + 1 - 2 * j) % NB)
        at = jnp.where(odd_place == 1, last_at, next_at)
        far_pieces.append(proj_ref.at[:, pl.ds(pl.multiple_of(at * BLK, BLK), BLK)])
    stores = copies(
        [part_ref, *far_pieces, *near_pieces],
        [part_out, *(out.at[1] for out in pair_outs), *(out.at[0] for out in pair_outs)],
        out_sems,
    )
    start_all(stores[1:])
    hidden = hidden_ref[...].reshape(ROWS, D)
    part_ref[HD : 3 * HD, :] = dot(proj_ref[HD : 3 * HD, :], hidden).astype(BF16)
    stores[0].start()
    wait_all(stores)


def pack_body(*refs):
    *pair_ins, _, pack_out, pack_ref, in_sems, out_sems = refs
    loads = copies([pair.at[1] for pair in pair_ins], [pack_ref.at[j] for j in range(NB // 2)], in_sems)
    stores = copies(
        [pack_ref.at[j] for j in range(NB // 2)], [pack_out.at[j] for j in range(NB // 2)], out_sems
    )
    start_all(loads)
    for load, store in zip(loads, stores, strict=True):
        load.wait()
        store.start()
    wait_all(stores)


def sum_body(share_ref, total_ref):
    total = jnp.sum(share_ref[...].astype(F32), axis=0).astype(BF16)
    total_ref[...] = jnp.broadcast_to(total[None], total_ref.shape)


def scale_body(inv_root, total_ref, qkv_ref, out_ref):
    total = total_ref[...].astype(F32) * inv_root
    qkv_ref[...] = total[: 3 * HD]
    out_ref[...] = total[3 * HD :]


def head_terms(piece, weight):
    terms = piece.astype(F32).T.astype(BF16)
    return dot(terms[:, 3 * HD :], weight[3 * HD :, :]), dot(terms[:, : 3 * HD], weight[: 3 * HD, :])


def first_heads_body(*refs):
    n = NB // 2 - 1
    pair_ins, weight_ins, refs = refs[:n], refs[n : 2 * n], refs[2 * n :]
    sum_out, piece_ref, weight_ref, sum_ref, piece_sems, weight_sems, out_sems = refs
    pieces = copies([pair.at[0] for pair in pair_ins], [piece_ref.at[j] for j in range(n)], piece_sems)
    weights = copies(weight_ins, [weight_ref.at[j] for j in range(n)], weight_sems)
    start_all(pieces)
    start_all(weights)
    out = jnp.zeros((BLK, D), F32)
    back = jnp.zeros((BLK, D), F32)
    for j in range(n):
        pieces[j].wait()
        weights[j].wait()
        out_term, back_term = head_terms(piece_ref[j], weight_ref[j])
        out += out_term
        back += back_term
    sum_ref[0], sum_ref[1] = out, back
    store = pltpu.make_async_copy(sum_ref, sum_out, out_sems.at[0])
    store.start()
    store.wait()


def finish_body(col_ref, sum_in, pair_in, beside_in, *refs):
    half = NB // 2
    weight_ins, refs = refs[: half + 1], refs[half + 1 :]
    state_in, grad_in, gain_in, layer_out, back_out, *refs = refs
    sum_ref, pair_ref, piece_ref, weight_ref, state_ref, grad_ref, gain_ref, layer_ref, back_ref, *refs = refs
    piece_sems, weight_sems, in_sems, out_sems = refs
    pieces = copies([pair_in.at[0], beside_in], [pair_ref, piece_ref], piece_sems)
    weights = copies(weight_ins, [weight_ref.at[k] for k in range(half + 1)], weight_sems)
    loads = copies([sum_in, state_in, grad_in, gain_in], [sum_ref, state_ref, grad_ref, gain_ref], in_sems)
    start_all(pieces)
    start_all(weights)
    start_all(loads)
    wait_all(pieces)
    wait_all(weights)
    odd_place = lax.rem(col_ref[0], 2)
    out, back = head_terms(pair_ref[...], weight_ref[half])
    for j in range(half):
        beside = jnp.where(odd_place == 1, j, (j + half - 1) % half)
        out_term, back_term = head_terms(piece_ref[j], weight_ref[beside])
        out += out_term
        back += back_term
    wait_all(loads)
    out += sum_ref[0]
    back += sum_ref[1]
    state = state_ref[...].astype(F32)
    gain = gain_ref[...]
    layer_ref[...] = (state + out).astype(BF16)
    stores = copies([layer_ref, back_ref], [layer_out, back_out], out_sems)
    stores[0].start()
    inv = lax.rsqrt(jnp.mean(state * state, axis=1, keepdims=True) + EPS)
    stat = jnp.sum(gain * back * state, axis=1, keepdims=True)
    back_ref[...] = (
        grad_ref[...].astype(F32) + inv * gain * back - state * (inv * inv * inv * stat / D)
    ).astype(BF16)
    stores[1].start()
    wait_all(stores)


def shards(
    node_states,
    norm_gain,
    qkv_weight,
    out_weight,
    local_slots,
    local_live,
    far_owner,
    far_slot,
    out_grad,
):
    doms = lax.axis_size("dom")
    me = lax.axis_index("dom")
    col_index = lax.axis_index("col").astype(jnp.int32)
    col = col_index.reshape(1)
    slots = doms * CAP
    entries = NB * DEG
    gain = norm_gain[None]

    where = jnp.stack([me.astype(jnp.int32), col_index])
    names = shaped(*far_owner.shape[::-1], kind=jnp.int32)
    places, home, count = call(
        tables_body,
        (names, shaped(CAP, far_owner.shape[0], kind=jnp.int32), shaped(NB, ROWS, kind=F32)),
        [scalars()] + [whole()] * 4,
        out_specs=[whole()] * 3,
        name="tables",
    )(where, far_owner.T, far_slot.T, local_slots, local_live)

    unit = 2 * ROWS * ROWS * BLK
    node = shaped(BLK, D)
    across = shaped(HD, ROWS)
    block, blocks, blocks_float = shaped(BLK, BLK), shaped(NB, BLK, BLK), shaped(NB, BLK, BLK, kind=F32)
    blocks_most = shaped(NB - 1, BLK, BLK)
    wide, wide_float = shaped(NB, BLK, DEG * BLK), shaped(NB, BLK, DEG * BLK, kind=F32)
    exchanged = shaped(slots, BLK, BLK)
    row = shaped(1, D, kind=F32)
    counts = shaped(NB, ROWS, kind=F32)
    states, states_most = shaped(NB, BLK, D), shaped(NB - 1, BLK, D)
    head_weight, out_piece = shaped(3 * HD, D), shaped(HD, D)

    x1, x7 = ring_round(node_states, node_states)
    x1, x7, home, places, count = lax.optimization_barrier((x1, x7, home, places, count))
    x2, x6 = ring_round(x1, x7)
    x3, x5 = ring_round(x2, x6)
    x4 = shifted(x3, 1)
    state_chunks = (node_states, x1, x7, x2, x6, x3, x5, x4)
    projected = call(
        project_most_body,
        (blocks, blocks, exchanged),
        [scalars()] + [left()] * (NB + 1),
        scratch=[
            *held(states_most, row, head_weight, shaped((NB - 1) * BLK, D), blocks_most, blocks_most, exchanged),
            dma_sems(NB + 1),
            dma_sems(2),
            dma_sems(4),
        ],
        flops=2 * ROWS * D * 256,
        name="project_most",
    )(home, node_states, x1, x7, x2, x6, x3, x5, gain, qkv_weight)
    query, kv, outgoing = call(
        project_last_body,
        (blocks, blocks, exchanged),
        [scalars()] + [left()] * 6,
        scratch=[
            *held(node, row, head_weight, block, block),
            dma_sems(3),
            dma_sems(2),
            dma_sems(slots),
        ],
        flops=2 * BLK * D * 256,
        name="project_last",
        aliases={4: 0, 5: 1, 6: 2},
    )(home, x4, gain, qkv_weight, *projected)

    outgoing, grad_own = lax.optimization_barrier((outgoing, out_grad))
    fetched = lax.all_to_all(outgoing, "dom", 0, 0, tiled=True)
    g1, g7 = ring_round(grad_own, grad_own)
    g2, g6 = ring_round(g1, g7)
    g3, g5 = ring_round(g2, g6)
    g4 = shifted(g3, 1)
    grad_chunks = (out_grad, g1, g7, g2, g6, g3, g5, g4)

    (attn_grad,) = call(
        attn_grad_body,
        (blocks_float,),
        [left()] * NB,
        scratch=[
            *held(states_most, out_piece, shaped(NB - 1, BLK, BLK, kind=F32)),
            dma_sems(NB),
            dma_sems(1),
        ],
        flops=2 * ROWS * D * BLK,
        name="attn_grad",
    )(*grad_chunks[:-1], out_weight)

    (near,) = call(
        near_forward_body,
        (blocks_float,),
        [scalars()] + [left()] * 3,
        scratch=[*held(blocks, blocks, counts, blocks_float, shaped(ROWS, BLK)), dma_sems(3), dma_sems(NB)],
        flops=2 * unit,
        name="near_forward",
    )(col, query, kv, count)

    (attn_grad,) = call(
        attn_grad_last_body,
        (blocks_float,),
        [left()] * 3,
        scratch=[*held(node, out_piece, shaped(BLK, BLK, kind=F32)), dma_sems(2), dma_sems(1)],
        flops=2 * BLK * D * BLK,
        name="attn_grad_last",
        aliases={2: 0},
    )(g4, out_weight, attn_grad)

    attn, scaled, extra, outgoing_back = call(
        far_body,
        (across, blocks, blocks_float, exchanged),
        [scalars()] * 2 + [left()] * 4,
        scratch=[
            *held(blocks, exchanged, blocks_float, blocks_float),
            *held(across, blocks, blocks_float, wide_float, wide, wide_float, blocks_float),
            *held(blocks, shaped(entries, BLK, BLK)),
            dma_sems(4),
            dma_sems(3),
            dma_sems(2),
            dma_sems(NB),
            dma_sems(entries),
        ],
        flops=2 * unit,
        name="far_both",
    )(where, places, query, fetched, near, attn_grad)

    outgoing_back, weights_own = lax.optimization_barrier(
        (outgoing_back, jnp.concatenate([qkv_weight, out_weight], axis=0))
    )
    returned = lax.all_to_all(outgoing_back, "dom", 0, 0, tiled=True)
    w1, w7 = ring_round(weights_own, weights_own)
    w2, w6 = ring_round(w1, w7)

    query_grad, near_grad, early, hidden = call(
        near_backward_body,
        (across, blocks_float, shaped(2 * HD, D), states),
        [scalars()] + [left()] * (2 * NB + 7),
        scratch=[
            *held(states, states, row, blocks, blocks, counts, blocks, blocks_float, across, states),
            *held(across, blocks_float, shaped(2 * HD, D), shaped(BLK, ROWS, kind=F32)),
            dma_sems(5),
            dma_sems(2 * NB + 2),
            dma_sems(4),
        ],
        flops=5 * unit,
        name="near_backward",
    )(col, *grad_chunks, *state_chunks, gain, query, kv, count, scaled, extra, attn)

    w2, w6, near_grad = lax.optimization_barrier((w2, w6, near_grad))
    w3, w5 = ring_round(w2, w6)
    returned, w3, w5 = lax.optimization_barrier((returned, w3, w5))
    w4 = shifted(w3, 1)

    half = NB // 2
    *pairs, part = call(
        gather_grads_body,
        (*(shaped(2, 4 * HD, BLK),) * half, shaped(4 * HD, D)),
        [scalars()] * 2 + [left()] * 6,
        scratch=[
            *held(exchanged, blocks_float, shaped(NB + 1, BLK, BLK, kind=F32)),
            *held(shaped(NB + 1, BLK, BLK, kind=F32), shaped(4 * HD, ROWS), states, shaped(4 * HD, D)),
            dma_sems(4),
            dma_sems(6),
            dma_sems(1 + NB),
        ],
        flops=2 * ROWS * D * 128,
        name="gather_grads",
    )(col, home, returned, near_grad, query_grad, attn, hidden, early)

    share_rows = 4 * HD // doms
    shares = lax.all_to_all(part.reshape(doms, share_rows, D), "dom", 0, 0, tiled=True)
    *pairs, w4 = lax.optimization_barrier((*pairs, w4))
    pairs = [pairs[0], *(shifted(pairs[j], 2 * j) for j in range(1, half))]
    (totals,) = call(
        sum_body,
        (shaped(doms, share_rows, D),),
        [whole()],
        out_specs=[whole()],
        name="sum_shares",
        limit=4,
    )(shares)
    total = lax.all_to_all(totals, "dom", 0, 0, tiled=True).reshape(4 * HD, D)
    packed = shaped(half, 4 * HD, BLK)
    (beside,) = call(
        pack_body,
        (packed,),
        [left()] * (half + 1),
        scratch=[*held(packed), dma_sems(half), dma_sems(half)],
        name="pack",
    )(*pairs, totals)
    beside = paired(beside)
    sums, piece, weight = shaped(2, BLK, D, kind=F32), shaped(4 * HD, BLK), shaped(4 * HD, D)
    (first,) = call(
        first_heads_body,
        (sums,),
        [left()] * (2 * half - 2),
        scratch=[
            *held(shaped(half - 1, 4 * HD, BLK), shaped(half - 1, 4 * HD, D), sums),
            dma_sems(half - 1),
            dma_sems(half - 1),
            dma_sems(1),
        ],
        flops=unit // 100,
        name="first_heads",
    )(pairs[0], pairs[1], pairs[3], weights_own, w2, w6)
    layer_out, state_grad = call(
        finish_body,
        (node, node),
        [scalars()] + [left()] * (3 + half + 1 + 3),
        scratch=[
            *held(sums, piece, packed, shaped(half + 1, 4 * HD, D), node, node, row, node, node),
            dma_sems(2),
            dma_sems(half + 1),
            dma_sems(4),
            dma_sems(2),
        ],
        flops=unit // 100,
        name="finish",
    )(col, first, pairs[2], beside, w1, w3, w5, w7, w4, node_states, out_grad, gain)
    qkv_grad, out_weight_grad = call(
        functools.partial(scale_body, 1.0 / math.sqrt(far_owner.shape[0] * BLK)),
        (shaped(3 * HD, D, kind=F32), shaped(HD, D, kind=F32)),
        [whole()],
        out_specs=[whole()] * 2,
        flops=3 * unit,
        name="scale",
        limit=4,
    )(total)

    return (layer_out, state_grad, qkv_grad, out_weight_grad)


def solution(mesh):
    placed = (
        P(("dom", "col"), None),
        P(),
        P("col", None),
        P("col", None),
        P("dom", None),
        P("dom", None),
        P(),
        P(),
        P(("dom", "col"), None),
    )
    return jax.shard_map(
        shards,
        mesh=mesh,
        in_specs=placed,
        out_specs=(
            P(("dom", "col"), None),
            P(("dom", "col"), None),
            P("col", None),
            P("col", None),
        ),
        check_vma=False,
    )
```

```python
import functools
import math

import jax
import jax.numpy as jnp
from jax import lax
from jax.experimental import pallas as pl
from jax.experimental.pallas import tpu as pltpu
from jax.sharding import PartitionSpec as P

D = 512
HD = 64
BLK = 128
NB = 8
DEG = 4
CAP = 2
ROWS = NB * BLK
EPS = 1e-06
SCALE = 1.0 / math.sqrt(HD)

F32 = jnp.float32
BF16 = jnp.bfloat16
MIB = 1024 * 1024
LIMIT = 64
ORDER = (0, 1, 7, 2, 6, 3, 5, 4)

NT = (((1,), (1,)), ((), ()))
TN = (((0,), (0,)), ((), ()))


def dot(a, b):
    return jnp.dot(a, b, preferred_element_type=F32)


def dot_nt(a, b):
    return lax.dot_general(a, b, NT, preferred_element_type=F32)


def whole():
    return pl.BlockSpec(memory_space=pltpu.VMEM)


def scalars():
    return pl.BlockSpec(memory_space=pltpu.SMEM)


def left():
    return pl.BlockSpec(memory_space=pl.ANY)


def shaped(*dims, kind=BF16):
    return jax.ShapeDtypeStruct(dims, kind)


def call(body, outs, ins, scratch=(), flops=0, name=None, out_specs=None, limit=LIMIT, aliases=None):
    return pl.pallas_call(
        body,
        out_shape=outs,
        in_specs=ins,
        out_specs=out_specs or [left() for _ in outs],
        scratch_shapes=list(scratch),
        input_output_aliases=aliases or {},
        compiler_params=pltpu.CompilerParams(vmem_limit_bytes=limit * MIB),
        cost_estimate=pl.CostEstimate(flops=flops, bytes_accessed=1 << 20, transcendentals=0),
        name=name,
    )


def held(*shapes):
    return [pltpu.VMEM(s.shape, s.dtype) for s in shapes]


def dma_sems(n):
    return pltpu.SemaphoreType.DMA((n,))


def copies(sources, targets, sems):
    return [
        pltpu.make_async_copy(a, b, sems.at[i]) for i, (a, b) in enumerate(zip(sources, targets, strict=True))
    ]


def start_all(jobs):
    for job in jobs:
        job.start()


def wait_all(jobs):
    for job in jobs:
        job.wait()


def lanes_low(shape):
    return lax.broadcasted_iota(jnp.int32, shape, len(shape) - 1) < HD


def rows_at(i):
    return slice(i * BLK, (i + 1) * BLK)


def shifted(x, k):
    return lax.ppermute(x, "col", [(i, (i + k) % NB) for i in range(NB)])


def ring_round(behind, ahead):
    return shifted(behind, 1), shifted(ahead, -1)


def paired(x):
    return lax.ppermute(x, "col", [(i, i ^ 1) for i in range(NB)])


def block_at(col, i):
    return lax.rem(col + NB - ORDER[i], NB)


def tables_body(where_ref, owner_ref, slot_ref, near_ref, live_ref, place_ref, home_ref, count_ref):
    me, col = where_ref[0], where_ref[1]
    owner = owner_ref[...]
    lane = lax.broadcasted_iota(jnp.int32, owner.shape, 1)
    row = lax.rem(lane, NB)
    rank = jnp.zeros_like(owner)
    for d in range(1, NB):
        earlier = pltpu.roll(owner, d, 1)
        for j in range(DEG):
            same = (owner == earlier[j : j + 1, :]) & (row >= d)
            rank += same.astype(jnp.int32)
    place_ref[...] = owner * CAP + rank
    wanted = jnp.zeros_like(owner)
    for i in range(NB):
        wanted += jnp.where(slot_ref[...] == block_at(col, i), i, 0)
    for c in range(CAP):
        asked = jnp.where((owner == me) & (rank == c), wanted, NB)
        least = asked[0:1, :]
        for j in range(1, DEG):
            least = jnp.minimum(least, asked[j : j + 1, :])
        for d in (1, 2, 4):
            least = jnp.minimum(least, pltpu.roll(least, d, 1))
        home_ref[c : c + 1, :] = least
    near, live = near_ref[...], live_ref[...]
    own = lax.broadcasted_iota(jnp.int32, (NB, 1), 0)
    for i in range(NB):
        block = block_at(col, i)
        hits = ((near == block) & (live != 0)).astype(F32)
        count = jnp.sum(hits, axis=1, keepdims=True) + (own == block).astype(F32)
        count_ref[:, rows_at(i)] = jnp.broadcast_to(count, (NB, BLK))


def asked(home_ref, s):
    return home_ref[s % CAP, (s // CAP) * NB + NB - 1]


def normed(x_low, gain):
    x = x_low.astype(F32)
    inv = lax.rsqrt(jnp.mean(x * x, axis=1, keepdims=True) + EPS)
    return (x * inv * gain).astype(BF16)


def wide_weight(weight):
    return jnp.concatenate([weight[:HD], jnp.zeros((HD, D), BF16), weight[HD:]], axis=0)


def project_most_body(send_ref, *refs):
    chunk_ins, refs = refs[: NB - 1], refs[NB - 1 :]
    gain_in, weight_in, query_out, kv_out, sent_out, *refs = refs
    chunk_ref, gain_ref, weight_ref, hidden_ref, query_ref, kv_ref, sent_ref, *refs = refs
    in_sems, out_sems, sent_sems = refs
    loads = copies(
        [weight_in, gain_in, *chunk_ins],
        [weight_ref, gain_ref, *(chunk_ref.at[i] for i in range(NB - 1))],
        in_sems,
    )
    start_all(loads)
    wait_all(loads[:2])
    gain = gain_ref[...]
    wide = wide_weight(weight_ref[...])
    for i in range(NB - 1):
        loads[2 + i].wait()
        hidden_ref[rows_at(i), :] = normed(chunk_ref[i], gain)
    proj = dot_nt(hidden_ref[...], wide).astype(BF16)
    for i in range(NB - 1):
        query_ref[i] = proj[rows_at(i), :BLK] * jnp.asarray(SCALE, BF16)
        kv_ref[i] = proj[rows_at(i), BLK:]
    most = pl.ds(0, NB - 1)
    parts = sent_sems.shape[0]
    step = sent_ref.shape[0] // parts
    sends = copies(
        [sent_ref.at[pl.ds(i * step, step)] for i in range(parts)],
        [sent_out.at[pl.ds(i * step, step)] for i in range(parts)],
        sent_sems,
    )
    stores = copies([query_ref, kv_ref], [query_out.at[most], kv_out.at[most]], out_sems)
    start_all(stores)
    for i in range(parts):

        def fill(s, _):
            sent_ref[i * step + s] = kv_ref[jnp.minimum(asked(send_ref, i * step + s), NB - 2)]
            return 0

        lax.fori_loop(0, step, fill, 0, unroll=True)
        sends[i].start()
    wait_all(stores)
    wait_all(sends)


def project_last_body(send_ref, chunk_in, gain_in, weight_in, query_in, kv_in, sent_in, *refs):
    query_out, kv_out, sent_out, *refs = refs
    chunk_ref, gain_ref, weight_ref, query_ref, kv_ref, in_sems, out_sems, sent_sems = refs
    loads = copies([chunk_in, gain_in, weight_in], [chunk_ref, gain_ref, weight_ref], in_sems)
    start_all(loads)
    wait_all(loads)
    hidden = normed(chunk_ref[...], gain_ref[...])
    kv_ref[...] = dot_nt(hidden, weight_ref[HD:, :]).astype(BF16)

    def over_slots(act):
        for slot in range(sent_sems.shape[0]):

            @pl.when(asked(send_ref, slot) == NB - 1)
            def _():
                act(pltpu.make_async_copy(kv_ref, sent_out.at[slot], sent_sems.at[slot]))

    over_slots(lambda job: job.start())
    query = dot_nt(hidden, wide_weight(weight_ref[...])[:BLK]).astype(BF16)
    query_ref[...] = query * jnp.asarray(SCALE, BF16)
    stores = copies([query_ref, kv_ref], [query_out.at[NB - 1], kv_out.at[NB - 1]], out_sems)
    start_all(stores)
    over_slots(lambda job: job.wait())
    wait_all(stores)


def attn_grad_body(*refs):
    n = NB - 1
    chunk_ins, refs = refs[:n], refs[n:]
    weight_in, ag_out, chunk_ref, weight_ref, ag_ref, sems, out_sems = refs
    loads = copies([weight_in, *chunk_ins], [weight_ref, *(chunk_ref.at[i] for i in range(n))], sems)
    start_all(loads)
    wait_all(loads)
    wide = jnp.concatenate([jnp.zeros((HD, D), BF16), weight_ref[...]], axis=0)
    ag_ref[...] = dot_nt(chunk_ref[...].reshape(n * BLK, D), wide).reshape(n, BLK, BLK)
    store = pltpu.make_async_copy(ag_ref, ag_out.at[pl.ds(0, n)], out_sems.at[0])
    store.start()
    store.wait()


def attn_grad_last_body(chunk_in, weight_in, ag_in, ag_out, chunk_ref, weight_ref, ag_ref, sems, out_sems):
    loads = copies([chunk_in, weight_in], [chunk_ref, weight_ref], sems)
    start_all(loads)
    wait_all(loads)
    wide = jnp.concatenate([jnp.zeros((HD, D), BF16), weight_ref[...]], axis=0)
    ag_ref[...] = dot_nt(chunk_ref[...], wide)
    store = pltpu.make_async_copy(ag_ref, ag_out.at[NB - 1], out_sems.at[0])
    store.start()
    store.wait()


def near_forward_body(col_ref, query_in, kv_in, count_in, num_out, *refs):
    query_ref, kv_ref, count_ref, num_ref, ones_ref, in_sems, out_sems = refs
    loads = copies([kv_in, query_in, count_in], [kv_ref, query_ref, count_ref], in_sems)
    start_all(loads)
    wait_all(loads)
    kv = kv_ref[...].reshape(ROWS, BLK)
    ones_ref[...] = jnp.where(lanes_low(kv.shape), jnp.asarray(1, BF16), kv)
    stores = copies([num_ref.at[i] for i in range(NB)], [num_out.at[i] for i in range(NB)], out_sems)
    for i in range(NB):
        score = dot_nt(query_ref[i], kv_ref[...].reshape(ROWS, BLK))
        prob = jnp.exp(score) * count_ref[pl.ds(block_at(col_ref[0], i), 1), :]
        num_ref[i] = dot(prob.astype(BF16), ones_ref[...])
        stores[i].start()
    wait_all(stores)


def far_body(where_ref, place_ref, query_in, far_in, num_in, ag_in, *refs):
    attn_out, scaled_out, extra_out, back_out, *refs = refs
    query_ref, far_ref, num_ref, ag_ref, *refs = refs
    attn_ref, scaled_ref, extra_ref, prob_ref, prob_low_ref, diff_ref, den_ref, both_ref, stage_ref, *refs = refs
    far_sems, in_sems, out_sems, extra_sems, back_sems = refs
    me, col = where_ref[0], where_ref[1]
    places = [place_ref[j, me * NB + block_at(col, i)] for i in range(NB) for j in range(DEG)]
    parts = far_sems.shape[0]
    step = far_in.shape[0] // parts
    fetches = copies(
        [far_in.at[pl.ds(i * step, step)] for i in range(parts)],
        [far_ref.at[pl.ds(i * step, step)] for i in range(parts)],
        far_sems,
    )
    loads = copies([query_in, ag_in, num_in], [query_ref, ag_ref, num_ref], in_sems)
    loads[0].start()
    start_all(fetches)
    start_all(loads[1:])

    def keys(i):
        return jnp.concatenate([far_ref[places[i * DEG + j]] for j in range(DEG)], axis=0)

    wait_all(loads[:1])
    wait_all(fetches)
    wait_all(loads[1:2])
    for i in range(NB):
        kv = keys(i)
        both = jnp.concatenate([query_ref[i], ag_ref[i].astype(BF16)], axis=0)
        score = dot_nt(both, kv)
        prob = jnp.exp(score[:BLK])
        prob_ref[i] = prob
        diff_ref[i] = score[BLK:]
        prob_low = prob.astype(BF16)
        prob_low_ref[i] = prob_low
        values = jnp.where(lanes_low(kv.shape), jnp.asarray(1, BF16), kv)
        extra_ref[i] = dot(prob_low, values)
    loads[2].wait()
    stores = copies([attn_ref, scaled_ref], [attn_out, scaled_out], out_sems)
    for i in range(NB):
        num = num_ref[i] + extra_ref[i]
        den = jnp.where(lanes_low(num.shape), num, pltpu.roll(num, HD, 1))
        inv = 1.0 / den
        attn = num * inv
        grad = ag_ref[i]
        scaled = (grad * inv).astype(BF16)
        scaled_ref[i] = scaled
        den_ref[i] = inv
        extra_ref[i] = jnp.sum(grad * attn, axis=1, keepdims=True) * inv
        attn_ref[:, rows_at(i)] = attn.astype(BF16).T[HD:]
        both_ref[i] = (query_ref[i] + scaled).T
    start_all(stores)
    jobs = []
    for i in range(NB):
        kv = keys(i)
        corr = extra_ref[i]
        diff = diff_ref[i] * den_ref[i, :, :1] - corr[:, :1]
        score_grad = (prob_ref[i] * diff).astype(BF16)
        extra_ref[i] = jnp.where(lanes_low(corr.shape), dot(score_grad, kv), corr)
        key_grad = dot(both_ref[i, :HD], score_grad).astype(BF16)
        value_grad = dot(both_ref[i, HD:], prob_low_ref[i]).astype(BF16)
        for j in range(DEG):
            e = i * DEG + j
            stage_ref[e, :HD, :] = key_grad[:, rows_at(j)]
            stage_ref[e, HD:, :] = value_grad[:, rows_at(j)]
            jobs.append(pltpu.make_async_copy(stage_ref.at[e], back_out.at[places[e]], back_sems.at[e]))
            jobs[-1].start()
        jobs.append(pltpu.make_async_copy(extra_ref.at[i], extra_out.at[i], extra_sems.at[i]))
        jobs[-1].start()
    wait_all(stores)
    wait_all(jobs)


def near_backward_body(col_ref, *refs):
    grad_ins, state_ins, refs = refs[:NB], refs[NB : 2 * NB], refs[2 * NB :]
    gain_in, query_in, kv_in, count_in, scaled_in, extra_in, attn_in, *refs = refs
    query_grad_out, near_out, part_out, hidden_out, *refs = refs
    grad_ref, state_ref, gain_ref, query_ref, kv_ref, count_ref, scaled_ref, extra_ref, attn_ref, hidden_ref, *refs = refs
    query_grad_ref, near_ref, part_ref, acc_ref, in_sems, late_sems, out_sems = refs
    loads = copies(
        [kv_in, query_in, count_in, scaled_in, extra_in],
        [kv_ref, query_ref, count_ref, scaled_ref, extra_ref],
        in_sems,
    )
    late = copies(
        [gain_in, *state_ins, attn_in, *grad_ins],
        [
            gain_ref,
            *(state_ref.at[i] for i in range(NB)),
            attn_ref,
            *(grad_ref.at[i] for i in range(NB)),
        ],
        late_sems,
    )
    start_all(loads)
    start_all(late)
    wait_all(loads)
    acc_ref[...] = jnp.zeros_like(acc_ref)
    col = col_ref[0]
    for i in range(NB):
        query, scaled, extra = query_ref[i], scaled_ref[i], extra_ref[i]
        kv = kv_ref[...].reshape(ROWS, BLK)
        prob = jnp.exp(dot_nt(query, kv)) * count_ref[pl.ds(block_at(col, i), 1), :]
        diff = dot_nt(scaled, kv) - extra[:, HD : HD + 1]
        score_grad = (prob * diff).astype(BF16)
        query_grad = dot(score_grad, kv) + extra
        query_grad_ref[:, rows_at(i)] = (query_grad.T[:HD] * SCALE).astype(BF16)
        both = (query + scaled).astype(F32).T.astype(BF16)
        acc_ref[:HD, :] += dot(both[:HD], score_grad)
        acc_ref[HD:, :] += dot(both[HD:], prob.astype(BF16))
    for i in range(NB):
        near_ref[i] = acc_ref[:, rows_at(i)]
    stores = copies(
        [query_grad_ref, near_ref, hidden_ref, part_ref],
        [query_grad_out, near_out, hidden_out, part_out],
        out_sems,
    )
    start_all(stores[:2])
    wait_all(late)
    gain = gain_ref[...]
    for i in range(NB):
        hidden_ref[i] = normed(state_ref[i], gain)
    stores[2].start()
    part_ref[:HD, :] = dot(query_grad_ref[...], hidden_ref[...].reshape(ROWS, D)).astype(BF16)
    part_ref[HD:, :] = dot(attn_ref[...], grad_ref[...].reshape(ROWS, D)).astype(BF16)
    stores[3].start()
    wait_all(stores)


def gather_grads_body(col_ref, home_ref, returned_in, near_in, query_grad_in, attn_in, hidden_in, early_in, *refs):
    *pair_outs, part_out = refs[: 1 + NB // 2]
    refs = refs[1 + NB // 2 :]
    returned_ref, near_ref, even_ref, odd_ref, proj_ref, hidden_ref, part_ref, *refs = refs
    far_sems, in_sems, out_sems = refs
    parts = far_sems.shape[0]
    step = returned_in.shape[0] // parts
    fetches = copies(
        [returned_in.at[pl.ds(i * step, step)] for i in range(parts)],
        [returned_ref.at[pl.ds(i * step, step)] for i in range(parts)],
        far_sems,
    )
    loads = copies(
        [
            near_in,
            hidden_in,
            query_grad_in,
            attn_in,
            early_in.at[pl.ds(0, HD)],
            early_in.at[pl.ds(HD, HD)],
        ],
        [
            near_ref,
            hidden_ref,
            proj_ref.at[pl.ds(0, HD)],
            proj_ref.at[pl.ds(3 * HD, HD)],
            part_ref.at[pl.ds(0, HD)],
            part_ref.at[pl.ds(3 * HD, HD)],
        ],
        in_sems,
    )
    start_all(fetches)
    start_all(loads)
    even_ref[...] = jnp.zeros_like(even_ref)
    odd_ref[...] = jnp.zeros_like(odd_ref)
    for i in range(parts):
        fetches[i].wait()

        def add(s, _):
            at = i * step + 2 * s
            even, odd = asked(home_ref, at), asked(home_ref, at + 1)
            even_ref[even] += returned_ref[at].astype(F32)
            odd_ref[odd] += returned_ref[at + 1].astype(F32)
            return 0

        lax.fori_loop(0, step // 2, add, 0, unroll=True)
    wait_all(loads)
    for i in range(NB):
        proj_ref[HD : 3 * HD, rows_at(i)] = (near_ref[i] + (even_ref[i] + odd_ref[i])).astype(BF16)
    odd_place = lax.rem(col_ref[0], 2)
    far_pieces, near_pieces = [], []
    for j in range(NB // 2):
        at = ORDER.index((NB - 2 * j) % NB)
        near_pieces.append(proj_ref.at[:, pl.ds(at * BLK, BLK)])
        next_at, last_at = ORDER.index((NB - 1 - 2 * j) % NB), ORDER.index((NB + 1 - 2 * j) % NB)
        at = jnp.where(odd_place == 1, last_at, next_at)
        far_pieces.append(proj_ref.at[:, pl.ds(pl.multiple_of(at * BLK, BLK), BLK)])
    stores = copies(
        [part_ref, *far_pieces, *near_pieces],
        [part_out, *(out.at[1] for out in pair_outs), *(out.at[0] for out in pair_outs)],
        out_sems,
    )
    start_all(stores[1:])
    hidden = hidden_ref[...].reshape(ROWS, D)
    part_ref[HD : 3 * HD, :] = dot(proj_ref[HD : 3 * HD, :], hidden).astype(BF16)
    stores[0].start()
    wait_all(stores)


def pack_body(*refs):
    *pair_ins, _, pack_out, pack_ref, in_sems, out_sems = refs
    loads = copies([pair.at[1] for pair in pair_ins], [pack_ref.at[j] for j in range(NB // 2)], in_sems)
    stores = copies(
        [pack_ref.at[j] for j in range(NB // 2)], [pack_out.at[j] for j in range(NB // 2)], out_sems
    )
    start_all(loads)
    for load, store in zip(loads, stores, strict=True):
        load.wait()
        store.start()
    wait_all(stores)


def sum_body(share_ref, total_ref):
    total = jnp.sum(share_ref[...].astype(F32), axis=0).astype(BF16)
    total_ref[...] = jnp.broadcast_to(total[None], total_ref.shape)


def scale_body(inv_root, total_ref, qkv_ref, out_ref):
    total = total_ref[...].astype(F32) * inv_root
    qkv_ref[...] = total[: 3 * HD]
    out_ref[...] = total[3 * HD :]


def head_terms(piece, weight):
    out = lax.dot_general(piece[3 * HD :, :], weight[3 * HD :, :], TN, preferred_element_type=F32)
    back = lax.dot_general(piece[: 3 * HD, :], weight[: 3 * HD, :], TN, preferred_element_type=F32)
    return out, back


def first_heads_body(*refs):
    n = NB // 2 - 1
    pair_ins, weight_ins, refs = refs[:n], refs[n : 2 * n], refs[2 * n :]
    sum_out, piece_ref, weight_ref, sum_ref, piece_sems, weight_sems, out_sems = refs
    pieces = copies([pair.at[0] for pair in pair_ins], [piece_ref.at[j] for j in range(n)], piece_sems)
    weights = copies(weight_ins, [weight_ref.at[j] for j in range(n)], weight_sems)
    start_all(pieces)
    start_all(weights)
    out = jnp.zeros((BLK, D), F32)
    back = jnp.zeros((BLK, D), F32)
    for j in range(n):
        pieces[j].wait()
        weights[j].wait()
        out_term, back_term = head_terms(piece_ref[j], weight_ref[j])
        out += out_term
        back += back_term
    sum_ref[0], sum_ref[1] = out, back
    store = pltpu.make_async_copy(sum_ref, sum_out, out_sems.at[0])
    store.start()
    store.wait()


def finish_body(col_ref, sum_in, pair_in, beside_in, *refs):
    half = NB // 2
    weight_ins, refs = refs[: half + 1], refs[half + 1 :]
    state_in, grad_in, gain_in, layer_out, back_out, *refs = refs
    sum_ref, pair_ref, piece_ref, weight_ref, state_ref, grad_ref, gain_ref, layer_ref, back_ref, *refs = refs
    piece_sems, weight_sems, in_sems, out_sems = refs
    pieces = copies([pair_in.at[0], beside_in], [pair_ref, piece_ref], piece_sems)
    weights = copies(weight_ins, [weight_ref.at[k] for k in range(half + 1)], weight_sems)
    loads = copies([sum_in, state_in, grad_in, gain_in], [sum_ref, state_ref, grad_ref, gain_ref], in_sems)
    start_all(pieces)
    start_all(weights)
    start_all(loads)
    wait_all(pieces)
    wait_all(weights)
    odd_place = lax.rem(col_ref[0], 2)
    out, back = head_terms(pair_ref[...], weight_ref[half])
    for j in range(half):
        beside = jnp.where(odd_place == 1, j, (j + half - 1) % half)
        out_term, back_term = head_terms(piece_ref[j], weight_ref[beside])
        out += out_term
        back += back_term
    wait_all(loads)
    out += sum_ref[0]
    back += sum_ref[1]
    state = state_ref[...].astype(F32)
    gain = gain_ref[...]
    layer_ref[...] = (state + out).astype(BF16)
    stores = copies([layer_ref, back_ref], [layer_out, back_out], out_sems)
    stores[0].start()
    inv = lax.rsqrt(jnp.mean(state * state, axis=1, keepdims=True) + EPS)
    stat = jnp.sum(gain * back * state, axis=1, keepdims=True)
    back_ref[...] = (
        grad_ref[...].astype(F32) + inv * gain * back - state * (inv * inv * inv * stat / D)
    ).astype(BF16)
    stores[1].start()
    wait_all(stores)


def shards(
    node_states,
    norm_gain,
    qkv_weight,
    out_weight,
    local_slots,
    local_live,
    far_owner,
    far_slot,
    out_grad,
):
    doms = lax.axis_size("dom")
    me = lax.axis_index("dom")
    col_index = lax.axis_index("col").astype(jnp.int32)
    col = col_index.reshape(1)
    slots = doms * CAP
    entries = NB * DEG
    gain = norm_gain[None]

    where = jnp.stack([me.astype(jnp.int32), col_index])
    names = shaped(*far_owner.shape[::-1], kind=jnp.int32)
    places, home, count = call(
        tables_body,
        (names, shaped(CAP, far_owner.shape[0], kind=jnp.int32), shaped(NB, ROWS, kind=F32)),
        [scalars()] + [whole()] * 4,
        out_specs=[whole()] * 3,
        name="tables",
    )(where, far_owner.T, far_slot.T, local_slots, local_live)

    unit = 2 * ROWS * ROWS * BLK
    node = shaped(BLK, D)
    across = shaped(HD, ROWS)
    block, blocks, blocks_float = shaped(BLK, BLK), shaped(NB, BLK, BLK), shaped(NB, BLK, BLK, kind=F32)
    blocks_most = shaped(NB - 1, BLK, BLK)
    wide, wide_float = shaped(NB, BLK, DEG * BLK), shaped(NB, BLK, DEG * BLK, kind=F32)
    exchanged = shaped(slots, BLK, BLK)
    row = shaped(1, D, kind=F32)
    counts = shaped(NB, ROWS, kind=F32)
    states, states_most = shaped(NB, BLK, D), shaped(NB - 1, BLK, D)
    head_weight, out_piece = shaped(3 * HD, D), shaped(HD, D)

    x1, x7 = ring_round(node_states, node_states)
    x1, x7, home, places, count = lax.optimization_barrier((x1, x7, home, places, count))
    x2, x6 = ring_round(x1, x7)
    x3, x5 = ring_round(x2, x6)
    x4 = shifted(x3, 1)
    state_chunks = (node_states, x1, x7, x2, x6, x3, x5, x4)
    projected = call(
        project_most_body,
        (blocks, blocks, exchanged),
        [scalars()] + [left()] * (NB + 1),
        scratch=[
            *held(states_most, row, head_weight, shaped((NB - 1) * BLK, D), blocks_most, blocks_most, exchanged),
            dma_sems(NB + 1),
            dma_sems(2),
            dma_sems(4),
        ],
        flops=2 * ROWS * D * 256,
        name="project_most",
    )(home, node_states, x1, x7, x2, x6, x3, x5, gain, qkv_weight)
    query, kv, outgoing = call(
        project_last_body,
        (blocks, blocks, exchanged),
        [scalars()] + [left()] * 6,
        scratch=[
            *held(node, row, head_weight, block, block),
            dma_sems(3),
            dma_sems(2),
            dma_sems(slots),
        ],
        flops=2 * BLK * D * 256,
        name="project_last",
        aliases={4: 0, 5: 1, 6: 2},
    )(home, x4, gain, qkv_weight, *projected)

    outgoing, grad_own = lax.optimization_barrier((outgoing, out_grad))
    fetched = lax.all_to_all(outgoing, "dom", 0, 0, tiled=True)
    g1, g7 = ring_round(grad_own, grad_own)
    g2, g6 = ring_round(g1, g7)
    g3, g5 = ring_round(g2, g6)
    g4 = shifted(g3, 1)
    grad_chunks = (out_grad, g1, g7, g2, g6, g3, g5, g4)

    (attn_grad,) = call(
        attn_grad_body,
        (blocks_float,),
        [left()] * NB,
        scratch=[
            *held(states_most, out_piece, shaped(NB - 1, BLK, BLK, kind=F32)),
            dma_sems(NB),
            dma_sems(1),
        ],
        flops=2 * ROWS * D * BLK,
        name="attn_grad",
    )(*grad_chunks[:-1], out_weight)

    (near,) = call(
        near_forward_body,
        (blocks_float,),
        [scalars()] + [left()] * 3,
        scratch=[*held(blocks, blocks, counts, blocks_float, shaped(ROWS, BLK)), dma_sems(3), dma_sems(NB)],
        flops=2 * unit,
        name="near_forward",
    )(col, query, kv, count)

    (attn_grad,) = call(
        attn_grad_last_body,
        (blocks_float,),
        [left()] * 3,
        scratch=[*held(node, out_piece, shaped(BLK, BLK, kind=F32)), dma_sems(2), dma_sems(1)],
        flops=2 * BLK * D * BLK,
        name="attn_grad_last",
        aliases={2: 0},
    )(g4, out_weight, attn_grad)

    attn, scaled, extra, outgoing_back = call(
        far_body,
        (across, blocks, blocks_float, exchanged),
        [scalars()] * 2 + [left()] * 4,
        scratch=[
            *held(blocks, exchanged, blocks_float, blocks_float),
            *held(across, blocks, blocks_float, wide_float, wide, wide_float, blocks_float),
            *held(blocks, shaped(entries, BLK, BLK)),
            dma_sems(4),
            dma_sems(3),
            dma_sems(2),
            dma_sems(NB),
            dma_sems(entries),
        ],
        flops=2 * unit,
        name="far_both",
    )(where, places, query, fetched, near, attn_grad)

    outgoing_back, weights_own = lax.optimization_barrier(
        (outgoing_back, jnp.concatenate([qkv_weight, out_weight], axis=0))
    )
    returned = lax.all_to_all(outgoing_back, "dom", 0, 0, tiled=True)
    w1, w7 = ring_round(weights_own, weights_own)
    w2, w6 = ring_round(w1, w7)

    query_grad, near_grad, early, hidden = call(
        near_backward_body,
        (across, blocks_float, shaped(2 * HD, D), states),
        [scalars()] + [left()] * (2 * NB + 7),
        scratch=[
            *held(states, states, row, blocks, blocks, counts, blocks, blocks_float, across, states),
            *held(across, blocks_float, shaped(2 * HD, D), shaped(BLK, ROWS, kind=F32)),
            dma_sems(5),
            dma_sems(2 * NB + 2),
            dma_sems(4),
        ],
        flops=5 * unit,
        name="near_backward",
    )(col, *grad_chunks, *state_chunks, gain, query, kv, count, scaled, extra, attn)

    w2, w6, near_grad = lax.optimization_barrier((w2, w6, near_grad))
    w3, w5 = ring_round(w2, w6)
    returned, w3, w5 = lax.optimization_barrier((returned, w3, w5))
    w4 = shifted(w3, 1)

    half = NB // 2
    *pairs, part = call(
        gather_grads_body,
        (*(shaped(2, 4 * HD, BLK),) * half, shaped(4 * HD, D)),
        [scalars()] * 2 + [left()] * 6,
        scratch=[
            *held(exchanged, blocks_float, shaped(NB + 1, BLK, BLK, kind=F32)),
            *held(shaped(NB + 1, BLK, BLK, kind=F32), shaped(4 * HD, ROWS), states, shaped(4 * HD, D)),
            dma_sems(4),
            dma_sems(6),
            dma_sems(1 + NB),
        ],
        flops=2 * ROWS * D * 128,
        name="gather_grads",
    )(col, home, returned, near_grad, query_grad, attn, hidden, early)

    share_rows = 4 * HD // doms
    shares = lax.all_to_all(part.reshape(doms, share_rows, D), "dom", 0, 0, tiled=True)
    *pairs, w4 = lax.optimization_barrier((*pairs, w4))
    pairs = [pairs[0], *(shifted(pairs[j], 2 * j) for j in range(1, half))]
    (totals,) = call(
        sum_body,
        (shaped(doms, share_rows, D),),
        [whole()],
        out_specs=[whole()],
        name="sum_shares",
        limit=4,
    )(shares)
    total = lax.all_to_all(totals, "dom", 0, 0, tiled=True).reshape(4 * HD, D)
    packed = shaped(half, 4 * HD, BLK)
    (beside,) = call(
        pack_body,
        (packed,),
        [left()] * (half + 1),
        scratch=[*held(packed), dma_sems(half), dma_sems(half)],
        name="pack",
    )(*pairs, totals)
    beside = paired(beside)
    sums, piece, weight = shaped(2, BLK, D, kind=F32), shaped(4 * HD, BLK), shaped(4 * HD, D)
    (first,) = call(
        first_heads_body,
        (sums,),
        [left()] * (2 * half - 2),
        scratch=[
            *held(shaped(half - 1, 4 * HD, BLK), shaped(half - 1, 4 * HD, D), sums),
            dma_sems(half - 1),
            dma_sems(half - 1),
            dma_sems(1),
        ],
        flops=unit // 100,
        name="first_heads",
    )(pairs[0], pairs[1], pairs[3], weights_own, w2, w6)
    layer_out, state_grad = call(
        finish_body,
        (node, node),
        [scalars()] + [left()] * (3 + half + 1 + 3),
        scratch=[
            *held(sums, piece, packed, shaped(half + 1, 4 * HD, D), node, node, row, node, node),
            dma_sems(2),
            dma_sems(half + 1),
            dma_sems(4),
            dma_sems(2),
        ],
        flops=unit // 100,
        name="finish",
    )(col, first, pairs[2], beside, w1, w3, w5, w7, w4, node_states, out_grad, gain)
    qkv_grad, out_weight_grad = call(
        functools.partial(scale_body, 1.0 / math.sqrt(far_owner.shape[0] * BLK)),
        (shaped(3 * HD, D, kind=F32), shaped(HD, D, kind=F32)),
        [whole()],
        out_specs=[whole()] * 2,
        flops=3 * unit,
        name="scale",
        limit=4,
    )(total)

    return (layer_out, state_grad, qkv_grad, out_weight_grad)


def solution(mesh):
    placed = (
        P(("dom", "col"), None),
        P(),
        P("col", None),
        P("col", None),
        P("dom", None),
        P("dom", None),
        P(),
        P(),
        P(("dom", "col"), None),
    )
    return jax.shard_map(
        shards,
        mesh=mesh,
        in_specs=placed,
        out_specs=(
            P(("dom", "col"), None),
            P(("dom", "col"), None),
            P("col", None),
            P("col", None),
        ),
        check_vma=False,
    )
```

```python
import functools
import math

import jax
import jax.numpy as jnp
from jax import lax
from jax.experimental import pallas as pl
from jax.experimental.pallas import tpu as pltpu
from jax.sharding import PartitionSpec as P

D = 512
HD = 64
BLK = 128
NB = 8
DEG = 4
CAP = 2
ROWS = NB * BLK
EPS = 1e-06
SCALE = 1.0 / math.sqrt(HD)

F32 = jnp.float32
BF16 = jnp.bfloat16
MIB = 1024 * 1024
LIMIT = 64
ORDER = (0, 1, 7, 2, 6, 3, 5, 4)

NT = (((1,), (1,)), ((), ()))
TN = (((0,), (0,)), ((), ()))


def dot(a, b):
    return jnp.dot(a, b, preferred_element_type=F32)


def dot_nt(a, b):
    return lax.dot_general(a, b, NT, preferred_element_type=F32)


def whole():
    return pl.BlockSpec(memory_space=pltpu.VMEM)


def scalars():
    return pl.BlockSpec(memory_space=pltpu.SMEM)


def left():
    return pl.BlockSpec(memory_space=pl.ANY)


def shaped(*dims, kind=BF16):
    return jax.ShapeDtypeStruct(dims, kind)


def call(body, outs, ins, scratch=(), flops=0, name=None, out_specs=None, limit=LIMIT, aliases=None):
    return pl.pallas_call(
        body,
        out_shape=outs,
        in_specs=ins,
        out_specs=out_specs or [left() for _ in outs],
        scratch_shapes=list(scratch),
        input_output_aliases=aliases or {},
        compiler_params=pltpu.CompilerParams(vmem_limit_bytes=limit * MIB),
        cost_estimate=pl.CostEstimate(flops=flops, bytes_accessed=1 << 20, transcendentals=0),
        name=name,
    )


def held(*shapes):
    return [pltpu.VMEM(s.shape, s.dtype) for s in shapes]


def dma_sems(n):
    return pltpu.SemaphoreType.DMA((n,))


def copies(sources, targets, sems):
    return [
        pltpu.make_async_copy(a, b, sems.at[i]) for i, (a, b) in enumerate(zip(sources, targets, strict=True))
    ]


def start_all(jobs):
    for job in jobs:
        job.start()


def wait_all(jobs):
    for job in jobs:
        job.wait()


def lanes_low(shape):
    return lax.broadcasted_iota(jnp.int32, shape, len(shape) - 1) < HD


def rows_at(i):
    return slice(i * BLK, (i + 1) * BLK)


def shifted(x, k):
    return lax.ppermute(x, "col", [(i, (i + k) % NB) for i in range(NB)])


def ring_round(behind, ahead):
    return shifted(behind, 1), shifted(ahead, -1)


def paired(x):
    return lax.ppermute(x, "col", [(i, i ^ 1) for i in range(NB)])


def block_at(col, i):
    return lax.rem(col + NB - ORDER[i], NB)


def tables_body(where_ref, owner_ref, slot_ref, near_ref, live_ref, place_ref, home_ref, count_ref):
    me, col = where_ref[0], where_ref[1]
    owner = owner_ref[...]
    lane = lax.broadcasted_iota(jnp.int32, owner.shape, 1)
    row = lax.rem(lane, NB)
    rank = jnp.zeros_like(owner)
    for d in range(1, NB):
        earlier = pltpu.roll(owner, d, 1)
        for j in range(DEG):
            same = (owner == earlier[j : j + 1, :]) & (row >= d)
            rank += same.astype(jnp.int32)
    place_ref[...] = owner * CAP + rank
    wanted = jnp.zeros_like(owner)
    for i in range(NB):
        wanted += jnp.where(slot_ref[...] == block_at(col, i), i, 0)
    for c in range(CAP):
        asked = jnp.where((owner == me) & (rank == c), wanted, NB)
        least = asked[0:1, :]
        for j in range(1, DEG):
            least = jnp.minimum(least, asked[j : j + 1, :])
        for d in (1, 2, 4):
            least = jnp.minimum(least, pltpu.roll(least, d, 1))
        home_ref[c : c + 1, :] = least
    near, live = near_ref[...], live_ref[...]
    own = lax.broadcasted_iota(jnp.int32, (NB, 1), 0)
    for i in range(NB):
        block = block_at(col, i)
        hits = ((near == block) & (live != 0)).astype(F32)
        count = jnp.sum(hits, axis=1, keepdims=True) + (own == block).astype(F32)
        count_ref[:, rows_at(i)] = jnp.broadcast_to(count, (NB, BLK))


def asked(home_ref, s):
    return home_ref[s % CAP, (s // CAP) * NB + NB - 1]


def normed(x_low, gain):
    x = x_low.astype(F32)
    inv = lax.rsqrt(jnp.mean(x * x, axis=1, keepdims=True) + EPS)
    return (x * inv * gain).astype(BF16)


def wide_weight(weight):
    return jnp.concatenate([weight[:HD], jnp.zeros((HD, D), BF16), weight[HD:]], axis=0)


def project_most_body(send_ref, *refs):
    chunk_ins, refs = refs[: NB - 1], refs[NB - 1 :]
    gain_in, weight_in, query_out, kv_out, sent_out, *refs = refs
    chunk_ref, gain_ref, weight_ref, hidden_ref, query_ref, kv_ref, sent_ref, *refs = refs
    in_sems, out_sems, sent_sems = refs
    loads = copies(
        [weight_in, gain_in, *chunk_ins],
        [weight_ref, gain_ref, *(chunk_ref.at[i] for i in range(NB - 1))],
        in_sems,
    )
    start_all(loads)
    wait_all(loads[:2])
    gain = gain_ref[...]
    wide = wide_weight(weight_ref[...])
    for i in range(NB - 1):
        loads[2 + i].wait()
        hidden_ref[rows_at(i), :] = normed(chunk_ref[i], gain)
    proj = dot_nt(hidden_ref[...], wide).astype(BF16)
    for i in range(NB - 1):
        query_ref[i] = proj[rows_at(i), :BLK] * jnp.asarray(SCALE, BF16)
        kv_ref[i] = proj[rows_at(i), BLK:]
    most = pl.ds(0, NB - 1)
    parts = sent_sems.shape[0]
    step = sent_ref.shape[0] // parts
    sends = copies(
        [sent_ref.at[pl.ds(i * step, step)] for i in range(parts)],
        [sent_out.at[pl.ds(i * step, step)] for i in range(parts)],
        sent_sems,
    )
    stores = copies([query_ref, kv_ref], [query_out.at[most], kv_out.at[most]], out_sems)
    start_all(stores)
    for i in range(parts):

        def fill(s, _):
            sent_ref[i * step + s] = kv_ref[jnp.minimum(asked(send_ref, i * step + s), NB - 2)]
            return 0

        lax.fori_loop(0, step, fill, 0, unroll=True)
        sends[i].start()
    wait_all(stores)
    wait_all(sends)


def project_last_body(send_ref, chunk_in, gain_in, weight_in, query_in, kv_in, sent_in, *refs):
    query_out, kv_out, sent_out, *refs = refs
    chunk_ref, gain_ref, weight_ref, query_ref, kv_ref, in_sems, out_sems, sent_sems = refs
    loads = copies([chunk_in, gain_in, weight_in], [chunk_ref, gain_ref, weight_ref], in_sems)
    start_all(loads)
    wait_all(loads)
    hidden = normed(chunk_ref[...], gain_ref[...])
    kv_ref[...] = dot_nt(hidden, weight_ref[HD:, :]).astype(BF16)

    def over_slots(act):
        for slot in range(sent_sems.shape[0]):

            @pl.when(asked(send_ref, slot) == NB - 1)
            def _():
                act(pltpu.make_async_copy(kv_ref, sent_out.at[slot], sent_sems.at[slot]))

    over_slots(lambda job: job.start())
    query = dot_nt(hidden, wide_weight(weight_ref[...])[:BLK]).astype(BF16)
    query_ref[...] = query * jnp.asarray(SCALE, BF16)
    stores = copies([query_ref, kv_ref], [query_out.at[NB - 1], kv_out.at[NB - 1]], out_sems)
    start_all(stores)
    over_slots(lambda job: job.wait())
    wait_all(stores)


def attn_grad_body(*refs):
    n = NB - 1
    chunk_ins, refs = refs[:n], refs[n:]
    weight_in, ag_out, chunk_ref, weight_ref, ag_ref, sems, out_sems = refs
    loads = copies([weight_in, *chunk_ins], [weight_ref, *(chunk_ref.at[i] for i in range(n))], sems)
    start_all(loads)
    wait_all(loads)
    wide = jnp.concatenate([jnp.zeros((HD, D), BF16), weight_ref[...]], axis=0)
    ag_ref[...] = dot_nt(chunk_ref[...].reshape(n * BLK, D), wide).reshape(n, BLK, BLK)
    store = pltpu.make_async_copy(ag_ref, ag_out.at[pl.ds(0, n)], out_sems.at[0])
    store.start()
    store.wait()


def attn_grad_last_body(chunk_in, weight_in, ag_in, ag_out, chunk_ref, weight_ref, ag_ref, sems, out_sems):
    loads = copies([chunk_in, weight_in], [chunk_ref, weight_ref], sems)
    start_all(loads)
    wait_all(loads)
    wide = jnp.concatenate([jnp.zeros((HD, D), BF16), weight_ref[...]], axis=0)
    ag_ref[...] = dot_nt(chunk_ref[...], wide)
    store = pltpu.make_async_copy(ag_ref, ag_out.at[NB - 1], out_sems.at[0])
    store.start()
    store.wait()


def near_forward_body(col_ref, query_in, kv_in, count_in, num_out, *refs):
    query_ref, kv_ref, count_ref, num_ref, ones_ref, in_sems, out_sems = refs
    loads = copies([kv_in, query_in, count_in], [kv_ref, query_ref, count_ref], in_sems)
    start_all(loads)
    wait_all(loads)
    kv = kv_ref[...].reshape(ROWS, BLK)
    ones_ref[...] = jnp.where(lanes_low(kv.shape), jnp.asarray(1, BF16), kv)
    stores = copies([num_ref.at[i] for i in range(NB)], [num_out.at[i] for i in range(NB)], out_sems)
    for i in range(NB):
        score = dot_nt(query_ref[i], kv_ref[...].reshape(ROWS, BLK))
        prob = jnp.exp(score) * count_ref[pl.ds(block_at(col_ref[0], i), 1), :]
        num_ref[i] = dot(prob.astype(BF16), ones_ref[...])
        stores[i].start()
    wait_all(stores)


def far_body(where_ref, place_ref, query_in, far_in, num_in, ag_in, *refs):
    attn_out, scaled_out, extra_out, back_out, *refs = refs
    query_ref, far_ref, num_ref, ag_ref, *refs = refs
    attn_ref, scaled_ref, extra_ref, prob_ref, prob_low_ref, diff_ref, den_ref, both_ref, stage_ref, *refs = refs
    far_sems, in_sems, out_sems, extra_sems, back_sems = refs
    me, col = where_ref[0], where_ref[1]
    places = [place_ref[j, me * NB + block_at(col, i)] for i in range(NB) for j in range(DEG)]
    parts = far_sems.shape[0]
    step = far_in.shape[0] // parts
    fetches = copies(
        [far_in.at[pl.ds(i * step, step)] for i in range(parts)],
        [far_ref.at[pl.ds(i * step, step)] for i in range(parts)],
        far_sems,
    )
    loads = copies([query_in, ag_in, num_in], [query_ref, ag_ref, num_ref], in_sems)
    loads[0].start()
    start_all(fetches)
    start_all(loads[1:])

    def keys(i):
        return jnp.concatenate([far_ref[places[i * DEG + j]] for j in range(DEG)], axis=0)

    wait_all(loads[:1])
    wait_all(fetches)
    wait_all(loads[1:2])
    for i in range(NB):
        kv = keys(i)
        both = jnp.concatenate([query_ref[i], ag_ref[i].astype(BF16)], axis=0)
        score = dot_nt(both, kv)
        prob = jnp.exp(score[:BLK])
        prob_ref[i] = prob
        diff_ref[i] = score[BLK:]
        prob_low = prob.astype(BF16)
        prob_low_ref[i] = prob_low
        values = jnp.where(lanes_low(kv.shape), jnp.asarray(1, BF16), kv)
        extra_ref[i] = dot(prob_low, values)
    loads[2].wait()
    stores = copies([attn_ref, scaled_ref], [attn_out, scaled_out], out_sems)
    for i in range(NB):
        num = num_ref[i] + extra_ref[i]
        den = jnp.where(lanes_low(num.shape), num, pltpu.roll(num, HD, 1))
        inv = 1.0 / den
        attn = num * inv
        grad = ag_ref[i]
        scaled = (grad * inv).astype(BF16)
        scaled_ref[i] = scaled
        den_ref[i] = inv
        extra_ref[i] = jnp.sum(grad * attn, axis=1, keepdims=True) * inv
        attn_ref[:, rows_at(i)] = attn.astype(BF16).T[HD:]
        both_ref[i] = (query_ref[i] + scaled).T
    start_all(stores)
    jobs = []
    for i in range(NB):
        kv = keys(i)
        corr = extra_ref[i]
        diff = diff_ref[i] * den_ref[i, :, :1] - corr[:, :1]
        score_grad = (prob_ref[i] * diff).astype(BF16)
        extra_ref[i] = jnp.where(lanes_low(corr.shape), dot(score_grad, kv), corr)
        key_grad = dot(both_ref[i, :HD], score_grad).astype(BF16)
        value_grad = dot(both_ref[i, HD:], prob_low_ref[i]).astype(BF16)
        for j in range(DEG):
            e = i * DEG + j
            stage_ref[e, :HD, :] = key_grad[:, rows_at(j)]
            stage_ref[e, HD:, :] = value_grad[:, rows_at(j)]
            jobs.append(pltpu.make_async_copy(stage_ref.at[e], back_out.at[places[e]], back_sems.at[e]))
            jobs[-1].start()
        jobs.append(pltpu.make_async_copy(extra_ref.at[i], extra_out.at[i], extra_sems.at[i]))
        jobs[-1].start()
    wait_all(stores)
    wait_all(jobs)


def near_backward_body(col_ref, *refs):
    grad_ins, state_ins, refs = refs[:NB], refs[NB : 2 * NB], refs[2 * NB :]
    gain_in, query_in, kv_in, count_in, scaled_in, extra_in, attn_in, *refs = refs
    query_grad_out, near_out, part_out, hidden_out, *refs = refs
    grad_ref, state_ref, gain_ref, query_ref, kv_ref, count_ref, scaled_ref, extra_ref, attn_ref, hidden_ref, *refs = refs
    query_grad_ref, near_ref, part_ref, acc_ref, in_sems, late_sems, out_sems = refs
    loads = copies(
        [kv_in, query_in, count_in, scaled_in, extra_in],
        [kv_ref, query_ref, count_ref, scaled_ref, extra_ref],
        in_sems,
    )
    late = copies(
        [gain_in, *state_ins, attn_in, *grad_ins],
        [
            gain_ref,
            *(state_ref.at[i] for i in range(NB)),
            attn_ref,
            *(grad_ref.at[i] for i in range(NB)),
        ],
        late_sems,
    )
    start_all(loads)
    start_all(late)
    wait_all(loads)
    acc_ref[...] = jnp.zeros_like(acc_ref)
    col = col_ref[0]
    for i in range(NB):
        query, scaled, extra = query_ref[i], scaled_ref[i], extra_ref[i]
        kv = kv_ref[...].reshape(ROWS, BLK)
        prob = jnp.exp(dot_nt(query, kv)) * count_ref[pl.ds(block_at(col, i), 1), :]
        diff = dot_nt(scaled, kv) - extra[:, HD : HD + 1]
        score_grad = (prob * diff).astype(BF16)
        query_grad = dot(score_grad, kv) + extra
        query_grad_ref[:, rows_at(i)] = (query_grad.T[:HD] * SCALE).astype(BF16)
        both = (query + scaled).astype(F32).T.astype(BF16)
        acc_ref[:HD, :] += dot(both[:HD], score_grad)
        acc_ref[HD:, :] += dot(both[HD:], prob.astype(BF16))
    for i in range(NB):
        near_ref[i] = acc_ref[:, rows_at(i)]
    stores = copies(
        [query_grad_ref, near_ref, hidden_ref, part_ref],
        [query_grad_out, near_out, hidden_out, part_out],
        out_sems,
    )
    start_all(stores[:2])
    wait_all(late)
    gain = gain_ref[...]
    for i in range(NB):
        hidden_ref[i] = normed(state_ref[i], gain)
    stores[2].start()
    part_ref[:HD, :] = dot(query_grad_ref[...], hidden_ref[...].reshape(ROWS, D)).astype(BF16)
    part_ref[HD:, :] = dot(attn_ref[...], grad_ref[...].reshape(ROWS, D)).astype(BF16)
    stores[3].start()
    wait_all(stores)


def gather_grads_body(col_ref, home_ref, returned_in, near_in, query_grad_in, attn_in, hidden_in, early_in, *refs):
    *pair_outs, part_out = refs[: 1 + NB // 2]
    refs = refs[1 + NB // 2 :]
    returned_ref, near_ref, even_ref, odd_ref, proj_ref, hidden_ref, part_ref, *refs = refs
    far_sems, in_sems, out_sems = refs
    parts = far_sems.shape[0]
    step = returned_in.shape[0] // parts
    fetches = copies(
        [returned_in.at[pl.ds(i * step, step)] for i in range(parts)],
        [returned_ref.at[pl.ds(i * step, step)] for i in range(parts)],
        far_sems,
    )
    loads = copies(
        [
            near_in,
            hidden_in,
            query_grad_in,
            attn_in,
            early_in.at[pl.ds(0, HD)],
            early_in.at[pl.ds(HD, HD)],
        ],
        [
            near_ref,
            hidden_ref,
            proj_ref.at[pl.ds(0, HD)],
            proj_ref.at[pl.ds(3 * HD, HD)],
            part_ref.at[pl.ds(0, HD)],
            part_ref.at[pl.ds(3 * HD, HD)],
        ],
        in_sems,
    )
    start_all(fetches)
    start_all(loads)
    even_ref[...] = jnp.zeros_like(even_ref)
    odd_ref[...] = jnp.zeros_like(odd_ref)
    for i in range(parts):
        fetches[i].wait()

        def add(s, _):
            at = i * step + 2 * s
            even, odd = asked(home_ref, at), asked(home_ref, at + 1)
            even_ref[even] += returned_ref[at].astype(F32)
            odd_ref[odd] += returned_ref[at + 1].astype(F32)
            return 0

        lax.fori_loop(0, step // 2, add, 0, unroll=True)
    wait_all(loads)
    for i in range(NB):
        proj_ref[HD : 3 * HD, rows_at(i)] = (near_ref[i] + (even_ref[i] + odd_ref[i])).astype(BF16)
    odd_place = lax.rem(col_ref[0], 2)
    far_pieces, near_pieces = [], []
    for j in range(NB // 2):
        at = ORDER.index((NB - 2 * j) % NB)
        near_pieces.append(proj_ref.at[:, pl.ds(at * BLK, BLK)])
        next_at, last_at = ORDER.index((NB - 1 - 2 * j) % NB), ORDER.index((NB + 1 - 2 * j) % NB)
        at = jnp.where(odd_place == 1, last_at, next_at)
        far_pieces.append(proj_ref.at[:, pl.ds(pl.multiple_of(at * BLK, BLK), BLK)])
    stores = copies(
        [
            *(part_ref.at[pl.ds(at, rows)] for at, rows in ((HD, 2 * HD), (0, HD), (3 * HD, HD))),
            *far_pieces,
            *near_pieces,
        ],
        [
            *(part_out.at[pl.ds(at, rows)] for at, rows in ((HD, 2 * HD), (0, HD), (3 * HD, HD))),
            *(out.at[1] for out in pair_outs),
            *(out.at[0] for out in pair_outs),
        ],
        out_sems,
    )
    start_all(stores[1:])
    hidden = hidden_ref[...].reshape(ROWS, D)
    part_ref[HD : 3 * HD, :] = dot(proj_ref[HD : 3 * HD, :], hidden).astype(BF16)
    stores[0].start()
    wait_all(stores)


def pack_body(*refs):
    *pair_ins, _, pack_out, pack_ref, in_sems, out_sems = refs
    loads = copies([pair.at[1] for pair in pair_ins], [pack_ref.at[j] for j in range(NB // 2)], in_sems)
    stores = copies(
        [pack_ref.at[j] for j in range(NB // 2)], [pack_out.at[j] for j in range(NB // 2)], out_sems
    )
    start_all(loads)
    for load, store in zip(loads, stores, strict=True):
        load.wait()
        store.start()
    wait_all(stores)


def sum_body(share_ref, total_ref):
    total = jnp.sum(share_ref[...].astype(F32), axis=0).astype(BF16)
    total_ref[...] = jnp.broadcast_to(total[None], total_ref.shape)


def scale_body(inv_root, total_ref, qkv_ref, out_ref):
    total = total_ref[...].astype(F32) * inv_root
    qkv_ref[...] = total[: 3 * HD]
    out_ref[...] = total[3 * HD :]


def head_terms(piece, weight):
    out = lax.dot_general(piece[3 * HD :, :], weight[3 * HD :, :], TN, preferred_element_type=F32)
    back = lax.dot_general(piece[: 3 * HD, :], weight[: 3 * HD, :], TN, preferred_element_type=F32)
    return out, back


def first_heads_body(*refs):
    n = NB // 2 - 1
    pair_ins, weight_ins, refs = refs[:n], refs[n : 2 * n], refs[2 * n :]
    sum_out, piece_ref, weight_ref, sum_ref, piece_sems, weight_sems, out_sems = refs
    pieces = copies([pair.at[0] for pair in pair_ins], [piece_ref.at[j] for j in range(n)], piece_sems)
    weights = copies(weight_ins, [weight_ref.at[j] for j in range(n)], weight_sems)
    start_all(pieces)
    start_all(weights)
    out = jnp.zeros((BLK, D), F32)
    back = jnp.zeros((BLK, D), F32)
    for j in range(n):
        pieces[j].wait()
        weights[j].wait()
        out_term, back_term = head_terms(piece_ref[j], weight_ref[j])
        out += out_term
        back += back_term
    sum_ref[0], sum_ref[1] = out, back
    store = pltpu.make_async_copy(sum_ref, sum_out, out_sems.at[0])
    store.start()
    store.wait()


def finish_body(col_ref, sum_in, pair_in, beside_in, *refs):
    half = NB // 2
    weight_ins, refs = refs[: half + 1], refs[half + 1 :]
    state_in, grad_in, gain_in, layer_out, back_out, *refs = refs
    sum_ref, pair_ref, piece_ref, weight_ref, state_ref, grad_ref, gain_ref, layer_ref, back_ref, *refs = refs
    piece_sems, weight_sems, in_sems, out_sems = refs
    pieces = copies([pair_in.at[0], beside_in], [pair_ref, piece_ref], piece_sems)
    weights = copies(weight_ins, [weight_ref.at[k] for k in range(half + 1)], weight_sems)
    loads = copies([sum_in, state_in, grad_in, gain_in], [sum_ref, state_ref, grad_ref, gain_ref], in_sems)
    start_all(pieces)
    start_all(weights)
    start_all(loads)
    wait_all(pieces)
    wait_all(weights)
    odd_place = lax.rem(col_ref[0], 2)
    out, back = head_terms(pair_ref[...], weight_ref[half])
    for j in range(half):
        beside = jnp.where(odd_place == 1, j, (j + half - 1) % half)
        out_term, back_term = head_terms(piece_ref[j], weight_ref[beside])
        out += out_term
        back += back_term
    wait_all(loads)
    out += sum_ref[0]
    back += sum_ref[1]
    state = state_ref[...].astype(F32)
    gain = gain_ref[...]
    layer_ref[...] = (state + out).astype(BF16)
    stores = copies([layer_ref, back_ref], [layer_out, back_out], out_sems)
    stores[0].start()
    inv = lax.rsqrt(jnp.mean(state * state, axis=1, keepdims=True) + EPS)
    stat = jnp.sum(gain * back * state, axis=1, keepdims=True)
    back_ref[...] = (
        grad_ref[...].astype(F32) + inv * gain * back - state * (inv * inv * inv * stat / D)
    ).astype(BF16)
    stores[1].start()
    wait_all(stores)


def shards(
    node_states,
    norm_gain,
    qkv_weight,
    out_weight,
    local_slots,
    local_live,
    far_owner,
    far_slot,
    out_grad,
):
    doms = lax.axis_size("dom")
    me = lax.axis_index("dom")
    col_index = lax.axis_index("col").astype(jnp.int32)
    col = col_index.reshape(1)
    slots = doms * CAP
    entries = NB * DEG
    gain = norm_gain[None]

    where = jnp.stack([me.astype(jnp.int32), col_index])
    names = shaped(*far_owner.shape[::-1], kind=jnp.int32)
    places, home, count = call(
        tables_body,
        (names, shaped(CAP, far_owner.shape[0], kind=jnp.int32), shaped(NB, ROWS, kind=F32)),
        [scalars()] + [whole()] * 4,
        out_specs=[whole()] * 3,
        name="tables",
    )(where, far_owner.T, far_slot.T, local_slots, local_live)

    unit = 2 * ROWS * ROWS * BLK
    node = shaped(BLK, D)
    across = shaped(HD, ROWS)
    block, blocks, blocks_float = shaped(BLK, BLK), shaped(NB, BLK, BLK), shaped(NB, BLK, BLK, kind=F32)
    blocks_most = shaped(NB - 1, BLK, BLK)
    wide, wide_float = shaped(NB, BLK, DEG * BLK), shaped(NB, BLK, DEG * BLK, kind=F32)
    exchanged = shaped(slots, BLK, BLK)
    row = shaped(1, D, kind=F32)
    counts = shaped(NB, ROWS, kind=F32)
    states, states_most = shaped(NB, BLK, D), shaped(NB - 1, BLK, D)
    head_weight, out_piece = shaped(3 * HD, D), shaped(HD, D)

    x1, x7 = ring_round(node_states, node_states)
    x1, x7, home, places, count = lax.optimization_barrier((x1, x7, home, places, count))
    x2, x6 = ring_round(x1, x7)
    x3, x5 = ring_round(x2, x6)
    x4 = shifted(x3, 1)
    state_chunks = (node_states, x1, x7, x2, x6, x3, x5, x4)
    projected = call(
        project_most_body,
        (blocks, blocks, exchanged),
        [scalars()] + [left()] * (NB + 1),
        scratch=[
            *held(states_most, row, head_weight, shaped((NB - 1) * BLK, D), blocks_most, blocks_most, exchanged),
            dma_sems(NB + 1),
            dma_sems(2),
            dma_sems(4),
        ],
        flops=2 * ROWS * D * 256,
        name="project_most",
    )(home, node_states, x1, x7, x2, x6, x3, x5, gain, qkv_weight)
    query, kv, outgoing = call(
        project_last_body,
        (blocks, blocks, exchanged),
        [scalars()] + [left()] * 6,
        scratch=[
            *held(node, row, head_weight, block, block),
            dma_sems(3),
            dma_sems(2),
            dma_sems(slots),
        ],
        flops=2 * BLK * D * 256,
        name="project_last",
        aliases={4: 0, 5: 1, 6: 2},
    )(home, x4, gain, qkv_weight, *projected)

    outgoing, grad_own = lax.optimization_barrier((outgoing, out_grad))
    fetched = lax.all_to_all(outgoing, "dom", 0, 0, tiled=True)
    g1, g7 = ring_round(grad_own, grad_own)
    g2, g6 = ring_round(g1, g7)
    g3, g5 = ring_round(g2, g6)
    g4 = shifted(g3, 1)
    grad_chunks = (out_grad, g1, g7, g2, g6, g3, g5, g4)

    (attn_grad,) = call(
        attn_grad_body,
        (blocks_float,),
        [left()] * NB,
        scratch=[
            *held(states_most, out_piece, shaped(NB - 1, BLK, BLK, kind=F32)),
            dma_sems(NB),
            dma_sems(1),
        ],
        flops=2 * ROWS * D * BLK,
        name="attn_grad",
    )(*grad_chunks[:-1], out_weight)

    (near,) = call(
        near_forward_body,
        (blocks_float,),
        [scalars()] + [left()] * 3,
        scratch=[*held(blocks, blocks, counts, blocks_float, shaped(ROWS, BLK)), dma_sems(3), dma_sems(NB)],
        flops=2 * unit,
        name="near_forward",
    )(col, query, kv, count)

    (attn_grad,) = call(
        attn_grad_last_body,
        (blocks_float,),
        [left()] * 3,
        scratch=[*held(node, out_piece, shaped(BLK, BLK, kind=F32)), dma_sems(2), dma_sems(1)],
        flops=2 * BLK * D * BLK,
        name="attn_grad_last",
        aliases={2: 0},
    )(g4, out_weight, attn_grad)

    attn, scaled, extra, outgoing_back = call(
        far_body,
        (across, blocks, blocks_float, exchanged),
        [scalars()] * 2 + [left()] * 4,
        scratch=[
            *held(blocks, exchanged, blocks_float, blocks_float),
            *held(across, blocks, blocks_float, wide_float, wide, wide_float, blocks_float),
            *held(blocks, shaped(entries, BLK, BLK)),
            dma_sems(4),
            dma_sems(3),
            dma_sems(2),
            dma_sems(NB),
            dma_sems(entries),
        ],
        flops=2 * unit,
        name="far_both",
    )(where, places, query, fetched, near, attn_grad)

    outgoing_back, weights_own = lax.optimization_barrier(
        (outgoing_back, jnp.concatenate([qkv_weight, out_weight], axis=0))
    )
    returned = lax.all_to_all(outgoing_back, "dom", 0, 0, tiled=True)
    w1, w7 = ring_round(weights_own, weights_own)
    w2, w6 = ring_round(w1, w7)

    query_grad, near_grad, early, hidden = call(
        near_backward_body,
        (across, blocks_float, shaped(2 * HD, D), states),
        [scalars()] + [left()] * (2 * NB + 7),
        scratch=[
            *held(states, states, row, blocks, blocks, counts, blocks, blocks_float, across, states),
            *held(across, blocks_float, shaped(2 * HD, D), shaped(BLK, ROWS, kind=F32)),
            dma_sems(5),
            dma_sems(2 * NB + 2),
            dma_sems(4),
        ],
        flops=5 * unit,
        name="near_backward",
    )(col, *grad_chunks, *state_chunks, gain, query, kv, count, scaled, extra, attn)

    w2, w6, near_grad = lax.optimization_barrier((w2, w6, near_grad))
    w3, w5 = ring_round(w2, w6)
    returned, w3, w5 = lax.optimization_barrier((returned, w3, w5))
    w4 = shifted(w3, 1)

    half = NB // 2
    *pairs, part = call(
        gather_grads_body,
        (*(shaped(2, 4 * HD, BLK),) * half, shaped(4 * HD, D)),
        [scalars()] * 2 + [left()] * 6,
        scratch=[
            *held(exchanged, blocks_float, shaped(NB + 1, BLK, BLK, kind=F32)),
            *held(shaped(NB + 1, BLK, BLK, kind=F32), shaped(4 * HD, ROWS), states, shaped(4 * HD, D)),
            dma_sems(4),
            dma_sems(6),
            dma_sems(3 + NB),
        ],
        flops=2 * ROWS * D * 128,
        name="gather_grads",
    )(col, home, returned, near_grad, query_grad, attn, hidden, early)

    share_rows = 4 * HD // doms
    shares = lax.all_to_all(part.reshape(doms, share_rows, D), "dom", 0, 0, tiled=True)
    *pairs, w4 = lax.optimization_barrier((*pairs, w4))
    pairs = [pairs[0], *(shifted(pairs[j], 2 * j) for j in range(1, half))]
    (totals,) = call(
        sum_body,
        (shaped(doms, share_rows, D),),
        [whole()],
        out_specs=[whole()],
        name="sum_shares",
        limit=4,
    )(shares)
    total = lax.all_to_all(totals, "dom", 0, 0, tiled=True).reshape(4 * HD, D)
    packed = shaped(half, 4 * HD, BLK)
    (beside,) = call(
        pack_body,
        (packed,),
        [left()] * (half + 1),
        scratch=[*held(packed), dma_sems(half), dma_sems(half)],
        name="pack",
    )(*pairs, totals)
    beside = paired(beside)
    sums, piece, weight = shaped(2, BLK, D, kind=F32), shaped(4 * HD, BLK), shaped(4 * HD, D)
    (first,) = call(
        first_heads_body,
        (sums,),
        [left()] * (2 * half - 2),
        scratch=[
            *held(shaped(half - 1, 4 * HD, BLK), shaped(half - 1, 4 * HD, D), sums),
            dma_sems(half - 1),
            dma_sems(half - 1),
            dma_sems(1),
        ],
        flops=unit // 100,
        name="first_heads",
    )(pairs[0], pairs[1], pairs[3], weights_own, w2, w6)
    layer_out, state_grad = call(
        finish_body,
        (node, node),
        [scalars()] + [left()] * (3 + half + 1 + 3),
        scratch=[
            *held(sums, piece, packed, shaped(half + 1, 4 * HD, D), node, node, row, node, node),
            dma_sems(2),
            dma_sems(half + 1),
            dma_sems(4),
            dma_sems(2),
        ],
        flops=unit // 100,
        name="finish",
    )(col, first, pairs[2], beside, w1, w3, w5, w7, w4, node_states, out_grad, gain)
    qkv_grad, out_weight_grad = call(
        functools.partial(scale_body, 1.0 / math.sqrt(far_owner.shape[0] * BLK)),
        (shaped(3 * HD, D, kind=F32), shaped(HD, D, kind=F32)),
        [whole()],
        out_specs=[whole()] * 2,
        flops=3 * unit,
        name="scale",
        limit=4,
    )(total)

    return (layer_out, state_grad, qkv_grad, out_weight_grad)


def solution(mesh):
    placed = (
        P(("dom", "col"), None),
        P(),
        P("col", None),
        P("col", None),
        P("dom", None),
        P("dom", None),
        P(),
        P(),
        P(("dom", "col"), None),
    )
    return jax.shard_map(
        shards,
        mesh=mesh,
        in_specs=placed,
        out_specs=(
            P(("dom", "col"), None),
            P(("dom", "col"), None),
            P("col", None),
            P("col", None),
        ),
        check_vma=False,
    )
```
